32 devices in a mesh: fsdp: 16 (over z, y, core), ctx: 2 (over x).
Axes of the slice: x: 2, y: 2, z: 4, core: 2. Of those that a mesh axis runs over, the one named last changes fastest.
Arguments:
- tokens: bfloat16 [32, 1024, 640], P('fsdp', 'ctx'), may hold values from -6 to 6
- cotangent: bfloat16 [32, 1024, 640], P('fsdp', 'ctx'), may hold values from -6 to 6
- norm_gain: bfloat16 [640], P('fsdp'), may hold values from 0.099609375 to 1.8984375
- query_weight: bfloat16 [640, 1024], P('fsdp'), may hold values from -0.25 to 0.25
- key_weight: bfloat16 [640, 256], P('fsdp'), may hold values from -0.25 to 0.25
- value_weight: bfloat16 [640, 256], P('fsdp'), may hold values from -0.25 to 0.25
- query_norm: bfloat16 [256], P('fsdp'), may hold values from 0.099609375 to 1.8984375
- key_norm: bfloat16 [256], P('fsdp'), may hold values from 0.099609375 to 1.8984375
- output_weight: bfloat16 [1024, 640], P('fsdp'), may hold values from -0.1875 to 0.1875
- attn_post_gain: bfloat16 [640], P('fsdp'), may hold values from 0.099609375 to 1.8984375
- mlp_pre_gain: bfloat16 [640], P('fsdp'), may hold values from 0.099609375 to 1.8984375
- gate_weight: bfloat16 [640, 2048], P('fsdp'), may hold values from -0.25 to 0.25
- up_weight: bfloat16 [640, 2048], P('fsdp'), may hold values from -0.25 to 0.25
- down_weight: bfloat16 [2048, 640], P('fsdp'), may hold values from -0.125 to 0.125
- mlp_post_gain: bfloat16 [640], P('fsdp'), may hold values from 0.099609375 to 1.8984375
Outputs:
- block_output: bfloat16 [32, 1024, 640], P('fsdp', 'ctx')
- token_grad: bfloat16 [32, 1024, 640], P('fsdp', 'ctx')
- grad_norm_gain: float32 [640], P('fsdp')
- grad_query_weight: float32 [640, 1024], P('fsdp')
- grad_key_weight: float32 [640, 256], P('fsdp')
- grad_value_weight: float32 [640, 256], P('fsdp')
- grad_query_norm: float32 [256], P('fsdp')
- grad_key_norm: float32 [256], P('fsdp')
- grad_output_weight: float32 [1024, 640], P('fsdp')
- grad_attn_post_gain: float32 [640], P('fsdp')
- grad_mlp_pre_gain: float32 [640], P('fsdp')
- grad_gate_weight: float32 [640, 2048], P('fsdp')
- grad_up_weight: float32 [640, 2048], P('fsdp')
- grad_down_weight: float32 [2048, 640], P('fsdp')
- grad_mlp_post_gain: float32 [640], P('fsdp')
The draws below stay inside these ranges and needn't reach their ends.
All inputs are finite; a program needn't handle non-finite values.
Results may differ from the reference program's by a relative error of at most 0.018.
Values may be sent and summed in bfloat16 or wider, within the bound.
No kernel may reach another device: no remote copies, remote signals or barrier semaphores. Data moves between devices by JAX's collectives and lax.ppermute only.
A program may use at most 192 MiB of HBM per device.

```python
import jax
import jax.numpy as jnp
from jax import lax

D = 640
HEADS = 4
HEAD_FEATURES = 256
FF = 2048
WINDOW = 512
SEQS = 32
LENGTH = 1024


def block_levels(rng, shape, shards, low, top_value):
    factor_of = 1.0
    for dim, parts in shards:
        draws = jax.random.uniform(jax.random.fold_in(jax.random.fold_in(rng, 6), dim), (parts,), jnp.float32, low / len(shards), top_value / len(shards))
        factor_of = factor_of * jnp.repeat(jnp.exp(draws), shape[dim] // parts).reshape((-1,) + (1,) * (len(shape) - 1 - dim))
    return factor_of


def scatter_about(key, extent, deviation, limit, cuts=(), held_as=jnp.bfloat16):
    drawn = deviation * jax.random.normal(key, extent, jnp.float32)
    if cuts:
        drawn = drawn * block_levels(key, extent, cuts, -0.22, 0.18)
    return jnp.clip(drawn, -limit, limit).astype(held_as)


def setup_inputs(seed: int = 0) -> dict:
    keys = jax.random.split(jax.random.key(seed), 16)
    tokens = scatter_about(keys[0], (SEQS, LENGTH, D), 1.0, 6.0, ((0, 16), (1, 2)))
    cotangent = scatter_about(keys[1], (SEQS, LENGTH, D), 1.0, 6.0, ((0, 16), (1, 2)))
    norm_gain = jnp.clip(1.0 + 0.18 * jax.random.normal(keys[2], (D,), jnp.float32), 0.099609375, 1.8984375).astype(jnp.bfloat16)
    query_weight = scatter_about(keys[3], (D, HEADS * HEAD_FEATURES), D ** -0.5, 0.25, ((0, 16),))
    key_weight = scatter_about(keys[4], (D, HEAD_FEATURES), D ** -0.5, 0.25, ((0, 16),))
    value_weight = scatter_about(keys[5], (D, HEAD_FEATURES), D ** -0.5, 0.25, ((0, 16),))
    query_norm = jnp.clip(1.0 + 0.18 * jax.random.normal(keys[6], (HEAD_FEATURES,), jnp.float32), 0.099609375, 1.8984375).astype(jnp.bfloat16)
    key_norm = jnp.clip(1.0 + 0.18 * jax.random.normal(keys[7], (HEAD_FEATURES,), jnp.float32), 0.099609375, 1.8984375).astype(jnp.bfloat16)
    output_weight = scatter_about(keys[8], (HEADS * HEAD_FEATURES, D), (HEADS * HEAD_FEATURES) ** -0.5, 0.1875, ((0, 16),))
    attn_post_gain = jnp.clip(1.0 + 0.18 * jax.random.normal(keys[9], (D,), jnp.float32), 0.099609375, 1.8984375).astype(jnp.bfloat16)
    mlp_pre_gain = jnp.clip(1.0 + 0.18 * jax.random.normal(keys[10], (D,), jnp.float32), 0.099609375, 1.8984375).astype(jnp.bfloat16)
    gate_weight = scatter_about(keys[11], (D, FF), D ** -0.5, 0.25, ((0, 16),))
    up_weight = scatter_about(keys[12], (D, FF), D ** -0.5, 0.25, ((0, 16),))
    down_weight = scatter_about(keys[13], (FF, D), FF ** -0.5, 0.125, ((0, 16),))
    mlp_post_gain = jnp.clip(1.0 + 0.18 * jax.random.normal(keys[14], (D,), jnp.float32), 0.099609375, 1.8984375).astype(jnp.bfloat16)
    return {"tokens": tokens, "cotangent": cotangent, "norm_gain": norm_gain, "query_weight": query_weight, "key_weight": key_weight, "value_weight": value_weight, "query_norm": query_norm, "key_norm": key_norm, "output_weight": output_weight, "attn_post_gain": attn_post_gain, "mlp_pre_gain": mlp_pre_gain, "gate_weight": gate_weight, "up_weight": up_weight, "down_weight": down_weight, "mlp_post_gain": mlp_post_gain}


@jax.custom_vjp
def reduced_dtype(v):
    return lax.optimization_barrier(v.astype(jnp.bfloat16)).astype(jnp.float32)

@jax.custom_vjp
def low_back(v):
    return v

def low_keep(v):
    return (reduced_dtype(v), None)

def low_pass(kept, grad):
    return (grad,)

def back_keep(v):
    return (v, None)

def back_low(kept, grad):
    return (reduced_dtype(grad),)
reduced_dtype.defvjp(low_keep, low_pass)
low_back.defvjp(back_keep, back_low)
EPSILON = 1e-06
MASKED = -1e+30
FULL_PRECISION = lax.Precision.HIGHEST

def rms_gain(values_in, gain_vector):
    return values_in * lax.rsqrt(lax.optimization_barrier(jnp.mean(values_in * values_in, axis=-1, keepdims=True)) + EPSILON) * gain_vector

def rotate(values_in, cosine_table, sine_table):
    half_dim = values_in.shape[-1] // 2
    front_half = values_in[..., :half_dim]
    back_half = values_in[..., half_dim:]
    return jnp.concatenate([front_half * cosine_table - back_half * sine_table, back_half * cosine_table + front_half * sine_table], axis=-1)

def angle_tables(offset, length_rows, head_dim):
    half_dim = head_dim // 2
    frequency = 10000.0 ** (-(jnp.arange(half_dim).astype(jnp.float32) * 2.0 / head_dim))
    positions = (offset + jnp.arange(length_rows)).astype(jnp.float32)
    angles = positions[:, None] * frequency[None, :]
    return (jnp.cos(angles), jnp.sin(angles))

def window_mask(offset, blocks, window):
    row_index = jnp.arange(window)[:, None]
    col_index = jnp.arange(2 * window)[None, :]
    inside = (col_index > row_index) & (col_index <= row_index + window)
    key_start = offset + jnp.arange(blocks) * window - window
    return inside[None, :, :] & (key_start[:, None, None] + col_index[None, :, :] >= 0)

def blocks_of(rows_in, blocks):
    length_rows, last_dim = rows_in.shape
    zero_rows = jnp.zeros((WINDOW, last_dim), rows_in.dtype)
    extended = jnp.concatenate([zero_rows, rows_in], axis=0)
    earlier = extended[:length_rows].reshape(blocks, WINDOW, last_dim)
    return jnp.concatenate([earlier, rows_in.reshape(blocks, WINDOW, last_dim)], axis=1)

def product(rows_in, matrix):
    return jnp.dot(rows_in, matrix, precision=FULL_PRECISION, preferred_element_type=jnp.float32)

def layer_forward(tokens_in, norm_gain, query_weight, key_weight, value_weight, query_norm, key_norm, output_weight, attn_post_gain, mlp_pre_gain, gate_weight, up_weight, down_weight, mlp_post_gain):
    length_rows = tokens_in.shape[0]
    blocks = length_rows // WINDOW
    normed = reduced_dtype(rms_gain(tokens_in, norm_gain))
    query_raw = low_back(product(normed, query_weight))
    key_raw = low_back(product(normed, key_weight))
    value_rows = reduced_dtype(low_back(product(normed, value_weight)))
    cosine_table, sine_table = angle_tables(0, length_rows, HEAD_FEATURES)
    query_heads = rms_gain(query_raw.reshape(length_rows, HEADS, HEAD_FEATURES), query_norm)
    query_rot = reduced_dtype(rotate(query_heads, cosine_table[:, None, :], sine_table[:, None, :]))
    key_rot = reduced_dtype(rotate(rms_gain(key_raw, key_norm), cosine_table, sine_table))
    window_key_rows = blocks_of(key_rot, blocks)
    window_value_rows = blocks_of(value_rows, blocks)
    query_rows = query_rot.reshape(blocks, WINDOW, HEADS, HEAD_FEATURES)
    logit_scores = jnp.einsum('tawg,tsg->twas', query_rows, window_key_rows, precision=FULL_PRECISION) * HEAD_FEATURES ** (-0.5)
    logit_scores = low_back(logit_scores)
    allowed = window_mask(0, blocks, WINDOW)
    logit_scores = jnp.where(allowed[:, None], logit_scores, MASKED)
    normalized_probs = jax.nn.softmax(logit_scores, axis=-1)
    attended_output = jnp.einsum('luts,lsv->ltuv', reduced_dtype(normalized_probs), window_value_rows, precision=FULL_PRECISION)
    attended_output = reduced_dtype(low_back(attended_output.reshape(length_rows, HEADS * HEAD_FEATURES)))
    attention_raw = low_back(product(attended_output, output_weight))
    middle = tokens_in + rms_gain(attention_raw, attn_post_gain)
    mlp_input = reduced_dtype(rms_gain(middle, mlp_pre_gain))
    gate_raw = low_back(product(mlp_input, gate_weight))
    up_raw = low_back(product(mlp_input, up_weight))
    hidden = reduced_dtype(jax.nn.gelu(gate_raw, approximate=True) * up_raw)
    mlp_raw = low_back(product(hidden, down_weight))
    return middle + rms_gain(mlp_raw, mlp_post_gain)

def reference(tokens, cotangent, norm_gain, query_weight, key_weight, value_weight, query_norm, key_norm, output_weight, attn_post_gain, mlp_pre_gain, gate_weight, up_weight, down_weight, mlp_post_gain):
    weights = tuple((weight_in.astype(jnp.float32) for weight_in in (norm_gain, query_weight, key_weight, value_weight, query_norm, key_norm, output_weight, attn_post_gain, mlp_pre_gain, gate_weight, up_weight, down_weight, mlp_post_gain)))

    def one_sequence(carried, sequence):
        tokens_in, upstream = sequence
        result, pullback = jax.vjp(layer_forward, tokens_in.astype(jnp.float32), *weights)
        gradients = pullback(upstream.astype(jnp.float32))
        summed = tuple((running + grad_piece for running, grad_piece in zip(carried, gradients[1:])))
        return (summed, (result.astype(jnp.bfloat16), gradients[0].astype(jnp.bfloat16)))
    initial = tuple((jnp.zeros(weight_in.shape, jnp.float32) for weight_in in weights))
    summed, (outputs, token_grads) = lax.scan(one_sequence, initial, (tokens, cotangent))
    return (outputs, token_grads, summed[0], summed[1], summed[2], summed[3], summed[4], summed[5], summed[6], summed[7], summed[8], summed[9], summed[10], summed[11], summed[12])
```

```python
import jax
import jax.numpy as jnp
from jax import lax
from jax.sharding import PartitionSpec as P

WINDOW = 512


EPSILON = 1e-06
MASKED = -1e30


LANES = 128


def swap(value, axis, mask):
    count = lax.axis_size(axis)
    return lax.ppermute(value, axis, [(source, source ^ mask) for source in range(count)])


def gather_pairs(shard, axis):
    count = lax.axis_size(axis)
    index = lax.axis_index(axis)
    held = shard[None]
    mask = count // 2
    while mask:
        other = swap(held, axis, mask)
        upper = (index & mask) != 0
        held = jnp.stack(
            [jnp.where(upper, other, held), jnp.where(upper, held, other)], axis=1
        ).reshape((-1,) + shard.shape)
        mask //= 2
    return held.reshape((-1,) + shard.shape[1:])


def halve(value, axis, mask, bit):
    half = value.shape[0] // 2
    parts = value.reshape((2, half) + value.shape[1:])
    kept = lax.dynamic_index_in_dim(parts, bit, 0, keepdims=False)
    sent = lax.dynamic_index_in_dim(parts, 1 - bit, 0, keepdims=False)
    return kept.astype(jnp.float32) + swap(sent, axis, mask).astype(jnp.float32)


def shared_sum(value, axis):
    count = lax.axis_size(axis)
    total = 0.0
    for step in range(1, count):
        total = total + swap(value, axis, step).astype(jnp.float32)
    return total


def scatter_pairs(shards, axis, summed):
    count = lax.axis_size(axis)
    index = lax.axis_index(axis)
    value = shards
    value = jnp.moveaxis(value.reshape((count // 2, 2) + value.shape[1:]), 1, 0).reshape(value.shape)
    value = halve(value, axis, 1, index & 1).astype(jnp.bfloat16)
    mask = count // 2
    while mask > 1:
        value = halve(value, axis, mask, (index & mask) // mask).astype(jnp.bfloat16)
        mask //= 2
    value = value[0]
    total = value.astype(jnp.float32)
    for other in summed:
        total = total + shared_sum(value, other)
    return total


def shifted(value, axis, steps):
    count = lax.axis_size(axis)
    leading, last = (max(0, -steps), min(count, count - steps))
    return lax.ppermute(value, axis, [(source, source + steps) for source in range(leading, last)])


def rms_gain(values_in, gain_vector):
    return (
        values_in
        * lax.rsqrt(jnp.mean(values_in * values_in, axis=-1, keepdims=True) + EPSILON)
        * gain_vector
    )


def rotate(values_in, cosine_table, sine_table):
    half_dim = values_in.shape[-1] // 2
    front_half = values_in[..., :half_dim]
    back_half = values_in[..., half_dim:]
    return jnp.concatenate(
        [
            front_half * cosine_table - back_half * sine_table,
            back_half * cosine_table + front_half * sine_table,
        ],
        axis=-1,
    )


def angle_tables(offset, length_rows, head_dim):
    half_dim = head_dim // 2
    frequency = 10000.0 ** (-(jnp.arange(half_dim).astype(jnp.float32) * 2.0 / head_dim))
    positions = (offset + jnp.arange(length_rows)).astype(jnp.float32)
    angles = positions[:, None] * frequency[None, :]
    return (jnp.cos(angles), jnp.sin(angles))


def window_mask(offset, blocks, window):
    row_index = jnp.arange(window)[:, None]
    col_index = jnp.arange(2 * window)[None, :]
    inside = (col_index > row_index) & (col_index <= row_index + window)
    key_start = offset + jnp.arange(blocks) * window - window
    return inside[None, :, :] & (key_start[:, None, None] + col_index[None, :, :] >= 0)


def query_key(query_raw, key_raw, query_gain, key_gain, cosine_table, sine_table):
    query_rot = rotate(
        rms_gain(query_raw, query_gain), cosine_table[:, None, :], sine_table[:, None, :]
    )
    key_rot = rotate(rms_gain(key_raw, key_gain), cosine_table, sine_table)
    return (query_rot, key_rot)


def key_blocks(before, current, blocks, window):
    sequences, span_len, last_dim = current.shape
    extended = jnp.concatenate([before, current], axis=1)
    earlier = extended[:, :span_len].reshape(sequences, blocks, window, last_dim)
    return jnp.concatenate([earlier, current.reshape(sequences, blocks, window, last_dim)], axis=2)


def split_blocks(gradients, span_len, window):
    sequences = gradients.shape[0]
    last_dim = gradients.shape[-1]
    earlier = gradients[:, :, :window].reshape(sequences, span_len, last_dim)
    current = gradients[:, :, window:].reshape(sequences, span_len, last_dim)
    zero_rows = jnp.zeros((sequences, window, last_dim), jnp.float32)
    extended = jnp.concatenate([earlier, zero_rows], axis=1) + jnp.concatenate(
        [zero_rows, current], axis=1
    )
    return (extended[:, :window], extended[:, window:])


def block_scores(query_rows, window_key_rows, allowed, score_scale):
    raw_scores = (
        jnp.einsum(
            "snqhd,snkd->snhqk", query_rows, window_key_rows, preferred_element_type=jnp.float32
        )
        * score_scale
    )
    return jnp.where(allowed[None, :, None], raw_scores, MASKED)


def post_attention(residual, attention_raw, attn_gain, mlp_gain):
    middle = residual + rms_gain(attention_raw, attn_gain)
    return (middle, rms_gain(middle, mlp_gain))


def gated_unit(gate_raw, up_raw):
    return jax.nn.gelu(gate_raw, approximate=True) * up_raw


def block_tail(middle, mlp_raw, final_gain):
    return middle + rms_gain(mlp_raw, final_gain)


def project(rows_in, matrix):
    return jnp.dot(rows_in, matrix, preferred_element_type=jnp.float32)


def weight_grad(rows_in, grad_rows):
    return jnp.einsum("scd,sce->de", rows_in, grad_rows, preferred_element_type=jnp.float32)


def back_project(grad_rows, matrix):
    return jnp.einsum("sce,de->scd", grad_rows, matrix, preferred_element_type=jnp.float32)


def per_device(
    tokens,
    cotangent,
    norm_gain,
    query_weight,
    key_weight,
    value_weight,
    query_norm,
    key_norm,
    output_weight,
    attn_post_gain,
    mlp_pre_gain,
    gate_weight,
    up_weight,
    down_weight,
    mlp_post_gain,
):
    fsdp = lax.axis_size("fsdp")
    rows = norm_gain.shape[0]
    head_rows = query_norm.shape[0]
    gain_columns = jnp.stack(
        [
            norm_gain,
            attn_post_gain,
            mlp_pre_gain,
            mlp_post_gain,
            jnp.pad(query_norm, (0, rows - head_rows)),
            jnp.pad(key_norm, (0, rows - head_rows)),
        ],
        axis=1,
    )
    gain_columns = jnp.pad(gain_columns, ((0, 0), (0, LANES - gain_columns.shape[1])))
    query_columns = query_weight.shape[1]
    head_dim = key_weight.shape[1]
    ff = gate_weight.shape[1]
    first_shard = jnp.concatenate([query_weight, key_weight, value_weight, gain_columns], axis=1)
    rest_shard = jnp.concatenate(
        [
            gate_weight,
            up_weight,
            down_weight.reshape(rows, -1),
            output_weight.reshape(rows, -1),
        ],
        axis=1,
    )
    first_full = gather_pairs(first_shard, "fsdp")
    rest_full = lax.all_gather(rest_shard, "fsdp", axis=0, tiled=True)
    qkv_columns = query_columns + 2 * head_dim
    query_full = first_full[:, :query_columns]
    key_full = first_full[:, query_columns : query_columns + head_dim]
    value_full = first_full[:, query_columns + head_dim : qkv_columns]
    gains = first_full[:, qkv_columns : qkv_columns + 6].astype(jnp.float32).T
    gain_first, gain_attn, gain_mlp, gain_final = gains[0], gains[1], gains[2], gains[3]
    gain_query = gains[4].reshape(fsdp, rows)[:, :head_rows].reshape(-1)
    gain_key = gains[5].reshape(fsdp, rows)[:, :head_rows].reshape(-1)
    gate_full = rest_full[:, :ff]
    up_full = rest_full[:, ff : 2 * ff]
    down_full = rest_full[:, 2 * ff : 3 * ff].reshape(ff, -1)
    output_full = rest_full[:, 3 * ff :].reshape(query_columns, -1)
    sequences, span_len, model_width = tokens.shape
    head_count = query_columns // head_dim
    window = WINDOW
    blocks = span_len // window
    offset = lax.axis_index("ctx") * span_len
    score_scale = head_dim ** (-0.5)
    residual = tokens.astype(jnp.float32)
    normed, norm_pull = jax.vjp(rms_gain, residual, gain_first)
    normed_low = normed.astype(jnp.bfloat16)
    query_raw = project(normed_low, query_full)
    key_raw = project(normed_low, key_full)
    value_low = project(normed_low, value_full).astype(jnp.bfloat16)
    cosine_table, sine_table = angle_tables(offset, span_len, head_dim)

    def rotary(query_in, key_in, query_gain, key_gain):
        return query_key(query_in, key_in, query_gain, key_gain, cosine_table, sine_table)

    (query_rot, key_rot), rotary_pull = jax.vjp(
        rotary,
        query_raw.reshape(sequences, span_len, head_count, head_dim),
        key_raw,
        gain_query,
        gain_key,
    )
    query_low = query_rot.astype(jnp.bfloat16)
    key_low = key_rot.astype(jnp.bfloat16)
    key_prev, value_prev = shifted((key_low, value_low), "ctx", 1)
    window_key_rows = key_blocks(key_prev, key_low, blocks, window)
    window_value_rows = key_blocks(value_prev, value_low, blocks, window)
    query_rows = query_low.reshape(sequences, blocks, window, head_count, head_dim)
    allowed = window_mask(offset, blocks, window)
    logit_scores = block_scores(query_rows, window_key_rows, allowed, score_scale)
    row_max = jnp.max(logit_scores, axis=-1, keepdims=True)
    exp_terms = jnp.exp(logit_scores - row_max)
    row_total = jnp.sum(exp_terms, axis=-1, keepdims=True)
    log_total = row_max + jnp.log(row_total)
    normalized_probs = exp_terms / row_total
    attended_output = jnp.einsum(
        "snhqk,snkd->snqhd",
        normalized_probs.astype(jnp.bfloat16),
        window_value_rows,
        preferred_element_type=jnp.float32,
    )
    attended_low = attended_output.reshape(sequences, span_len, head_count * head_dim).astype(
        jnp.bfloat16
    )
    attention_raw = project(attended_low, output_full)
    (middle, mlp_input), post_pull = jax.vjp(
        post_attention, residual, attention_raw, gain_attn, gain_mlp
    )
    mlp_low = mlp_input.astype(jnp.bfloat16)
    gate_raw = project(mlp_low, gate_full)
    up_raw = project(mlp_low, up_full)
    hidden, gated_pull = jax.vjp(gated_unit, gate_raw, up_raw)
    hidden_low = hidden.astype(jnp.bfloat16)
    mlp_raw = project(hidden_low, down_full)
    block_output, tail_pull = jax.vjp(block_tail, middle, mlp_raw, gain_final)
    upstream = cotangent.astype(jnp.float32)
    grad_middle, grad_mlp_raw, grad_final_gain = tail_pull(upstream)
    grad_mlp_low = grad_mlp_raw.astype(jnp.bfloat16)
    grad_down_weight = weight_grad(hidden_low, grad_mlp_low)
    grad_hidden = back_project(grad_mlp_low, down_full)
    grad_gate_raw, grad_up_raw = gated_pull(grad_hidden)
    grad_gate_low = grad_gate_raw.astype(jnp.bfloat16)
    grad_up_low = grad_up_raw.astype(jnp.bfloat16)
    grad_gate_weight = weight_grad(mlp_low, grad_gate_low)
    grad_up_weight = weight_grad(mlp_low, grad_up_low)
    grad_mlp_input = back_project(grad_gate_low, gate_full) + back_project(grad_up_low, up_full)
    grad_resid_post, grad_attention_raw, grad_attn_gain, grad_mlp_gain = post_pull(
        (grad_middle, grad_mlp_input)
    )
    grad_attention_low = grad_attention_raw.astype(jnp.bfloat16)
    grad_output_weight = weight_grad(attended_low, grad_attention_low)
    grad_attended = back_project(grad_attention_low, output_full).astype(jnp.bfloat16)
    grad_attended = grad_attended.reshape(sequences, blocks, window, head_count, head_dim)
    logit_scores = block_scores(query_rows, window_key_rows, allowed, score_scale)
    normalized_probs = jnp.exp(logit_scores - log_total)
    grad_value_block = jnp.einsum(
        "snhqk,snqhd->snkd",
        normalized_probs.astype(jnp.bfloat16),
        grad_attended,
        preferred_element_type=jnp.float32,
    )
    grad_weights = jnp.einsum(
        "snqhd,snkd->snhqk", grad_attended, window_value_rows, preferred_element_type=jnp.float32
    )
    inner_sum = jnp.sum(grad_weights * normalized_probs, axis=-1, keepdims=True)
    grad_scores = (normalized_probs * (grad_weights - inner_sum)).astype(jnp.bfloat16)
    grad_queries = (
        jnp.einsum(
            "snhqk,snkd->snqhd", grad_scores, window_key_rows, preferred_element_type=jnp.float32
        )
        * score_scale
    )
    grad_key_block = (
        jnp.einsum("snhqk,snqhd->snkd", grad_scores, query_rows, preferred_element_type=jnp.float32)
        * score_scale
    )
    key_send, grad_key_rot = split_blocks(grad_key_block, span_len, window)
    value_send, grad_value = split_blocks(grad_value_block, span_len, window)
    key_back, value_back = (
        shifted(key_send.astype(jnp.bfloat16), "ctx", -1).astype(key_send.dtype),
        shifted(value_send.astype(jnp.bfloat16), "ctx", -1).astype(value_send.dtype),
    )
    zero_rows = jnp.zeros((sequences, span_len - window, head_dim), jnp.float32)
    grad_key_rot = grad_key_rot + jnp.concatenate([zero_rows, key_back], axis=1)
    grad_value = grad_value + jnp.concatenate([zero_rows, value_back], axis=1)
    grad_query_raw, grad_key_raw, grad_query_gain, grad_key_gain = rotary_pull(
        (grad_queries.reshape(sequences, span_len, head_count, head_dim), grad_key_rot)
    )
    grad_query_low = grad_query_raw.reshape(sequences, span_len, head_count * head_dim).astype(
        jnp.bfloat16
    )
    grad_key_low = grad_key_raw.astype(jnp.bfloat16)
    grad_value_low = grad_value.astype(jnp.bfloat16)
    grad_query_weight = weight_grad(normed_low, grad_query_low)
    grad_key_weight = weight_grad(normed_low, grad_key_low)
    grad_value_weight = weight_grad(normed_low, grad_value_low)
    grad_normed = (
        back_project(grad_query_low, query_full)
        + back_project(grad_key_low, key_full)
        + back_project(grad_value_low, value_full)
    )
    grad_resid_norm, grad_norm_gain = norm_pull(grad_normed)
    token_grad = (grad_resid_post + grad_resid_norm).astype(jnp.bfloat16)
    def to_shards(grad):
        return grad.astype(jnp.bfloat16).reshape(fsdp, rows, -1)

    rest_grads = jnp.concatenate(
        [
            to_shards(grad_gate_weight),
            to_shards(grad_up_weight),
            to_shards(grad_down_weight),
            to_shards(grad_output_weight),
        ],
        axis=2,
    ).reshape(fsdp * rows, -1)
    rest_sum = lax.psum_scatter(rest_grads, "fsdp", scatter_dimension=0, tiled=True)
    rest_sum = rest_sum.astype(jnp.float32) + shared_sum(rest_sum, "ctx")

    def head_gain(grad):
        return jnp.pad(grad.reshape(fsdp, head_rows), ((0, 0), (0, rows - head_rows))).reshape(-1)

    gain_grads = jnp.stack(
        [
            grad_norm_gain,
            grad_attn_gain,
            grad_mlp_gain,
            grad_final_gain,
            head_gain(grad_query_gain),
            head_gain(grad_key_gain),
        ],
        axis=1,
    )
    gain_grads = jnp.pad(gain_grads, ((0, 0), (0, LANES - gain_grads.shape[1])))
    first_grads = jnp.concatenate(
        [grad_query_weight, grad_key_weight, grad_value_weight, gain_grads], axis=1
    ).astype(jnp.bfloat16)
    first_sum = scatter_pairs(first_grads.reshape(fsdp, rows, -1), "fsdp", ("ctx",))
    return (
        block_output.astype(jnp.bfloat16),
        token_grad,
        first_sum[:, qkv_columns],
        first_sum[:, :query_columns],
        first_sum[:, query_columns : query_columns + head_dim],
        first_sum[:, query_columns + head_dim : qkv_columns],
        first_sum[:head_rows, qkv_columns + 4],
        first_sum[:head_rows, qkv_columns + 5],
        rest_sum[:, 3 * ff :].reshape(output_weight.shape),
        first_sum[:, qkv_columns + 1],
        first_sum[:, qkv_columns + 2],
        rest_sum[:, :ff],
        rest_sum[:, ff : 2 * ff],
        rest_sum[:, 2 * ff : 3 * ff].reshape(down_weight.shape),
        first_sum[:, qkv_columns + 3],
    )


def solution(mesh):
    return jax.shard_map(
        per_device,
        mesh=mesh,
        in_specs=(
            P("fsdp", "ctx", None),
            P("fsdp", "ctx", None),
            P("fsdp"),
            P("fsdp", None),
            P("fsdp", None),
            P("fsdp", None),
            P("fsdp"),
            P("fsdp"),
            P("fsdp", None),
            P("fsdp"),
            P("fsdp"),
            P("fsdp", None),
            P("fsdp", None),
            P("fsdp", None),
            P("fsdp"),
        ),
        out_specs=(
            P("fsdp", "ctx", None),
            P("fsdp", "ctx", None),
            P("fsdp"),
            P("fsdp", None),
            P("fsdp", None),
            P("fsdp", None),
            P("fsdp"),
            P("fsdp"),
            P("fsdp", None),
            P("fsdp"),
            P("fsdp"),
            P("fsdp", None),
            P("fsdp", None),
            P("fsdp", None),
            P("fsdp"),
        ),
        check_vma=False,
    )
```

```python
import functools

import jax
import jax.numpy as jnp
from jax import lax
from jax.experimental import pallas as pl
from jax.experimental.pallas import tpu as pltpu
from jax.sharding import PartitionSpec as P

WINDOW = 512


EPSILON = 1e-06
MASKED = -1e30
ROOT = (2.0 / jnp.pi) ** 0.5
ROWS = 256
VMEM_BYTES = 60 * 1024 * 1024


LANES = 128


def swap(value, axis, mask):
    count = lax.axis_size(axis)
    return lax.ppermute(value, axis, [(source, source ^ mask) for source in range(count)])


def gather_pairs(shard, axis):
    count = lax.axis_size(axis)
    index = lax.axis_index(axis)
    held = shard[None]
    mask = count // 2
    while mask:
        other = swap(held, axis, mask)
        upper = (index & mask) != 0
        held = jnp.stack(
            [jnp.where(upper, other, held), jnp.where(upper, held, other)], axis=1
        ).reshape((-1,) + shard.shape)
        mask //= 2
    return held.reshape((-1,) + shard.shape[1:])


def halve(value, axis, mask, bit):
    half = value.shape[0] // 2
    parts = value.reshape((2, half) + value.shape[1:])
    kept = lax.dynamic_index_in_dim(parts, bit, 0, keepdims=False)
    sent = lax.dynamic_index_in_dim(parts, 1 - bit, 0, keepdims=False)
    return kept.astype(jnp.float32) + swap(sent, axis, mask).astype(jnp.float32)


def shared_sum(value, axis):
    count = lax.axis_size(axis)
    total = 0.0
    for step in range(1, count):
        total = total + swap(value, axis, step).astype(jnp.float32)
    return total


def scatter_pairs(shards, axis, summed):
    count = lax.axis_size(axis)
    index = lax.axis_index(axis)
    value = shards
    value = jnp.moveaxis(value.reshape((count // 2, 2) + value.shape[1:]), 1, 0).reshape(value.shape)
    value = halve(value, axis, 1, index & 1).astype(jnp.bfloat16)
    mask = count // 2
    while mask > 1:
        value = halve(value, axis, mask, (index & mask) // mask).astype(jnp.bfloat16)
        mask //= 2
    value = value[0]
    total = value.astype(jnp.float32)
    for other in summed:
        total = total + shared_sum(value, other)
    return total


def shifted(value, axis, steps):
    count = lax.axis_size(axis)
    leading, last = (max(0, -steps), min(count, count - steps))
    return lax.ppermute(value, axis, [(source, source + steps) for source in range(leading, last)])


def dot(left, right):
    return jnp.dot(left, right, preferred_element_type=jnp.float32)


def dot_nt(left, right):
    return lax.dot_general(left, right, (((1,), (1,)), ((), ())), preferred_element_type=jnp.float32)


def dot_tn(left, right):
    return lax.dot_general(left, right, (((0,), (0,)), ((), ())), preferred_element_type=jnp.float32)


def inverse_rms(rows):
    return lax.rsqrt(jnp.mean(rows * rows, axis=-1, keepdims=True) + EPSILON)


def rms_back(rows, scale, gain, grad):
    weighted = gain * grad
    inner = jnp.mean(rows * weighted, axis=-1, keepdims=True)
    return scale * weighted - rows * (scale * scale * scale * inner), grad * rows * scale


def turn(rows, cosine, sine):
    half = rows.shape[-1] // 2
    front, back = rows[:, :half], rows[:, half:]
    return jnp.concatenate([front * cosine - back * sine, back * cosine + front * sine], axis=-1)


def turn_back(rows, cosine, sine):
    return turn(rows, cosine, -sine)


def projection_kernel(head_dim, x_ref, w_ref, gain_ref, head_gain_ref, cos_ref, sin_ref, q_ref, k_ref, v_ref):
    x = x_ref[...].astype(jnp.float32)
    normed = (x * inverse_rms(x) * gain_ref[0:1, :]).astype(jnp.bfloat16)
    cosine, sine = cos_ref[...], sin_ref[...]
    queries = q_ref.shape[1]
    for start in range(0, queries + head_dim, head_dim):
        raw = dot(normed, w_ref[:, start : start + head_dim])
        gain = head_gain_ref[0:1, :] if start < queries else head_gain_ref[1:2, :]
        turned = turn(raw * inverse_rms(raw) * gain, cosine, sine).astype(jnp.bfloat16)
        if start < queries:
            q_ref[:, start : start + head_dim] = turned
        else:
            k_ref[...] = turned
    v_ref[...] = dot(normed, w_ref[:, queries + head_dim : queries + 2 * head_dim]).astype(jnp.bfloat16)


def window_parts(rows, now, before, has_before, product):
    half = rows.shape[0] // 2
    low = lax.broadcasted_iota(jnp.int32, (half, half), 1) <= lax.broadcasted_iota(
        jnp.int32, (half, half), 0
    )
    top, bottom = rows[:half], rows[half:]
    before_left = product(top, before[:half])
    before_right = product(top, before[half:])
    before_low = product(bottom, before[half:])
    if has_before is not None:
        before_left = jnp.where(has_before, before_left, MASKED)
        before_right = jnp.where(has_before, before_right, MASKED)
        before_low = jnp.where(has_before, before_low, MASKED)
    upper = jnp.concatenate([jnp.where(low, product(top, now[:half]), before_left), before_right], axis=1)
    lower = jnp.concatenate(
        [product(bottom, now[:half]), jnp.where(low, product(bottom, now[half:]), before_low)], axis=1
    )
    return jnp.concatenate([upper, lower], axis=0)


def window_split(matrix):
    half = matrix.shape[0] // 2
    low = lax.broadcasted_iota(jnp.int32, (half, half), 1) <= lax.broadcasted_iota(
        jnp.int32, (half, half), 0
    )
    first, last = matrix[:half, :half], matrix[half:, half:]
    zero = jnp.zeros_like(first)
    return (
        jnp.where(low, first, zero),
        jnp.where(low, zero, first),
        jnp.where(low, last, zero),
        jnp.where(low, zero, last),
        matrix[:half, half:],
        matrix[half:, :half],
    )


def window_apply(matrix, now, before):
    half = matrix.shape[0] // 2
    first_now, first_before, last_now, last_before, right, left = window_split(matrix)
    top = dot(first_now, now[:half]) + dot(first_before, before[:half]) + dot(right, before[half:])
    bottom = dot(left, now[:half]) + dot(last_now, now[half:]) + dot(last_before, before[half:])
    return jnp.concatenate([top, bottom], axis=0)


def window_apply_back(matrix, rows):
    half = matrix.shape[0] // 2
    first_now, first_before, last_now, last_before, right, left = window_split(matrix)
    top, bottom = rows[:half], rows[half:]
    now = jnp.concatenate([dot_tn(first_now, top) + dot_tn(left, bottom), dot_tn(last_now, bottom)], axis=0)
    before = jnp.concatenate(
        [dot_tn(first_before, top), dot_tn(right, top) + dot_tn(last_before, bottom)], axis=0
    )
    return now, before


def window_probs(query, key, key_before, has_before, scale):
    scores = window_parts(query, key, key_before, has_before, dot_nt) * scale
    terms = jnp.exp(scores - jnp.max(scores, axis=-1, keepdims=True))
    return terms * (1.0 / jnp.sum(terms, axis=-1, keepdims=True))


def attention_kernel(scale, flag_ref, q_ref, k_ref, v_ref, kb_ref, vb_ref, o_ref):
    has_before = flag_ref[0] > 0
    probs = window_probs(q_ref[...], k_ref[...], kb_ref[...], has_before, scale)
    o_ref[...] = window_apply(probs.astype(jnp.bfloat16), v_ref[...], vb_ref[...]).astype(jnp.bfloat16)


def attention_back_kernel(
    scale, flag_ref, q_ref, k_ref, v_ref, kb_ref, vb_ref, do_ref, dq_ref, dk_ref, dv_ref, dkb_ref, dvb_ref
):
    has_before = flag_ref[0] > 0
    query, grad = q_ref[...], do_ref[...]
    probs = window_probs(query, k_ref[...], kb_ref[...], has_before, scale)
    grad_probs = window_parts(grad, v_ref[...], vb_ref[...], None, dot_nt)
    inner = jnp.sum(grad_probs * probs, axis=-1, keepdims=True)
    grad_scores = (probs * (grad_probs - inner)).astype(jnp.bfloat16)
    dq_ref[...] = window_apply(grad_scores, k_ref[...], kb_ref[...]) * scale
    key_now, key_before = window_apply_back(grad_scores, query)
    value_now, value_before = window_apply_back(probs.astype(jnp.bfloat16), grad)

    @pl.when(pl.program_id(1) == 0)
    def _():
        dk_ref[...] = key_now * scale
        dkb_ref[...] = key_before * scale
        dv_ref[...] = value_now
        dvb_ref[...] = value_before

    @pl.when(pl.program_id(1) > 0)
    def _():
        dk_ref[...] += key_now * scale
        dkb_ref[...] += key_before * scale
        dv_ref[...] += value_now
        dvb_ref[...] += value_before


def middle_kernel(
    chunk,
    x_ref,
    dy_ref,
    att_ref,
    wo_ref,
    wg_ref,
    wu_ref,
    wd_ref,
    gain_ref,
    out_ref,
    dmid_ref,
    datt_ref,
    gain_grad_ref,
    go_ref,
    gg_ref,
    gu_ref,
    gd_ref,
    mlp_all,
    hidden_all,
    dmlp_all,
    dgate_all,
    dup_all,
    dattn_all,
):
    step = pl.program_id(0)
    block = x_ref.shape[0]
    rows = pl.ds(pl.multiple_of(step * block, block), block)
    ff = wg_ref.shape[1]
    gain_attn, gain_mlp, gain_final = gain_ref[1:2, :], gain_ref[2:3, :], gain_ref[3:4, :]
    x = x_ref[...].astype(jnp.float32)
    raw = dot(att_ref[rows, :], wo_ref[...])
    raw_scale = inverse_rms(raw)
    middle = x + raw * raw_scale * gain_attn
    middle_scale = inverse_rms(middle)
    mlp_low = (middle * middle_scale * gain_mlp).astype(jnp.bfloat16)
    mlp_all[rows, :] = mlp_low
    kept = []
    mlp_raw = None
    for start in range(0, ff, chunk):
        part = slice(start, start + chunk)
        gate = dot(mlp_low, wg_ref[:, part])
        up = dot(mlp_low, wu_ref[:, part])
        square = gate * gate
        bend = jnp.tanh(ROOT * (gate + 0.044715 * (gate * square)))
        half = 0.5 * (1.0 + bend)
        gelu = gate * half
        slope = half + (0.5 * ROOT) * gate * (1.0 - bend * bend) * (1.0 + (3 * 0.044715) * square)
        hidden = (gelu * up).astype(jnp.bfloat16)
        hidden_all[rows, part] = hidden
        kept.append((up * slope, gelu))
        term = dot(hidden, wd_ref[part, :])
        mlp_raw = term if mlp_raw is None else mlp_raw + term
    mlp_scale = inverse_rms(mlp_raw)
    out_ref[...] = (middle + mlp_raw * mlp_scale * gain_final).astype(jnp.bfloat16)
    dy = dy_ref[...].astype(jnp.float32)
    grad_raw, final_rows = rms_back(mlp_raw, mlp_scale, gain_final, dy)
    dmlp_low = grad_raw.astype(jnp.bfloat16)
    dmlp_all[rows, :] = dmlp_low
    grad_in = None
    for index, start in enumerate(range(0, ff, chunk)):
        part = slice(start, start + chunk)
        grad_hidden = dot_nt(dmlp_low, wd_ref[part, :])
        up_slope, gelu = kept[index]
        dgate = (grad_hidden * up_slope).astype(jnp.bfloat16)
        dup = (grad_hidden * gelu).astype(jnp.bfloat16)
        dgate_all[rows, part] = dgate
        dup_all[rows, part] = dup
        term = dot_nt(dgate, wg_ref[:, part]) + dot_nt(dup, wu_ref[:, part])
        grad_in = term if grad_in is None else grad_in + term
    grad_middle, mlp_rows = rms_back(middle, middle_scale, gain_mlp, grad_in)
    grad_middle = dy + grad_middle
    dmid_ref[...] = grad_middle
    grad_attn, attn_rows = rms_back(raw, raw_scale, gain_attn, grad_middle)
    dattn_low = grad_attn.astype(jnp.bfloat16)
    dattn_all[rows, :] = dattn_low
    datt_ref[...] = dot_nt(dattn_low, wo_ref[...]).astype(jnp.bfloat16)
    sums = [jnp.sum(part, axis=0, keepdims=True) for part in (attn_rows, mlp_rows, final_rows)]
    gain_sums = jnp.concatenate(sums + [jnp.zeros((8 - len(sums), x.shape[1]), jnp.float32)], axis=0)

    @pl.when(step == 0)
    def _():
        gain_grad_ref[...] = gain_sums

    @pl.when(step > 0)
    def _():
        gain_grad_ref[...] += gain_sums

    @pl.when(step == pl.num_programs(0) - 1)
    def _():
        for start in range(0, ff, chunk):
            part = slice(start, start + chunk)
            gg_ref[:, part] = dot_tn(mlp_all[...], dgate_all[:, part]).astype(jnp.bfloat16)
            gu_ref[:, part] = dot_tn(mlp_all[...], dup_all[:, part]).astype(jnp.bfloat16)
            gd_ref[part, :] = dot_tn(hidden_all[:, part], dmlp_all[...]).astype(jnp.bfloat16)
        for start in range(0, go_ref.shape[0], chunk):
            part = slice(start, start + chunk)
            go_ref[part, :] = dot_tn(att_ref[:, part], dattn_all[...]).astype(jnp.bfloat16)


def head_back_kernel(
    head_dim,
    x_ref,
    w_ref,
    gain_ref,
    head_gain_ref,
    cos_ref,
    sin_ref,
    dq_ref,
    dk_ref,
    dv_ref,
    dkb_ref,
    dvb_ref,
    dmid_ref,
    token_ref,
    gw_ref,
    gain_grad_ref,
    head_grad_ref,
    normed_all,
    draw_all,
):
    step = pl.program_id(0)
    block = x_ref.shape[0]
    rows = pl.ds(pl.multiple_of(step * block, block), block)
    x = x_ref[...].astype(jnp.float32)
    x_scale = inverse_rms(x)
    normed = (x * x_scale * gain_ref[0:1, :]).astype(jnp.bfloat16)
    normed_all[rows, :] = normed
    cosine, sine = cos_ref[...], sin_ref[...]
    queries = dq_ref.shape[1]
    query_rows = None
    for start in range(0, queries + head_dim, head_dim):
        part = slice(start, start + head_dim)
        raw = dot(normed, w_ref[:, part])
        scale = inverse_rms(raw)
        if start < queries:
            grad = turn_back(dq_ref[:, part], cosine, sine)
            grad_raw, head_rows = rms_back(raw, scale, head_gain_ref[0:1, :], grad)
            query_rows = head_rows if query_rows is None else query_rows + head_rows
        else:
            grad = turn_back(dk_ref[...] + dkb_ref[...].astype(jnp.float32), cosine, sine)
            grad_raw, key_rows = rms_back(raw, scale, head_gain_ref[1:2, :], grad)
        draw_all[rows, part] = grad_raw.astype(jnp.bfloat16)
    draw_all[rows, queries + head_dim : queries + 2 * head_dim] = (
        dv_ref[...] + dvb_ref[...].astype(jnp.float32)
    ).astype(jnp.bfloat16)
    grad_normed = dot_nt(draw_all[rows, :], w_ref[:, : queries + 2 * head_dim])
    grad_x, norm_rows = rms_back(x, x_scale, gain_ref[0:1, :], grad_normed)
    token_ref[...] = (dmid_ref[...] + grad_x).astype(jnp.bfloat16)

    def padded(parts):
        sums = [jnp.sum(part, axis=0, keepdims=True) for part in parts]
        return jnp.concatenate(sums + [jnp.zeros((8 - len(sums), sums[0].shape[1]), jnp.float32)], axis=0)

    norm_sums, head_sums = padded([norm_rows]), padded([query_rows, key_rows])

    @pl.when(step == 0)
    def _():
        gain_grad_ref[...] = norm_sums
        head_grad_ref[...] = head_sums

    @pl.when(step > 0)
    def _():
        gain_grad_ref[...] += norm_sums
        head_grad_ref[...] += head_sums

    @pl.when(step == pl.num_programs(0) - 1)
    def _():
        for start in range(0, gw_ref.shape[1], 512):
            part = slice(start, start + 512)
            gw_ref[:, part] = dot_tn(normed_all[...], draw_all[:, part]).astype(jnp.bfloat16)


def angle_tables(offset, length_rows, head_dim):
    half_dim = head_dim // 2
    frequency = 10000.0 ** (-(jnp.arange(half_dim).astype(jnp.float32) * 2.0 / head_dim))
    positions = (offset + jnp.arange(length_rows)).astype(jnp.float32)
    angles = positions[:, None] * frequency[None, :]
    return (jnp.cos(angles), jnp.sin(angles))


def per_device(
    tokens,
    cotangent,
    norm_gain,
    query_weight,
    key_weight,
    value_weight,
    query_norm,
    key_norm,
    output_weight,
    attn_post_gain,
    mlp_pre_gain,
    gate_weight,
    up_weight,
    down_weight,
    mlp_post_gain,
):
    fsdp = lax.axis_size("fsdp")
    rows = norm_gain.shape[0]
    head_rows = query_norm.shape[0]
    gain_columns = jnp.stack(
        [
            norm_gain,
            attn_post_gain,
            mlp_pre_gain,
            mlp_post_gain,
            jnp.pad(query_norm, (0, rows - head_rows)),
            jnp.pad(key_norm, (0, rows - head_rows)),
        ],
        axis=1,
    )
    gain_columns = jnp.pad(gain_columns, ((0, 0), (0, LANES - gain_columns.shape[1])))
    query_columns = query_weight.shape[1]
    head_dim = key_weight.shape[1]
    ff = gate_weight.shape[1]
    first_shard = jnp.concatenate([query_weight, key_weight, value_weight, gain_columns], axis=1)
    rest_shard = jnp.concatenate(
        [
            gate_weight,
            up_weight,
            down_weight.reshape(rows, -1),
            output_weight.reshape(rows, -1),
        ],
        axis=1,
    )
    first_full = gather_pairs(first_shard, "fsdp")
    rest_full = lax.all_gather(rest_shard, "fsdp", axis=0, tiled=True)
    qkv_columns = query_columns + 2 * head_dim
    query_full = first_full[:, :query_columns]
    key_full = first_full[:, query_columns : query_columns + head_dim]
    value_full = first_full[:, query_columns + head_dim : qkv_columns]
    gains = first_full[:, qkv_columns : qkv_columns + 6].astype(jnp.float32).T
    gain_first, gain_attn, gain_mlp, gain_final = gains[0], gains[1], gains[2], gains[3]
    gain_query = gains[4].reshape(fsdp, rows)[:, :head_rows].reshape(-1)
    gain_key = gains[5].reshape(fsdp, rows)[:, :head_rows].reshape(-1)
    gate_full = rest_full[:, :ff]
    up_full = rest_full[:, ff : 2 * ff]
    down_full = rest_full[:, 2 * ff : 3 * ff].reshape(ff, -1)
    output_full = rest_full[:, 3 * ff :].reshape(query_columns, -1)
    sequences, span_len, model_width = tokens.shape
    head_count = query_columns // head_dim
    assert span_len == WINDOW
    offset = lax.axis_index("ctx") * span_len
    score_scale = head_dim ** (-0.5)
    cosine_table, sine_table = angle_tables(offset, span_len, head_dim)
    has_before = jnp.full((1,), lax.axis_index("ctx"), jnp.int32)
    total = sequences * span_len
    steps = total // ROWS
    span_steps = span_len // ROWS
    x = tokens.reshape(total, model_width)
    upstream = cotangent.reshape(total, model_width)
    gain_rows = jnp.stack([gain_first, gain_attn, gain_mlp, gain_final] + [gain_final] * 4)
    head_gain_rows = jnp.stack([gain_query, gain_key] + [gain_key] * 6)
    params = pltpu.CompilerParams(vmem_limit_bytes=VMEM_BYTES)
    whole = pl.BlockSpec(memory_space=pltpu.VMEM)

    def by_rows(columns):
        return pl.BlockSpec((ROWS, columns), lambda i: (i, 0))

    table = pl.BlockSpec((ROWS, head_dim // 2), lambda i: (i % span_steps, 0))

    def bf16(*shape):
        return jax.ShapeDtypeStruct(shape, jnp.bfloat16)

    def f32(*shape):
        return jax.ShapeDtypeStruct(shape, jnp.float32)

    query_low, key_low, value_low = pl.pallas_call(
        functools.partial(projection_kernel, head_dim),
        grid=(steps,),
        in_specs=[by_rows(model_width), whole, whole, whole, table, table],
        out_specs=[by_rows(query_columns), by_rows(head_dim), by_rows(head_dim)],
        out_shape=[bf16(total, query_columns), bf16(total, head_dim), bf16(total, head_dim)],
        compiler_params=params,
        name="projection",
    )(x, first_full, gain_rows, head_gain_rows, cosine_table, sine_table)
    key_prev, value_prev = shifted((key_low, value_low), "ctx", 1)
    flag = pl.BlockSpec(memory_space=pltpu.SMEM)
    head = pl.BlockSpec((span_len, head_dim), lambda s, h: (s, h))
    shared = pl.BlockSpec((span_len, head_dim), lambda s, h: (s, 0))
    attended_low = pl.pallas_call(
        functools.partial(attention_kernel, score_scale),
        grid=(sequences, head_count),
        in_specs=[flag, head, shared, shared, shared, shared],
        out_specs=head,
        out_shape=bf16(total, query_columns),
        compiler_params=params,
        name="attention",
    )(has_before, query_low, key_low, value_low, key_prev, value_prev)
    (
        block_output,
        grad_middle,
        grad_attended,
        middle_gains,
        grad_output_weight,
        grad_gate_weight,
        grad_up_weight,
        grad_down_weight,
    ) = pl.pallas_call(
        functools.partial(middle_kernel, 512),
        grid=(steps,),
        in_specs=[by_rows(model_width), by_rows(model_width), whole, whole, whole, whole, whole, whole],
        out_specs=[by_rows(model_width), by_rows(model_width), by_rows(query_columns)] + [whole] * 5,
        out_shape=[
            bf16(total, model_width),
            f32(total, model_width),
            bf16(total, query_columns),
            f32(8, model_width),
            bf16(query_columns, model_width),
            bf16(model_width, ff),
            bf16(model_width, ff),
            bf16(ff, model_width),
        ],
        scratch_shapes=[
            pltpu.VMEM((total, model_width), jnp.bfloat16),
            pltpu.VMEM((total, ff), jnp.bfloat16),
            pltpu.VMEM((total, model_width), jnp.bfloat16),
            pltpu.VMEM((total, ff), jnp.bfloat16),
            pltpu.VMEM((total, ff), jnp.bfloat16),
            pltpu.VMEM((total, model_width), jnp.bfloat16),
        ],
        compiler_params=params,
        name="middle",
    )(x, upstream, attended_low, output_full, gate_full, up_full, down_full, gain_rows)
    grad_query, grad_key, grad_value, key_send, value_send = pl.pallas_call(
        functools.partial(attention_back_kernel, score_scale),
        grid=(sequences, head_count),
        in_specs=[flag, head, shared, shared, shared, shared, head],
        out_specs=[head, shared, shared, shared, shared],
        out_shape=[f32(total, query_columns)] + [f32(total, head_dim)] * 4,
        compiler_params=params,
        name="attention_back",
    )(has_before, query_low, key_low, value_low, key_prev, value_prev, grad_attended)
    key_back, value_back = shifted(
        (key_send.astype(jnp.bfloat16), value_send.astype(jnp.bfloat16)), "ctx", -1
    )
    token_grad, grad_first_weight, norm_gains, head_gains = pl.pallas_call(
        functools.partial(head_back_kernel, head_dim),
        grid=(steps,),
        in_specs=[by_rows(model_width), whole, whole, whole, table, table, by_rows(query_columns)]
        + [by_rows(head_dim)] * 4
        + [by_rows(model_width)],
        out_specs=[by_rows(model_width), whole, whole, whole],
        out_shape=[
            bf16(total, model_width),
            bf16(model_width, qkv_columns),
            f32(8, model_width),
            f32(8, head_dim),
        ],
        scratch_shapes=[
            pltpu.VMEM((total, model_width), jnp.bfloat16),
            pltpu.VMEM((total, qkv_columns), jnp.bfloat16),
        ],
        compiler_params=params,
        name="head_back",
    )(
        x,
        first_full,
        gain_rows,
        head_gain_rows,
        cosine_table,
        sine_table,
        grad_query,
        grad_key,
        grad_value,
        key_back,
        value_back,
        grad_middle,
    )
    grad_norm_gain = norm_gains[0]
    grad_attn_gain, grad_mlp_gain, grad_final_gain = middle_gains[0], middle_gains[1], middle_gains[2]
    grad_query_gain, grad_key_gain = head_gains[0], head_gains[1]

    def to_shards(grad):
        return grad.astype(jnp.bfloat16).reshape(fsdp, rows, -1)

    rest_grads = jnp.concatenate(
        [
            to_shards(grad_gate_weight),
            to_shards(grad_up_weight),
            to_shards(grad_down_weight),
            to_shards(grad_output_weight),
        ],
        axis=2,
    ).reshape(fsdp * rows, -1)
    rest_sum = lax.psum_scatter(rest_grads, "fsdp", scatter_dimension=0, tiled=True)
    rest_sum = rest_sum.astype(jnp.float32) + shared_sum(rest_sum, "ctx")

    def head_gain(grad):
        return jnp.pad(grad.reshape(fsdp, head_rows), ((0, 0), (0, rows - head_rows))).reshape(-1)

    gain_grads = jnp.stack(
        [
            grad_norm_gain,
            grad_attn_gain,
            grad_mlp_gain,
            grad_final_gain,
            head_gain(grad_query_gain),
            head_gain(grad_key_gain),
        ],
        axis=1,
    )
    gain_grads = jnp.pad(gain_grads, ((0, 0), (0, LANES - gain_grads.shape[1])))
    first_grads = jnp.concatenate([grad_first_weight, gain_grads.astype(jnp.bfloat16)], axis=1)
    first_sum = scatter_pairs(first_grads.reshape(fsdp, rows, -1), "fsdp", ("ctx",))
    return (
        block_output.reshape(tokens.shape),
        token_grad.reshape(tokens.shape),
        first_sum[:, qkv_columns],
        first_sum[:, :query_columns],
        first_sum[:, query_columns : query_columns + head_dim],
        first_sum[:, query_columns + head_dim : qkv_columns],
        first_sum[:head_rows, qkv_columns + 4],
        first_sum[:head_rows, qkv_columns + 5],
        rest_sum[:, 3 * ff :].reshape(output_weight.shape),
        first_sum[:, qkv_columns + 1],
        first_sum[:, qkv_columns + 2],
        rest_sum[:, :ff],
        rest_sum[:, ff : 2 * ff],
        rest_sum[:, 2 * ff : 3 * ff].reshape(down_weight.shape),
        first_sum[:, qkv_columns + 3],
    )


def solution(mesh):
    return jax.shard_map(
        per_device,
        mesh=mesh,
        in_specs=(
            P("fsdp", "ctx", None),
            P("fsdp", "ctx", None),
            P("fsdp"),
            P("fsdp", None),
            P("fsdp", None),
            P("fsdp", None),
            P("fsdp"),
            P("fsdp"),
            P("fsdp", None),
            P("fsdp"),
            P("fsdp"),
            P("fsdp", None),
            P("fsdp", None),
            P("fsdp", None),
            P("fsdp"),
        ),
        out_specs=(
            P("fsdp", "ctx", None),
            P("fsdp", "ctx", None),
            P("fsdp"),
            P("fsdp", None),
            P("fsdp", None),
            P("fsdp", None),
            P("fsdp"),
            P("fsdp"),
            P("fsdp", None),
            P("fsdp"),
            P("fsdp"),
            P("fsdp", None),
            P("fsdp", None),
            P("fsdp", None),
            P("fsdp"),
        ),
        check_vma=False,
    )
```

```python
import functools

import jax
import jax.numpy as jnp
from jax import lax
from jax.experimental import pallas as pl
from jax.experimental.pallas import tpu as pltpu
from jax.sharding import PartitionSpec as P

WINDOW = 512


EPSILON = 1e-06
MASKED = -1e30
ROOT = (2.0 / jnp.pi) ** 0.5
ROWS = 256
VMEM_BYTES = 60 * 1024 * 1024


LANES = 128


def swap(value, axis, mask):
    count = lax.axis_size(axis)
    return lax.ppermute(value, axis, [(source, source ^ mask) for source in range(count)])


def after(value, *others):
    return lax.optimization_barrier((value, others))[0]


def widen(held, axis, mask, *others):
    return jnp.concatenate([held, after(swap(held, axis, mask), *others)], axis=0)


def places(axis):
    count = lax.axis_size(axis)
    relative = jnp.arange(count, dtype=jnp.int32) ^ lax.axis_index(axis)
    place = jnp.zeros((count,), jnp.int32)
    low, high = 0, count // 2
    while high > 1:
        place = place + jnp.where((relative & high) != 0, 1 << low, 0)
        low, high = low + 1, high // 2
    return place


def cost(flops, spent):
    return pl.CostEstimate(flops=int(flops / spent / 16), bytes_accessed=0, transcendentals=0)


def add(left, right):
    return (left.astype(jnp.float32) + right.astype(jnp.float32)).astype(jnp.bfloat16)


def folded(value, axis, mask, dim):
    kept, sent = jnp.split(value, 2, axis=dim)
    return kept, swap(sent, axis, mask)


def other_spans(value, axis):
    mask = 2
    while mask < lax.axis_size(axis):
        value = add(value, swap(value, axis, mask))
        mask *= 2
    return value


def shifted(value, axis, steps):
    count = lax.axis_size(axis)
    leading, last = (max(0, -steps), min(count, count - steps))
    return lax.ppermute(value, axis, [(source, source + steps) for source in range(leading, last)])


def dot(left, right):
    return jnp.dot(left, right, preferred_element_type=jnp.float32)


def dot_nt(left, right):
    return lax.dot_general(left, right, (((1,), (1,)), ((), ())), preferred_element_type=jnp.float32)


def dot_tn(left, right):
    return lax.dot_general(left, right, (((0,), (0,)), ((), ())), preferred_element_type=jnp.float32)


def inverse_rms(rows):
    return lax.rsqrt(jnp.mean(rows * rows, axis=-1, keepdims=True) + EPSILON)


def rms_back(rows, scale, gain, grad):
    weighted = gain * grad
    inner = jnp.mean(rows * weighted, axis=-1, keepdims=True)
    return scale * weighted - rows * (scale * scale * scale * inner), grad * rows * scale


def turn(rows, cosine, sine):
    half = rows.shape[-1] // 2
    front, back = rows[:, :half], rows[:, half:]
    return jnp.concatenate([front * cosine - back * sine, back * cosine + front * sine], axis=-1)


def turn_back(rows, cosine, sine):
    return turn(rows, cosine, -sine)


def each_core(core, body):
    for value in (0, 1):
        pl.when(core == value)(functools.partial(body, value))


def whole_block(ref, place):
    return [ref[place]]


def join_pairs(out_ref, near_ref, far_ref, core, info_ref, rows, read=whole_block):
    pairs = 1
    while (2 * rows * pairs) % 16:
        pairs *= 2
    size = 2 * rows * pairs

    def body(value):
        first, second = (near_ref, far_ref) if value == 0 else (far_ref, near_ref)

        def group(index, carry):
            blocks = []
            for pair in range(pairs):
                place = info_ref[2 * (index * pairs + pair)]
                blocks += read(first, place) + read(second, place)
            if rows % 8:
                blocks = [block.astype(jnp.float32) for block in blocks]
            lines = pl.ds(pl.multiple_of(index * size, size), size)
            out_ref[lines, :] = jnp.concatenate(blocks, axis=0).astype(jnp.bfloat16)
            return carry

        lax.fori_loop(0, near_ref.shape[0] // pairs, group, 0)

    each_core(core, body)


def projection_kernel(
    head_dim,
    columns,
    x_ref,
    xb_ref,
    near_ref,
    far_ref,
    pick_ref,
    info_ref,
    cos_ref,
    sin_ref,
    cosb_ref,
    sinb_ref,
    q_ref,
    k_ref,
    v_ref,
    kb_ref,
    vb_ref,
    w_ref,
    gain_ref,
    head_gain_ref,
    all_ref,
):
    count = info_ref.shape[0] - 3

    @pl.when(pl.program_id(0) == 0)
    def _():
        join_pairs(all_ref, near_ref, far_ref, info_ref[count], info_ref, near_ref.shape[1])
        w_ref[...] = all_ref[:, :columns]
        gains = all_ref[:, columns : columns + LANES].astype(jnp.float32).T[:8]
        gain_ref[...] = gains
        head_gain_ref[...] = dot(gains.astype(jnp.bfloat16), pick_ref[...])

    gain = gain_ref[0:1, :]
    queries = q_ref.shape[1]
    x = x_ref[...].astype(jnp.float32)
    normed = (x * inverse_rms(x) * gain).astype(jnp.bfloat16)
    x = xb_ref[...].astype(jnp.float32)
    normed_before = (x * inverse_rms(x) * gain).astype(jnp.bfloat16)
    key_part = slice(queries, queries + head_dim)
    value_part = slice(queries + head_dim, queries + 2 * head_dim)

    def turned(rows, part, head_gain, cosine, sine):
        raw = dot(rows, w_ref[:, part])
        return turn(raw * inverse_rms(raw) * head_gain, cosine, sine).astype(jnp.bfloat16)

    for start in range(0, queries, head_dim):
        part = slice(start, start + head_dim)
        q_ref[:, part] = turned(normed, part, head_gain_ref[4:5, :], cos_ref[...], sin_ref[...])
    k_ref[...] = turned(normed, key_part, head_gain_ref[5:6, :], cos_ref[...], sin_ref[...])
    v_ref[...] = dot(normed, w_ref[:, value_part]).astype(jnp.bfloat16)
    kb_ref[...] = turned(normed_before, key_part, head_gain_ref[5:6, :], cosb_ref[...], sinb_ref[...])
    vb_ref[...] = dot(normed_before, w_ref[:, value_part]).astype(jnp.bfloat16)


def window_parts(rows, now, before, has_before, product):
    half = rows.shape[0] // 2
    low = lax.broadcasted_iota(jnp.int32, (half, half), 1) <= lax.broadcasted_iota(
        jnp.int32, (half, half), 0
    )
    top, bottom = rows[:half], rows[half:]
    before_left = product(top, before[:half])
    before_right = product(top, before[half:])
    before_low = product(bottom, before[half:])
    if has_before is not None:
        before_left = jnp.where(has_before, before_left, MASKED)
        before_right = jnp.where(has_before, before_right, MASKED)
        before_low = jnp.where(has_before, before_low, MASKED)
    upper = jnp.concatenate([jnp.where(low, product(top, now[:half]), before_left), before_right], axis=1)
    lower = jnp.concatenate(
        [product(bottom, now[:half]), jnp.where(low, product(bottom, now[half:]), before_low)], axis=1
    )
    return jnp.concatenate([upper, lower], axis=0)


def window_split(matrix):
    half = matrix.shape[0] // 2
    low = lax.broadcasted_iota(jnp.int32, (half, half), 1) <= lax.broadcasted_iota(
        jnp.int32, (half, half), 0
    )
    first, last = matrix[:half, :half], matrix[half:, half:]
    zero = jnp.zeros_like(first)
    return (
        jnp.where(low, first, zero),
        jnp.where(low, zero, first),
        jnp.where(low, last, zero),
        jnp.where(low, zero, last),
        matrix[:half, half:],
        matrix[half:, :half],
    )


def window_apply(matrix, now, before):
    half = matrix.shape[0] // 2
    first_now, first_before, last_now, last_before, right, left = window_split(matrix)
    top = dot(first_now, now[:half]) + dot(first_before, before[:half]) + dot(right, before[half:])
    bottom = dot(left, now[:half]) + dot(last_now, now[half:]) + dot(last_before, before[half:])
    return jnp.concatenate([top, bottom], axis=0)


def window_apply_back(matrix, rows):
    half = matrix.shape[0] // 2
    first_now, first_before, last_now, last_before, right, left = window_split(matrix)
    top, bottom = rows[:half], rows[half:]
    now = jnp.concatenate([dot_tn(first_now, top) + dot_tn(left, bottom), dot_tn(last_now, bottom)], axis=0)
    before = jnp.concatenate(
        [dot_tn(first_before, top), dot_tn(right, top) + dot_tn(last_before, bottom)], axis=0
    )
    return now, before


def window_probs(query, key, key_before, has_before, scale):
    scores = window_parts(query, key, key_before, has_before, dot_nt) * scale
    terms = jnp.exp(scores - jnp.max(scores, axis=-1, keepdims=True))
    return terms * (1.0 / jnp.sum(terms, axis=-1, keepdims=True))


def attention_kernel(scale, flag_ref, q_ref, k_ref, v_ref, kb_ref, vb_ref, o_ref):
    has_before = flag_ref[flag_ref.shape[0] - 1] > 0
    probs = window_probs(q_ref[...], k_ref[...], kb_ref[...], has_before, scale)
    o_ref[...] = window_apply(probs.astype(jnp.bfloat16), v_ref[...], vb_ref[...]).astype(jnp.bfloat16)


def attention_back_kernel(scale, flag_ref, q_ref, k_ref, v_ref, kb_ref, vb_ref, do_ref, *refs):
    dq_ref, dk_ref, dv_ref, dkb_ref, dvb_ref = refs[-5:]
    has_before = flag_ref[flag_ref.shape[0] - 1] > 0
    query, grad = q_ref[...], do_ref[...]
    probs = window_probs(query, k_ref[...], kb_ref[...], has_before, scale)
    grad_probs = window_parts(grad, v_ref[...], vb_ref[...], None, dot_nt)
    inner = jnp.sum(grad_probs * probs, axis=-1, keepdims=True)
    grad_scores = (probs * (grad_probs - inner)).astype(jnp.bfloat16)
    dq_ref[...] = window_apply(grad_scores, k_ref[...], kb_ref[...]) * scale
    key_now, key_before = window_apply_back(grad_scores, query)
    value_now, value_before = window_apply_back(probs.astype(jnp.bfloat16), grad)

    @pl.when(pl.program_id(0) == 0)
    def _():
        dk_ref[...] = key_now * scale
        dkb_ref[...] = key_before * scale
        dv_ref[...] = value_now
        dvb_ref[...] = value_before

    @pl.when(pl.program_id(0) > 0)
    def _():
        dk_ref[...] += key_now * scale
        dkb_ref[...] += key_before * scale
        dv_ref[...] += value_now
        dvb_ref[...] += value_before


def middle_kernel(
    chunk,
    down_rows,
    x_ref,
    dy_ref,
    att_ref,
    rows_near,
    rows_far,
    mine_near,
    mine_far,
    other_near,
    other_far,
    gain_ref,
    info_ref,
    out_ref,
    dmid_ref,
    datt_ref,
    gain_grad_ref,
    wide_near,
    wide_far,
    tall_near,
    tall_far,
    wo_ref,
    wg_ref,
    wu_ref,
    wd_ref,
    mlp_all,
    hidden_all,
    dmlp_all,
    dgate_all,
    dup_all,
    dattn_all,
    sems,
):
    count = info_ref.shape[0] - 3
    core, span = info_ref[count], info_ref[count + 1]
    half = rows_near.shape[2]
    out_rows = 2 * half - down_rows
    feature_rows = mine_near.shape[1]

    @pl.when(pl.program_id(0) == 0)
    def _():
        copies = [
            pltpu.make_async_copy(source, target, sems.at[index])
            for index, (source, target) in enumerate(
                (
                    (rows_near, tall_near),
                    (rows_far, tall_far),
                    (mine_near, wide_near.at[0]),
                    (other_near, wide_near.at[1]),
                    (mine_far, wide_far.at[0]),
                    (other_far, wide_far.at[1]),
                )
            )
        ]
        for copy in copies:
            copy.start()
        for copy in copies:
            copy.wait()

        def down_block(ref, place):
            return [ref[place, 0], ref[place, 1, : down_rows - half]]

        def out_block(ref, place):
            return [ref[place, 1, down_rows - half :]]

        join_pairs(wd_ref, tall_near, tall_far, core, info_ref, down_rows, down_block)
        join_pairs(wo_ref, tall_near, tall_far, core, info_ref, out_rows, out_block)
        for value in (0, 1):
            first, second = (wg_ref, wu_ref) if value == 0 else (wu_ref, wg_ref)

            @pl.when(span == value)
            def _():
                join_pairs(first, wide_near.at[0], wide_far.at[0], core, info_ref, feature_rows)
                join_pairs(second, wide_near.at[1], wide_far.at[1], core, info_ref, feature_rows)

    step = pl.program_id(0)
    block = x_ref.shape[0]
    rows = pl.ds(pl.multiple_of(step * block, block), block)
    ff = wg_ref.shape[1]
    gain_attn, gain_mlp, gain_final = gain_ref[1:2, :], gain_ref[2:3, :], gain_ref[3:4, :]
    x = x_ref[...].astype(jnp.float32)
    raw = dot(att_ref[rows, :], wo_ref[...])
    raw_scale = inverse_rms(raw)
    middle = x + raw * raw_scale * gain_attn
    middle_scale = inverse_rms(middle)
    mlp_low = (middle * middle_scale * gain_mlp).astype(jnp.bfloat16)
    mlp_all[rows, :] = mlp_low
    kept = []
    mlp_raw = None
    for start in range(0, ff, chunk):
        part = slice(start, start + chunk)
        gate = dot(mlp_low, wg_ref[:, part])
        up = dot(mlp_low, wu_ref[:, part])
        square = gate * gate
        bend = jnp.tanh(ROOT * (gate + 0.044715 * (gate * square)))
        lift = 0.5 * (1.0 + bend)
        gelu = gate * lift
        slope = lift + (0.5 * ROOT) * gate * (1.0 - bend * bend) * (1.0 + (3 * 0.044715) * square)
        hidden = (gelu * up).astype(jnp.bfloat16)
        hidden_all[rows, part] = hidden
        kept.append((up * slope, gelu))
        term = dot(hidden, wd_ref[part, :])
        mlp_raw = term if mlp_raw is None else mlp_raw + term
    mlp_scale = inverse_rms(mlp_raw)
    out_ref[...] = (middle + mlp_raw * mlp_scale * gain_final).astype(jnp.bfloat16)
    dy = dy_ref[...].astype(jnp.float32)
    grad_raw, final_rows = rms_back(mlp_raw, mlp_scale, gain_final, dy)
    dmlp_low = grad_raw.astype(jnp.bfloat16)
    dmlp_all[rows, :] = dmlp_low
    grad_in = None
    for index, start in enumerate(range(0, ff, chunk)):
        part = slice(start, start + chunk)
        grad_hidden = dot_nt(dmlp_low, wd_ref[part, :])
        up_slope, gelu = kept[index]
        dgate = (grad_hidden * up_slope).astype(jnp.bfloat16)
        dup = (grad_hidden * gelu).astype(jnp.bfloat16)
        dgate_all[rows, part] = dgate
        dup_all[rows, part] = dup
        term = dot_nt(dgate, wg_ref[:, part]) + dot_nt(dup, wu_ref[:, part])
        grad_in = term if grad_in is None else grad_in + term
    grad_middle, mlp_rows = rms_back(middle, middle_scale, gain_mlp, grad_in)
    grad_middle = dy + grad_middle
    dmid_ref[...] = grad_middle
    grad_attn, attn_rows = rms_back(raw, raw_scale, gain_attn, grad_middle)
    dattn_low = grad_attn.astype(jnp.bfloat16)
    dattn_all[rows, :] = dattn_low
    datt_ref[...] = dot_nt(dattn_low, wo_ref[...]).astype(jnp.bfloat16)
    sums = [jnp.sum(part, axis=0, keepdims=True) for part in (attn_rows, mlp_rows, final_rows)]
    gain_sums = jnp.concatenate(sums + [jnp.zeros((8 - len(sums), x.shape[1]), jnp.float32)], axis=0)

    @pl.when(step == 0)
    def _():
        gain_grad_ref[...] = gain_sums

    @pl.when(step > 0)
    def _():
        gain_grad_ref[...] += gain_sums

    @pl.when(step == pl.num_programs(0) - 1)
    def _():
        for start in range(0, ff, chunk):
            part = slice(start, start + chunk)
            gate_grad = dot_tn(mlp_all[...], dgate_all[:, part])
            up_grad = dot_tn(mlp_all[...], dup_all[:, part])
            down_grad = dot_tn(hidden_all[:, part], dmlp_all[...]).astype(jnp.bfloat16)

            def store(value):
                for index in range(0, count, 2):
                    place = info_ref[index]
                    for other in (0, 1):
                        to = wide_near if other == value else wide_far
                        lines = slice((index + other) * feature_rows, (index + other + 1) * feature_rows)
                        to[span, place, :, part] = gate_grad[lines].astype(jnp.bfloat16)
                        to[1 - span, place, :, part] = up_grad[lines].astype(jnp.bfloat16)
                for line in range(0, chunk, down_rows):
                    index = (start + line) // down_rows
                    to = tall_near if index % 2 == value else tall_far
                    place = info_ref[index]
                    to[place, span] = down_grad[line : line + half]
                    to[place, 1 - span, : down_rows - half] = down_grad[line + half : line + down_rows]

            each_core(core, store)
        for start in range(0, wo_ref.shape[0], chunk):
            part = slice(start, start + chunk)
            out_grad = dot_tn(att_ref[:, part], dattn_all[...]).astype(jnp.bfloat16)

            def store_out(value):
                for line in range(0, chunk, out_rows):
                    index = (start + line) // out_rows
                    to = tall_near if index % 2 == value else tall_far
                    to[info_ref[index], 1 - span, down_rows - half :] = out_grad[line : line + out_rows]

            each_core(core, store_out)


def head_back_kernel(
    head_dim,
    x_ref,
    xb_ref,
    w_ref,
    gain_ref,
    head_gain_ref,
    pick_ref,
    middle_gain_ref,
    info_ref,
    cos_ref,
    sin_ref,
    cosb_ref,
    sinb_ref,
    dq_ref,
    dk_ref,
    dv_ref,
    dkb_ref,
    dvb_ref,
    dmid_ref,
    token_ref,
    before_ref,
    near_ref,
    far_ref,
    normed_all,
    draw_all,
    normed_before_all,
    draw_before_all,
    gain_sum,
    head_sum,
    grad_all,
):
    step = pl.program_id(0)
    block = x_ref.shape[0]
    rows = pl.ds(pl.multiple_of(step * block, block), block)
    queries = dq_ref.shape[1]
    keys = slice(queries, queries + head_dim)
    pair = slice(queries, queries + 2 * head_dim)
    norm_gain = gain_ref[0:1, :]
    query_gain, key_gain = head_gain_ref[4:5, :], head_gain_ref[5:6, :]
    x = x_ref[...].astype(jnp.float32)
    x_scale = inverse_rms(x)
    normed = (x * x_scale * norm_gain).astype(jnp.bfloat16)
    normed_all[rows, :] = normed
    cosine, sine = cos_ref[...], sin_ref[...]
    query_rows = None
    for start in range(0, queries, head_dim):
        part = slice(start, start + head_dim)
        raw = dot(normed, w_ref[:, part])
        grad = turn_back(dq_ref[:, part], cosine, sine)
        grad_raw, head_rows = rms_back(raw, inverse_rms(raw), query_gain, grad)
        query_rows = head_rows if query_rows is None else query_rows + head_rows
        draw_all[rows, part] = grad_raw.astype(jnp.bfloat16)
    raw = dot(normed, w_ref[:, keys])
    grad_raw, key_rows = rms_back(raw, inverse_rms(raw), key_gain, turn_back(dk_ref[...], cosine, sine))
    draw_all[rows, keys] = grad_raw.astype(jnp.bfloat16)
    draw_all[rows, queries + head_dim : queries + 2 * head_dim] = dv_ref[...].astype(jnp.bfloat16)
    grad_normed = dot_nt(draw_all[rows, :], w_ref[...])
    grad_x, norm_rows = rms_back(x, x_scale, norm_gain, grad_normed)
    token_ref[...] = dmid_ref[...] + grad_x

    xb = xb_ref[...].astype(jnp.float32)
    xb_scale = inverse_rms(xb)
    normed_before = (xb * xb_scale * norm_gain).astype(jnp.bfloat16)
    normed_before_all[rows, :] = normed_before
    raw = dot(normed_before, w_ref[:, keys])
    grad = turn_back(dkb_ref[...], cosb_ref[...], sinb_ref[...])
    grad_raw, key_before_rows = rms_back(raw, inverse_rms(raw), key_gain, grad)
    draw_before = jnp.concatenate([grad_raw, dvb_ref[...]], axis=1).astype(jnp.bfloat16)
    draw_before_all[rows, :] = draw_before
    grad_xb, norm_before_rows = rms_back(xb, xb_scale, norm_gain, dot_nt(draw_before, w_ref[:, pair]))
    before_ref[...] = grad_xb.astype(jnp.bfloat16)

    norm_sums = jnp.sum(norm_rows + norm_before_rows, axis=0, keepdims=True)
    head_sums = jnp.concatenate(
        [
            jnp.zeros((4, head_dim), jnp.float32),
            jnp.sum(query_rows, axis=0, keepdims=True),
            jnp.sum(key_rows + key_before_rows, axis=0, keepdims=True),
            jnp.zeros((2, head_dim), jnp.float32),
        ],
        axis=0,
    )

    @pl.when(step == 0)
    def _():
        gain_sum[...] = jnp.zeros_like(gain_sum)
        gain_sum[0:1, :] = norm_sums
        gain_sum[1:4, :] = middle_gain_ref[0:3, :]
        head_sum[...] = head_sums

    @pl.when(step > 0)
    def _():
        gain_sum[0:1, :] += norm_sums
        head_sum[...] += head_sums

    @pl.when(step == pl.num_programs(0) - 1)
    def _():
        count = info_ref.shape[0] - 3
        core, span = info_ref[count], info_ref[count + 1]
        total = queries + 2 * head_dim
        feature_rows = near_ref.shape[2]
        half = near_ref.shape[3]
        for start in range(0, queries, 512):
            part = slice(start, start + 512)
            grad_all[:, part] = dot_tn(normed_all[...], draw_all[:, part])
        grad_all[:, pair] = dot_tn(normed_all[...], draw_all[:, pair]) + dot_tn(
            normed_before_all[...], draw_before_all[...]
        )
        heads = dot_nt(head_sum[...].astype(jnp.bfloat16), pick_ref[...])
        sums = jnp.concatenate(
            [gain_sum[...] + heads, jnp.zeros((LANES - gain_sum.shape[0], gain_sum.shape[1]), jnp.float32)],
            axis=0,
        )
        grad_all[:, total : total + LANES] = sums.T
        grad_all[:, total + LANES :] = jnp.zeros((grad_all.shape[0], grad_all.shape[1] - total - LANES), jnp.float32)

        def store(value):
            for index in range(count):
                to = near_ref if index % 2 == value else far_ref
                place = info_ref[index]
                lines = slice(index * feature_rows, (index + 1) * feature_rows)
                to[span, place] = grad_all[lines, :half].astype(jnp.bfloat16)
                to[1 - span, place] = grad_all[lines, half:].astype(jnp.bfloat16)

        each_core(core, store)


def angle_tables(offset, length_rows, head_dim):
    half_dim = head_dim // 2
    frequency = 10000.0 ** (-(jnp.arange(half_dim).astype(jnp.float32) * 2.0 / head_dim))
    positions = (offset + jnp.arange(length_rows)).astype(jnp.float32)
    angles = positions[:, None] * frequency[None, :]
    return (jnp.cos(angles), jnp.sin(angles))


def per_device(
    tokens,
    cotangent,
    norm_gain,
    query_weight,
    key_weight,
    value_weight,
    query_norm,
    key_norm,
    output_weight,
    attn_post_gain,
    mlp_pre_gain,
    gate_weight,
    up_weight,
    down_weight,
    mlp_post_gain,
):
    fsdp = lax.axis_size("fsdp")
    rows = norm_gain.shape[0]
    head_rows = query_norm.shape[0]
    gain_columns = jnp.stack(
        [
            norm_gain,
            attn_post_gain,
            mlp_pre_gain,
            mlp_post_gain,
            jnp.pad(query_norm, (0, rows - head_rows)),
            jnp.pad(key_norm, (0, rows - head_rows)),
        ],
        axis=1,
    )
    query_columns = query_weight.shape[1]
    head_dim = key_weight.shape[1]
    ff = gate_weight.shape[1]
    qkv_columns = query_columns + 2 * head_dim
    first_columns = -(-(qkv_columns + LANES) // (2 * LANES)) * 2 * LANES
    gain_columns = jnp.pad(
        gain_columns, ((0, 0), (0, first_columns - qkv_columns - gain_columns.shape[1]))
    )
    first_shard = jnp.concatenate([query_weight, key_weight, value_weight, gain_columns], axis=1)
    tall_shard = jnp.concatenate([down_weight, output_weight], axis=0)
    core = lax.axis_index("fsdp") & 1
    span = lax.axis_index("ctx") & 1
    low_span = span == 0
    info = jnp.concatenate(
        [
            places("fsdp"),
            jnp.stack([core, span, (lax.axis_index("ctx") > 0).astype(jnp.int32)]),
        ]
    )
    sequences, span_len, model_width = tokens.shape
    head_count = query_columns // head_dim
    assert span_len == WINDOW
    offset = lax.axis_index("ctx") * span_len
    score_scale = head_dim ** (-0.5)
    tables = angle_tables(offset, span_len, head_dim)
    tables_before = angle_tables(offset - span_len, span_len, head_dim)
    row = jnp.arange(fsdp * rows)
    pick = (
        (row[:, None] // rows == jnp.arange(head_dim)[None, :] // head_rows)
        & (row[:, None] % rows == jnp.arange(head_dim)[None, :] % head_rows)
    ).astype(jnp.bfloat16)
    chip_masks = [1 << bit for bit in range(fsdp.bit_length() - 2, 0, -1)]
    before = shifted(tokens, "ctx", 1)
    first_shard, info, pick, tables, tables_before = lax.optimization_barrier(
        (first_shard, info, pick, tables, tables_before)
    )
    mine_near = jnp.where(low_span, gate_weight, up_weight)[None]
    first_near, tall_near = first_shard[None], tall_shard[None]
    for mask in chip_masks:
        first_near = widen(first_near, "fsdp", mask)
        mine_near = widen(mine_near, "fsdp", mask, first_near)
        if mask != chip_masks[-1]:
            tall_near = widen(tall_near, "fsdp", mask, mine_near)
            mine_near = after(mine_near, tall_near)
    first_far = swap(first_near, "fsdp", 1)
    mine_far = swap(mine_near, "fsdp", 1)
    other_near = swap(mine_near, "ctx", 1)
    tall_late = swap(tall_near, "fsdp", chip_masks[-1])
    total = sequences * span_len
    steps = total // ROWS
    span_steps = span_len // ROWS
    x = tokens.reshape(total, model_width)
    x_before = before.reshape(total, model_width)
    upstream = cotangent.reshape(total, model_width)
    params = pltpu.CompilerParams(vmem_limit_bytes=VMEM_BYTES)
    whole = pl.BlockSpec(memory_space=pltpu.VMEM)
    scalars = pl.BlockSpec(memory_space=pltpu.SMEM)

    def by_rows(columns):
        return pl.BlockSpec((ROWS, columns), lambda i: (i, 0))

    table = pl.BlockSpec((ROWS, head_dim // 2), lambda i: (i % span_steps, 0))

    def bf16(*shape):
        return jax.ShapeDtypeStruct(shape, jnp.bfloat16)

    def f32(*shape):
        return jax.ShapeDtypeStruct(shape, jnp.float32)

    def scratch(*shape):
        return pltpu.VMEM(shape, jnp.bfloat16)

    one_head = by_rows(head_dim)
    model = by_rows(model_width)
    (
        query_low,
        key_low,
        value_low,
        key_prev,
        value_prev,
        first_full,
        gain_rows,
        head_gain_rows,
    ) = pl.pallas_call(
        functools.partial(projection_kernel, head_dim, qkv_columns),
        grid=(steps,),
        in_specs=[model, model, whole, whole, whole, scalars] + [table] * 4,
        out_specs=[by_rows(query_columns)] + [one_head] * 4 + [whole] * 3,
        out_shape=[bf16(total, query_columns)]
        + [bf16(total, head_dim)] * 4
        + [bf16(model_width, qkv_columns), f32(8, model_width), f32(8, head_dim)],
        scratch_shapes=[scratch(model_width, first_columns)],
        compiler_params=params,
        cost_estimate=cost(2 * total * model_width * (qkv_columns + 2 * head_dim), 0.25),
        name="projection",
    )(x, x_before, first_near, first_far, pick, info, *tables, *tables_before)
    other_near = after(other_near, query_low)
    other_far = swap(other_near, "fsdp", 1)
    tall_near = jnp.concatenate([tall_near, after(tall_late, query_low)], axis=0)
    tall_far = swap(tall_near, "fsdp", 1)
    head = pl.BlockSpec((span_len, head_dim), lambda s, h: (s, h))
    shared = pl.BlockSpec((span_len, head_dim), lambda s, h: (s, 0))
    attended_low = pl.pallas_call(
        functools.partial(attention_kernel, score_scale),
        grid=(sequences, head_count),
        in_specs=[scalars, head, shared, shared, shared, shared],
        out_specs=head,
        out_shape=bf16(total, query_columns),
        compiler_params=params,
        cost_estimate=cost(3 * total * span_len * query_columns, 0.14),
        name="attention",
    )(info, query_low, key_low, value_low, key_prev, value_prev)
    down_rows, out_rows = down_weight.shape[0], output_weight.shape[0]
    half_rows = (down_rows + out_rows) // 2
    chips = fsdp // 2
    (
        block_output,
        grad_middle,
        grad_attended,
        middle_gains,
        wide_grad_near,
        wide_grad_far,
        tall_grad_near,
        tall_grad_far,
    ) = pl.pallas_call(
        functools.partial(middle_kernel, 512, down_rows),
        grid=(steps,),
        in_specs=[model, model, whole] + [pl.BlockSpec(memory_space=pl.ANY)] * 6 + [whole, scalars],
        out_specs=[model, model, by_rows(query_columns)] + [whole] * 5,
        out_shape=[
            bf16(total, model_width),
            f32(total, model_width),
            bf16(total, query_columns),
            f32(8, model_width),
            bf16(2, chips, rows, ff),
            bf16(2, chips, rows, ff),
            bf16(chips, 2, half_rows, model_width),
            bf16(chips, 2, half_rows, model_width),
        ],
        scratch_shapes=[
            scratch(query_columns, model_width),
            scratch(model_width, ff),
            scratch(model_width, ff),
            scratch(ff, model_width),
            scratch(total, model_width),
            scratch(total, ff),
            scratch(total, model_width),
            scratch(total, ff),
            scratch(total, ff),
            scratch(total, model_width),
            pltpu.SemaphoreType.DMA((6,)),
        ],
        compiler_params=params,
        cost_estimate=cost(6 * total * model_width * (3 * ff + query_columns), 0.4),
        name="middle",
    )(
        x,
        upstream,
        attended_low,
        tall_near.reshape(chips, 2, half_rows, model_width),
        tall_far.reshape(chips, 2, half_rows, model_width),
        mine_near,
        mine_far,
        other_near,
        other_far,
        gain_rows,
        info,
    )
    far_mask, near_masks = chip_masks[0], chip_masks[:0:-1]
    wide_far_sum = swap(wide_grad_far, "fsdp", 1)
    tall_far_sum = swap(tall_grad_far, "fsdp", 1)

    def attention_back(sequence, grad, done):
        one = pl.BlockSpec((span_len, head_dim), lambda h: (sequence, h))
        for_all = pl.BlockSpec((span_len, head_dim), lambda h: (sequence, 0))
        return pl.pallas_call(
            functools.partial(attention_back_kernel, score_scale),
            grid=(head_count,),
            in_specs=[scalars, one] + [for_all] * 4 + [one] + [pl.BlockSpec(memory_space=pl.ANY)] * len(done),
            out_specs=[one] + [for_all] * 4,
            out_shape=[f32(total, query_columns)] + [f32(total, head_dim)] * 4,
            input_output_aliases={7 + index: index for index in range(len(done))},
            compiler_params=params,
            cost_estimate=cost(7.5 * span_len * span_len * query_columns, 0.2),
            name="attention_back",
        )(info, query_low, key_low, value_low, key_prev, value_prev, grad, *done)

    back = attention_back(0, grad_attended, ())
    wide_far_sum, tall_far_sum = after((wide_far_sum, tall_far_sum), back[0])
    wide = add(wide_grad_near, wide_far_sum)
    tall = add(tall_grad_near, tall_far_sum)
    bits = (2,) * len(chip_masks)
    wide = wide.reshape((2,) + bits + wide.shape[2:])
    tall = tall.reshape(bits + tall.shape[1:])
    wide_kept, wide_come = folded(wide, "fsdp", near_masks[0], 1)
    tall_kept, tall_come = folded(tall, "fsdp", near_masks[1], 1)
    wide, tall, grad_attended = lax.optimization_barrier((wide, tall, grad_attended))
    for sequence in range(1, sequences):
        back = attention_back(sequence, grad_attended, back)
    grad_query, grad_key, grad_value, key_send, value_send = back
    token_part, before_part, first_grad_near, first_grad_far = pl.pallas_call(
        functools.partial(head_back_kernel, head_dim),
        grid=(steps,),
        in_specs=[model, model]
        + [whole] * 5
        + [scalars]
        + [table] * 4
        + [by_rows(query_columns)]
        + [one_head] * 4
        + [model],
        out_specs=[model, model, whole, whole],
        out_shape=[
            f32(total, model_width),
            bf16(total, model_width),
            bf16(2, chips, rows, first_columns // 2),
            bf16(2, chips, rows, first_columns // 2),
        ],
        scratch_shapes=[
            scratch(total, model_width),
            scratch(total, qkv_columns),
            scratch(total, model_width),
            scratch(total, 2 * head_dim),
            pltpu.VMEM((8, model_width), jnp.float32),
            pltpu.VMEM((8, head_dim), jnp.float32),
            pltpu.VMEM((model_width, first_columns), jnp.float32),
        ],
        compiler_params=params,
        cost_estimate=cost(6 * total * model_width * (qkv_columns + 2 * head_dim), 0.38),
        name="head_back",
    )(
        x,
        x_before,
        first_full,
        gain_rows,
        head_gain_rows,
        pick,
        middle_gains,
        info,
        *tables,
        *tables_before,
        grad_query,
        grad_key,
        grad_value,
        key_send,
        value_send,
        grad_middle,
    )
    tall = add(tall_kept, after(tall_come, token_part))
    wide = add(wide_kept, after(wide_come, token_part))
    first_grad_far, before_part = after((first_grad_far, before_part), tall, wide)
    tall_kept, tall_come = folded(tall, "fsdp", near_masks[0], 0)
    wide_kept, wide_come = folded(wide, "fsdp", near_masks[1], 2)
    before_come = shifted(before_part, "ctx", -1)
    first = add(first_grad_near, swap(first_grad_far, "fsdp", 1))
    first = first.reshape((2,) + bits + first.shape[2:])
    first_kept, first_come = folded(first, "fsdp", near_masks[0], 1)
    first = add(first_kept, first_come)
    first_kept, first_come = folded(first, "fsdp", near_masks[1], 2)
    tall = add(tall_kept, after(tall_come, first))
    tall_kept, tall_come = folded(tall, "ctx", 1, len(bits))
    wide = add(wide_kept, after(wide_come, tall))
    wide_kept, wide_come = folded(wide, "ctx", 1, 0)
    first = add(first_kept, after(first_come, wide))
    first_kept, first_come = folded(first, "ctx", 1, 0)
    tall = add(tall_kept, after(tall_come, first))
    wide = add(wide_kept, after(wide_come, tall))
    first = add(first_kept, after(first_come, wide))
    for index in range(2, len(bits)):
        mask = (near_masks + [far_mask])[index]
        tall_kept, tall_come = folded(tall, "fsdp", mask, index)
        wide_kept, wide_come = folded(wide, "fsdp", mask, index + 1)
        first_kept, first_come = folded(first, "fsdp", mask, index + 1)
        tall = add(tall_kept, tall_come)
        wide = add(wide_kept, after(wide_come, tall))
        first = add(first_kept, after(first_come, wide))
    tall = other_spans(tall.reshape(tall.shape[-2:]), "ctx")
    wide = other_spans(wide.reshape(wide.shape[-2:]), "ctx")
    first = other_spans(first.reshape(first.shape[-2:]), "ctx")
    before_come = after(before_come, first)
    token_grad = (token_part + before_come.astype(jnp.float32)).astype(jnp.bfloat16)

    def both(mine):
        other = swap(mine, "ctx", 1)
        left = jnp.where(low_span, mine, other).astype(jnp.float32)
        right = jnp.where(low_span, other, mine).astype(jnp.float32)
        return left, right

    grad_gate, grad_up = both(wide)
    grad_tall = jnp.concatenate(both(tall), axis=0)
    grad_first = jnp.concatenate(both(first), axis=1)
    return (
        block_output.reshape(tokens.shape),
        token_grad.reshape(tokens.shape),
        grad_first[:, qkv_columns],
        grad_first[:, :query_columns],
        grad_first[:, query_columns : query_columns + head_dim],
        grad_first[:, query_columns + head_dim : qkv_columns],
        grad_first[:head_rows, qkv_columns + 4],
        grad_first[:head_rows, qkv_columns + 5],
        grad_tall[down_rows:],
        grad_first[:, qkv_columns + 1],
        grad_first[:, qkv_columns + 2],
        grad_gate,
        grad_up,
        grad_tall[:down_rows],
        grad_first[:, qkv_columns + 3],
    )


def solution(mesh):
    return jax.shard_map(
        per_device,
        mesh=mesh,
        in_specs=(
            P("fsdp", "ctx", None),
            P("fsdp", "ctx", None),
            P("fsdp"),
            P("fsdp", None),
            P("fsdp", None),
            P("fsdp", None),
            P("fsdp"),
            P("fsdp"),
            P("fsdp", None),
            P("fsdp"),
            P("fsdp"),
            P("fsdp", None),
            P("fsdp", None),
            P("fsdp", None),
            P("fsdp"),
        ),
        out_specs=(
            P("fsdp", "ctx", None),
            P("fsdp", "ctx", None),
            P("fsdp"),
            P("fsdp", None),
            P("fsdp", None),
            P("fsdp", None),
            P("fsdp"),
            P("fsdp"),
            P("fsdp", None),
            P("fsdp"),
            P("fsdp"),
            P("fsdp", None),
            P("fsdp", None),
            P("fsdp", None),
            P("fsdp"),
        ),
        check_vma=False,
    )
```

```python
import functools

import jax
import jax.numpy as jnp
from jax import lax
from jax.experimental import pallas as pl
from jax.experimental.pallas import tpu as pltpu
from jax.sharding import PartitionSpec as P

WINDOW = 512


EPSILON = 1e-06
MASKED = -1e30
ROOT = (2.0 / jnp.pi) ** 0.5
ROWS = 256
VMEM_BYTES = 60 * 1024 * 1024


LANES = 128


def swap(value, axis, mask):
    count = lax.axis_size(axis)
    return lax.ppermute(value, axis, [(source, source ^ mask) for source in range(count)])


def after(value, *others):
    return lax.optimization_barrier((value, others))[0]


def widen(held, axis, mask, *others):
    return jnp.concatenate([held, after(swap(held, axis, mask), *others)], axis=0)


def places(axis):
    count = lax.axis_size(axis)
    relative = jnp.arange(count, dtype=jnp.int32) ^ lax.axis_index(axis)
    place = jnp.zeros((count,), jnp.int32)
    low, high = 0, count // 2
    while high > 1:
        place = place + jnp.where((relative & high) != 0, 1 << low, 0)
        low, high = low + 1, high // 2
    return place


def cost(flops, spent):
    return pl.CostEstimate(flops=int(flops / spent / 16), bytes_accessed=0, transcendentals=0)


def add(left, right):
    return (left.astype(jnp.float32) + right.astype(jnp.float32)).astype(jnp.bfloat16)


def folded(value, axis, mask, dim):
    kept, sent = jnp.split(value, 2, axis=dim)
    return kept, swap(sent, axis, mask)


def other_spans(value, axis):
    mask = 2
    while mask < lax.axis_size(axis):
        value = add(value, swap(value, axis, mask))
        mask *= 2
    return value


def shifted(value, axis, steps):
    count = lax.axis_size(axis)
    leading, last = (max(0, -steps), min(count, count - steps))
    return lax.ppermute(value, axis, [(source, source + steps) for source in range(leading, last)])


def dot(left, right):
    return jnp.dot(left, right, preferred_element_type=jnp.float32)


def dot_nt(left, right):
    return lax.dot_general(left, right, (((1,), (1,)), ((), ())), preferred_element_type=jnp.float32)


def dot_tn(left, right):
    return lax.dot_general(left, right, (((0,), (0,)), ((), ())), preferred_element_type=jnp.float32)


def inverse_rms(rows):
    return lax.rsqrt(jnp.mean(rows * rows, axis=-1, keepdims=True) + EPSILON)


def rms_back(rows, scale, gain, grad):
    weighted = gain * grad
    inner = jnp.mean(rows * weighted, axis=-1, keepdims=True)
    return scale * weighted - rows * (scale * scale * scale * inner), grad * rows * scale


def turn(rows, cosine, sine):
    half = rows.shape[-1] // 2
    front, back = rows[:, :half], rows[:, half:]
    return jnp.concatenate([front * cosine - back * sine, back * cosine + front * sine], axis=-1)


def turn_back(rows, cosine, sine):
    return turn(rows, cosine, -sine)


def each_core(core, body):
    for value in (0, 1):
        pl.when(core == value)(functools.partial(body, value))


def whole_block(ref, place):
    return [ref[place]]


def join_pairs(out_ref, near_ref, far_ref, core, info_ref, rows, read=whole_block):
    pairs = 1
    while (2 * rows * pairs) % 16:
        pairs *= 2
    size = 2 * rows * pairs

    def body(value):
        first, second = (near_ref, far_ref) if value == 0 else (far_ref, near_ref)

        def group(index, carry):
            blocks = []
            for pair in range(pairs):
                place = info_ref[2 * (index * pairs + pair)]
                blocks += read(first, place) + read(second, place)
            if rows % 8:
                blocks = [block.astype(jnp.float32) for block in blocks]
            lines = pl.ds(pl.multiple_of(index * size, size), size)
            out_ref[lines, :] = jnp.concatenate(blocks, axis=0).astype(jnp.bfloat16)
            return carry

        lax.fori_loop(0, near_ref.shape[0] // pairs, group, 0)

    each_core(core, body)


def projection_kernel(
    head_dim,
    columns,
    x_ref,
    xb_ref,
    near_ref,
    far_ref,
    pick_ref,
    info_ref,
    cos_ref,
    sin_ref,
    cosb_ref,
    sinb_ref,
    q_ref,
    k_ref,
    v_ref,
    kb_ref,
    vb_ref,
    w_ref,
    gain_ref,
    head_gain_ref,
    all_ref,
):
    count = info_ref.shape[0] - 3

    @pl.when(pl.program_id(0) == 0)
    def _():
        join_pairs(all_ref, near_ref, far_ref, info_ref[count], info_ref, near_ref.shape[1])
        w_ref[...] = all_ref[:, :columns]
        gains = all_ref[:, columns : columns + LANES].astype(jnp.float32).T[:8]
        gain_ref[...] = gains
        head_gain_ref[...] = dot(gains.astype(jnp.bfloat16), pick_ref[...])

    gain = gain_ref[0:1, :]
    queries = q_ref.shape[1]
    x = x_ref[...].astype(jnp.float32)
    normed = (x * inverse_rms(x) * gain).astype(jnp.bfloat16)
    x = xb_ref[...].astype(jnp.float32)
    normed_before = (x * inverse_rms(x) * gain).astype(jnp.bfloat16)
    key_part = slice(queries, queries + head_dim)
    value_part = slice(queries + head_dim, queries + 2 * head_dim)

    def turned(rows, part, head_gain, cosine, sine):
        raw = dot(rows, w_ref[:, part])
        return turn(raw * inverse_rms(raw) * head_gain, cosine, sine).astype(jnp.bfloat16)

    for start in range(0, queries, head_dim):
        part = slice(start, start + head_dim)
        q_ref[:, part] = turned(normed, part, head_gain_ref[4:5, :], cos_ref[...], sin_ref[...])
    k_ref[...] = turned(normed, key_part, head_gain_ref[5:6, :], cos_ref[...], sin_ref[...])
    v_ref[...] = dot(normed, w_ref[:, value_part]).astype(jnp.bfloat16)
    kb_ref[...] = turned(normed_before, key_part, head_gain_ref[5:6, :], cosb_ref[...], sinb_ref[...])
    vb_ref[...] = dot(normed_before, w_ref[:, value_part]).astype(jnp.bfloat16)


def window_parts(rows, now, before, has_before, product):
    half = rows.shape[0] // 2
    low = lax.broadcasted_iota(jnp.int32, (half, half), 1) <= lax.broadcasted_iota(
        jnp.int32, (half, half), 0
    )
    top, bottom = rows[:half], rows[half:]
    before_left = product(top, before[:half])
    before_right = product(top, before[half:])
    before_low = product(bottom, before[half:])
    if has_before is not None:
        before_left = jnp.where(has_before, before_left, MASKED)
        before_right = jnp.where(has_before, before_right, MASKED)
        before_low = jnp.where(has_before, before_low, MASKED)
    upper = jnp.concatenate([jnp.where(low, product(top, now[:half]), before_left), before_right], axis=1)
    lower = jnp.concatenate(
        [product(bottom, now[:half]), jnp.where(low, product(bottom, now[half:]), before_low)], axis=1
    )
    return jnp.concatenate([upper, lower], axis=0)


def window_split(matrix):
    half = matrix.shape[0] // 2
    low = lax.broadcasted_iota(jnp.int32, (half, half), 1) <= lax.broadcasted_iota(
        jnp.int32, (half, half), 0
    )
    first, last = matrix[:half, :half], matrix[half:, half:]
    zero = jnp.zeros_like(first)
    return (
        jnp.where(low, first, zero),
        jnp.where(low, zero, first),
        jnp.where(low, last, zero),
        jnp.where(low, zero, last),
        matrix[:half, half:],
        matrix[half:, :half],
    )


def window_apply(matrix, now, before):
    half = matrix.shape[0] // 2
    first_now, first_before, last_now, last_before, right, left = window_split(matrix)
    top = dot(first_now, now[:half]) + dot(first_before, before[:half]) + dot(right, before[half:])
    bottom = dot(left, now[:half]) + dot(last_now, now[half:]) + dot(last_before, before[half:])
    return jnp.concatenate([top, bottom], axis=0)


def window_apply_back(matrix, rows):
    half = matrix.shape[0] // 2
    first_now, first_before, last_now, last_before, right, left = window_split(matrix)
    top, bottom = rows[:half], rows[half:]
    now = jnp.concatenate([dot_tn(first_now, top) + dot_tn(left, bottom), dot_tn(last_now, bottom)], axis=0)
    before = jnp.concatenate(
        [dot_tn(first_before, top), dot_tn(right, top) + dot_tn(last_before, bottom)], axis=0
    )
    return now, before


def window_probs(query, key, key_before, has_before, scale):
    scores = window_parts(query, key, key_before, has_before, dot_nt) * scale
    terms = jnp.exp(scores - jnp.max(scores, axis=-1, keepdims=True))
    return terms * (1.0 / jnp.sum(terms, axis=-1, keepdims=True))


def attention_kernel(scale, flag_ref, q_ref, k_ref, v_ref, kb_ref, vb_ref, o_ref):
    has_before = flag_ref[flag_ref.shape[0] - 1] > 0
    probs = window_probs(q_ref[...], k_ref[...], kb_ref[...], has_before, scale)
    o_ref[...] = window_apply(probs.astype(jnp.bfloat16), v_ref[...], vb_ref[...]).astype(jnp.bfloat16)


def attention_back_kernel(scale, flag_ref, q_ref, k_ref, v_ref, kb_ref, vb_ref, do_ref, *refs):
    dq_ref, dk_ref, dv_ref, dkb_ref, dvb_ref = refs[-5:]
    has_before = flag_ref[flag_ref.shape[0] - 1] > 0
    query, grad = q_ref[...], do_ref[...]
    probs = window_probs(query, k_ref[...], kb_ref[...], has_before, scale)
    grad_probs = window_parts(grad, v_ref[...], vb_ref[...], None, dot_nt)
    inner = jnp.sum(grad_probs * probs, axis=-1, keepdims=True)
    grad_scores = (probs * (grad_probs - inner)).astype(jnp.bfloat16)
    dq_ref[...] = window_apply(grad_scores, k_ref[...], kb_ref[...]) * scale
    key_now, key_before = window_apply_back(grad_scores, query)
    value_now, value_before = window_apply_back(probs.astype(jnp.bfloat16), grad)

    @pl.when(pl.program_id(0) == 0)
    def _():
        dk_ref[...] = key_now * scale
        dkb_ref[...] = key_before * scale
        dv_ref[...] = value_now
        dvb_ref[...] = value_before

    @pl.when(pl.program_id(0) > 0)
    def _():
        dk_ref[...] += key_now * scale
        dkb_ref[...] += key_before * scale
        dv_ref[...] += value_now
        dvb_ref[...] += value_before


def middle_kernel(
    chunk,
    down_rows,
    x_ref,
    dy_ref,
    att_ref,
    rows_near,
    rows_far,
    mine_near,
    mine_far,
    other_near,
    other_far,
    gain_ref,
    info_ref,
    out_ref,
    dmid_ref,
    datt_ref,
    gain_grad_ref,
    wide_near,
    wide_far,
    tall_near,
    tall_far,
    wo_ref,
    wg_ref,
    wu_ref,
    wd_ref,
    mlp_all,
    hidden_all,
    dmlp_all,
    dgate_all,
    dup_all,
    dattn_all,
    sems,
):
    count = info_ref.shape[0] - 3
    core, span = info_ref[count], info_ref[count + 1]
    half = rows_near.shape[2]
    out_rows = 2 * half - down_rows
    feature_rows = mine_near.shape[1]

    @pl.when(pl.program_id(0) == 0)
    def _():
        copies = [
            pltpu.make_async_copy(source, target, sems.at[index])
            for index, (source, target) in enumerate(
                (
                    (rows_near, tall_near),
                    (rows_far, tall_far),
                    (mine_near, wide_near.at[0]),
                    (other_near, wide_near.at[1]),
                    (mine_far, wide_far.at[0]),
                    (other_far, wide_far.at[1]),
                )
            )
        ]
        for copy in copies:
            copy.start()
        for copy in copies:
            copy.wait()

        def down_block(ref, place):
            return [ref[place, 0], ref[place, 1, : down_rows - half]]

        def out_block(ref, place):
            return [ref[place, 1, down_rows - half :]]

        join_pairs(wd_ref, tall_near, tall_far, core, info_ref, down_rows, down_block)
        join_pairs(wo_ref, tall_near, tall_far, core, info_ref, out_rows, out_block)
        for value in (0, 1):
            first, second = (wg_ref, wu_ref) if value == 0 else (wu_ref, wg_ref)

            @pl.when(span == value)
            def _():
                join_pairs(first, wide_near.at[0], wide_far.at[0], core, info_ref, feature_rows)
                join_pairs(second, wide_near.at[1], wide_far.at[1], core, info_ref, feature_rows)

    step = pl.program_id(0)
    block = x_ref.shape[0]
    rows = pl.ds(pl.multiple_of(step * block, block), block)
    ff = wg_ref.shape[1]
    gain_attn, gain_mlp, gain_final = gain_ref[1:2, :], gain_ref[2:3, :], gain_ref[3:4, :]
    x = x_ref[...].astype(jnp.float32)
    raw = dot(att_ref[rows, :], wo_ref[...])
    raw_scale = inverse_rms(raw)
    middle = x + raw * raw_scale * gain_attn
    middle_scale = inverse_rms(middle)
    mlp_low = (middle * middle_scale * gain_mlp).astype(jnp.bfloat16)
    mlp_all[rows, :] = mlp_low
    kept = []
    mlp_raw = None
    for start in range(0, ff, chunk):
        part = slice(start, start + chunk)
        gate = dot(mlp_low, wg_ref[:, part])
        up = dot(mlp_low, wu_ref[:, part])
        square = gate * gate
        bend = jnp.tanh(ROOT * (gate + 0.044715 * (gate * square)))
        lift = 0.5 * (1.0 + bend)
        gelu = gate * lift
        slope = lift + (0.5 * ROOT) * gate * (1.0 - bend * bend) * (1.0 + (3 * 0.044715) * square)
        hidden = (gelu * up).astype(jnp.bfloat16)
        hidden_all[rows, part] = hidden
        kept.append((up * slope, gelu))
        term = dot(hidden, wd_ref[part, :])
        mlp_raw = term if mlp_raw is None else mlp_raw + term
    mlp_scale = inverse_rms(mlp_raw)
    out_ref[...] = (middle + mlp_raw * mlp_scale * gain_final).astype(jnp.bfloat16)
    dy = dy_ref[...].astype(jnp.float32)
    grad_raw, final_rows = rms_back(mlp_raw, mlp_scale, gain_final, dy)
    dmlp_low = grad_raw.astype(jnp.bfloat16)
    dmlp_all[rows, :] = dmlp_low
    grad_in = None
    for index, start in enumerate(range(0, ff, chunk)):
        part = slice(start, start + chunk)
        grad_hidden = dot_nt(dmlp_low, wd_ref[part, :])
        up_slope, gelu = kept[index]
        dgate = (grad_hidden * up_slope).astype(jnp.bfloat16)
        dup = (grad_hidden * gelu).astype(jnp.bfloat16)
        dgate_all[rows, part] = dgate
        dup_all[rows, part] = dup
        term = dot_nt(dgate, wg_ref[:, part]) + dot_nt(dup, wu_ref[:, part])
        grad_in = term if grad_in is None else grad_in + term
    grad_middle, mlp_rows = rms_back(middle, middle_scale, gain_mlp, grad_in)
    grad_middle = dy + grad_middle
    dmid_ref[...] = grad_middle
    grad_attn, attn_rows = rms_back(raw, raw_scale, gain_attn, grad_middle)
    dattn_low = grad_attn.astype(jnp.bfloat16)
    dattn_all[rows, :] = dattn_low
    datt_ref[...] = dot_nt(dattn_low, wo_ref[...]).astype(jnp.bfloat16)
    sums = [jnp.sum(part, axis=0, keepdims=True) for part in (attn_rows, mlp_rows, final_rows)]
    gain_sums = jnp.concatenate(sums + [jnp.zeros((8 - len(sums), x.shape[1]), jnp.float32)], axis=0)

    @pl.when(step == 0)
    def _():
        gain_grad_ref[...] = gain_sums

    @pl.when(step > 0)
    def _():
        gain_grad_ref[...] += gain_sums

    @pl.when(step == pl.num_programs(0) - 1)
    def _():
        for start in range(0, ff, chunk):
            part = slice(start, start + chunk)
            gate_grad = dot_tn(mlp_all[...], dgate_all[:, part])
            up_grad = dot_tn(mlp_all[...], dup_all[:, part])
            down_grad = dot_tn(hidden_all[:, part], dmlp_all[...]).astype(jnp.bfloat16)

            def store(value):
                for index in range(0, count, 2):
                    place = info_ref[index]
                    for other in (0, 1):
                        to = wide_near if other == value else wide_far
                        lines = slice((index + other) * feature_rows, (index + other + 1) * feature_rows)
                        to[span, place, :, part] = gate_grad[lines].astype(jnp.bfloat16)
                        to[1 - span, place, :, part] = up_grad[lines].astype(jnp.bfloat16)
                for line in range(0, chunk, down_rows):
                    index = (start + line) // down_rows
                    to = tall_near if index % 2 == value else tall_far
                    place = info_ref[index]
                    to[place, span] = down_grad[line : line + half]
                    to[place, 1 - span, : down_rows - half] = down_grad[line + half : line + down_rows]

            each_core(core, store)
        for start in range(0, wo_ref.shape[0], chunk):
            part = slice(start, start + chunk)
            out_grad = dot_tn(att_ref[:, part], dattn_all[...]).astype(jnp.bfloat16)

            def store_out(value):
                for line in range(0, chunk, out_rows):
                    index = (start + line) // out_rows
                    to = tall_near if index % 2 == value else tall_far
                    to[info_ref[index], 1 - span, down_rows - half :] = out_grad[line : line + out_rows]

            each_core(core, store_out)


def head_back_kernel(
    head_dim,
    x_ref,
    xb_ref,
    w_ref,
    gain_ref,
    head_gain_ref,
    pick_ref,
    middle_gain_ref,
    info_ref,
    cos_ref,
    sin_ref,
    cosb_ref,
    sinb_ref,
    dq_ref,
    dk_ref,
    dv_ref,
    dkb_ref,
    dvb_ref,
    dmid_ref,
    token_ref,
    before_ref,
    near_ref,
    far_ref,
    normed_all,
    draw_all,
    normed_before_all,
    draw_before_all,
    gain_sum,
    head_sum,
    grad_all,
):
    step = pl.program_id(0)
    block = x_ref.shape[0]
    rows = pl.ds(pl.multiple_of(step * block, block), block)
    queries = dq_ref.shape[1]
    keys = slice(queries, queries + head_dim)
    pair = slice(queries, queries + 2 * head_dim)
    norm_gain = gain_ref[0:1, :]
    query_gain, key_gain = head_gain_ref[4:5, :], head_gain_ref[5:6, :]
    x = x_ref[...].astype(jnp.float32)
    x_scale = inverse_rms(x)
    normed = (x * x_scale * norm_gain).astype(jnp.bfloat16)
    normed_all[rows, :] = normed
    cosine, sine = cos_ref[...], sin_ref[...]
    query_rows = None
    for start in range(0, queries, head_dim):
        part = slice(start, start + head_dim)
        raw = dot(normed, w_ref[:, part])
        grad = turn_back(dq_ref[:, part], cosine, sine)
        grad_raw, head_rows = rms_back(raw, inverse_rms(raw), query_gain, grad)
        query_rows = head_rows if query_rows is None else query_rows + head_rows
        draw_all[rows, part] = grad_raw.astype(jnp.bfloat16)
    raw = dot(normed, w_ref[:, keys])
    grad_raw, key_rows = rms_back(raw, inverse_rms(raw), key_gain, turn_back(dk_ref[...], cosine, sine))
    draw_all[rows, keys] = grad_raw.astype(jnp.bfloat16)
    draw_all[rows, queries + head_dim : queries + 2 * head_dim] = dv_ref[...].astype(jnp.bfloat16)
    grad_normed = dot_nt(draw_all[rows, :], w_ref[...])
    grad_x, norm_rows = rms_back(x, x_scale, norm_gain, grad_normed)
    token_ref[...] = dmid_ref[...] + grad_x

    xb = xb_ref[...].astype(jnp.float32)
    xb_scale = inverse_rms(xb)
    normed_before = (xb * xb_scale * norm_gain).astype(jnp.bfloat16)
    normed_before_all[rows, :] = normed_before
    raw = dot(normed_before, w_ref[:, keys])
    grad = turn_back(dkb_ref[...], cosb_ref[...], sinb_ref[...])
    grad_raw, key_before_rows = rms_back(raw, inverse_rms(raw), key_gain, grad)
    draw_before = jnp.concatenate([grad_raw, dvb_ref[...]], axis=1).astype(jnp.bfloat16)
    draw_before_all[rows, :] = draw_before
    grad_xb, norm_before_rows = rms_back(xb, xb_scale, norm_gain, dot_nt(draw_before, w_ref[:, pair]))
    before_ref[...] = grad_xb.astype(jnp.bfloat16)

    norm_sums = jnp.sum(norm_rows + norm_before_rows, axis=0, keepdims=True)
    head_sums = jnp.concatenate(
        [
            jnp.zeros((4, head_dim), jnp.float32),
            jnp.sum(query_rows, axis=0, keepdims=True),
            jnp.sum(key_rows + key_before_rows, axis=0, keepdims=True),
            jnp.zeros((2, head_dim), jnp.float32),
        ],
        axis=0,
    )

    @pl.when(step == 0)
    def _():
        gain_sum[...] = jnp.zeros_like(gain_sum)
        gain_sum[0:1, :] = norm_sums
        gain_sum[1:4, :] = middle_gain_ref[0:3, :]
        head_sum[...] = head_sums

    @pl.when(step > 0)
    def _():
        gain_sum[0:1, :] += norm_sums
        head_sum[...] += head_sums

    @pl.when(step == pl.num_programs(0) - 1)
    def _():
        count = info_ref.shape[0] - 3
        core = info_ref[count]
        total = queries + 2 * head_dim
        feature_rows = near_ref.shape[1]
        for start in range(0, queries, 512):
            part = slice(start, start + 512)
            grad_all[:, part] = dot_tn(normed_all[...], draw_all[:, part])
        grad_all[:, pair] = dot_tn(normed_all[...], draw_all[:, pair]) + dot_tn(
            normed_before_all[...], draw_before_all[...]
        )
        heads = dot_nt(head_sum[...].astype(jnp.bfloat16), pick_ref[...])
        sums = jnp.concatenate(
            [gain_sum[...] + heads, jnp.zeros((LANES - gain_sum.shape[0], gain_sum.shape[1]), jnp.float32)],
            axis=0,
        )
        grad_all[:, total : total + LANES] = sums.T
        grad_all[:, total + LANES :] = jnp.zeros((grad_all.shape[0], grad_all.shape[1] - total - LANES), jnp.float32)

        def store(value):
            for index in range(count):
                to = near_ref if index % 2 == value else far_ref
                place = info_ref[index]
                lines = slice(index * feature_rows, (index + 1) * feature_rows)
                to[place] = grad_all[lines, :].astype(jnp.bfloat16)

        each_core(core, store)


def angle_tables(offset, length_rows, head_dim):
    half_dim = head_dim // 2
    frequency = 10000.0 ** (-(jnp.arange(half_dim).astype(jnp.float32) * 2.0 / head_dim))
    positions = (offset + jnp.arange(length_rows)).astype(jnp.float32)
    angles = positions[:, None] * frequency[None, :]
    return (jnp.cos(angles), jnp.sin(angles))


def per_device(
    tokens,
    cotangent,
    norm_gain,
    query_weight,
    key_weight,
    value_weight,
    query_norm,
    key_norm,
    output_weight,
    attn_post_gain,
    mlp_pre_gain,
    gate_weight,
    up_weight,
    down_weight,
    mlp_post_gain,
):
    fsdp = lax.axis_size("fsdp")
    rows = norm_gain.shape[0]
    head_rows = query_norm.shape[0]
    gain_columns = jnp.stack(
        [
            norm_gain,
            attn_post_gain,
            mlp_pre_gain,
            mlp_post_gain,
            jnp.pad(query_norm, (0, rows - head_rows)),
            jnp.pad(key_norm, (0, rows - head_rows)),
        ],
        axis=1,
    )
    query_columns = query_weight.shape[1]
    head_dim = key_weight.shape[1]
    ff = gate_weight.shape[1]
    qkv_columns = query_columns + 2 * head_dim
    first_columns = -(-(qkv_columns + LANES) // (2 * LANES)) * 2 * LANES
    gain_columns = jnp.pad(
        gain_columns, ((0, 0), (0, first_columns - qkv_columns - gain_columns.shape[1]))
    )
    first_shard = jnp.concatenate([query_weight, key_weight, value_weight, gain_columns], axis=1)
    tall_shard = jnp.concatenate([down_weight, output_weight], axis=0)
    core = lax.axis_index("fsdp") & 1
    span = lax.axis_index("ctx") & 1
    low_span = span == 0
    info = jnp.concatenate(
        [
            places("fsdp"),
            jnp.stack([core, span, (lax.axis_index("ctx") > 0).astype(jnp.int32)]),
        ]
    )
    sequences, span_len, model_width = tokens.shape
    head_count = query_columns // head_dim
    assert span_len == WINDOW
    offset = lax.axis_index("ctx") * span_len
    score_scale = head_dim ** (-0.5)
    tables = angle_tables(offset, span_len, head_dim)
    tables_before = angle_tables(offset - span_len, span_len, head_dim)
    row = jnp.arange(fsdp * rows)
    pick = (
        (row[:, None] // rows == jnp.arange(head_dim)[None, :] // head_rows)
        & (row[:, None] % rows == jnp.arange(head_dim)[None, :] % head_rows)
    ).astype(jnp.bfloat16)
    chip_masks = [1 << bit for bit in range(fsdp.bit_length() - 2, 0, -1)]
    before = shifted(tokens, "ctx", 1)
    first_shard, info, pick, tables, tables_before = lax.optimization_barrier(
        (first_shard, info, pick, tables, tables_before)
    )
    mine_near = jnp.where(low_span, gate_weight, up_weight)[None]
    first_near, tall_near = first_shard[None], tall_shard[None]
    for step, mask in enumerate(chip_masks):
        if step == len(chip_masks) - 1:
            mine_near = after(mine_near, tall_first, before)
        mine_near = widen(mine_near, "fsdp", mask)
        first_near = widen(first_near, "fsdp", mask, mine_near)
        if step == 0:
            tall_near = after(tall_near, mine_near)
        if step < len(chip_masks) - 1:
            tall_near = widen(tall_near, "fsdp", mask)
        if step == 0:
            tall_first = tall_near
    first_near = after(first_near, tall_near)
    first_far = swap(first_near, "fsdp", 1)
    mine_far = swap(mine_near, "fsdp", 1)
    other_near = swap(mine_near, "ctx", 1)
    tall_late = swap(tall_near, "fsdp", chip_masks[-1])
    total = sequences * span_len
    steps = total // ROWS
    span_steps = span_len // ROWS
    x = tokens.reshape(total, model_width)
    x_before = before.reshape(total, model_width)
    upstream = cotangent.reshape(total, model_width)
    params = pltpu.CompilerParams(vmem_limit_bytes=VMEM_BYTES)
    whole = pl.BlockSpec(memory_space=pltpu.VMEM)
    scalars = pl.BlockSpec(memory_space=pltpu.SMEM)

    def by_rows(columns):
        return pl.BlockSpec((ROWS, columns), lambda i: (i, 0))

    table = pl.BlockSpec((ROWS, head_dim // 2), lambda i: (i % span_steps, 0))

    def bf16(*shape):
        return jax.ShapeDtypeStruct(shape, jnp.bfloat16)

    def f32(*shape):
        return jax.ShapeDtypeStruct(shape, jnp.float32)

    def scratch(*shape):
        return pltpu.VMEM(shape, jnp.bfloat16)

    one_head = by_rows(head_dim)
    model = by_rows(model_width)
    (
        query_low,
        key_low,
        value_low,
        key_prev,
        value_prev,
        first_full,
        gain_rows,
        head_gain_rows,
    ) = pl.pallas_call(
        functools.partial(projection_kernel, head_dim, qkv_columns),
        grid=(steps,),
        in_specs=[model, model, whole, whole, whole, scalars] + [table] * 4,
        out_specs=[by_rows(query_columns)] + [one_head] * 4 + [whole] * 3,
        out_shape=[bf16(total, query_columns)]
        + [bf16(total, head_dim)] * 4
        + [bf16(model_width, qkv_columns), f32(8, model_width), f32(8, head_dim)],
        scratch_shapes=[scratch(model_width, first_columns)],
        compiler_params=params,
        cost_estimate=cost(2 * total * model_width * (qkv_columns + 2 * head_dim), 0.25),
        name="projection",
    )(x, x_before, first_near, first_far, pick, info, *tables, *tables_before)
    other_near = after(other_near, query_low)
    other_far = swap(other_near, "fsdp", 1)
    tall_near = jnp.concatenate([tall_near, after(tall_late, query_low)], axis=0)
    tall_far = swap(tall_near, "fsdp", 1)
    head = pl.BlockSpec((span_len, head_dim), lambda s, h: (s, h))
    shared = pl.BlockSpec((span_len, head_dim), lambda s, h: (s, 0))
    attended_low = pl.pallas_call(
        functools.partial(attention_kernel, score_scale),
        grid=(sequences, head_count),
        in_specs=[scalars, head, shared, shared, shared, shared],
        out_specs=head,
        out_shape=bf16(total, query_columns),
        compiler_params=params,
        cost_estimate=cost(3 * total * span_len * query_columns, 0.14),
        name="attention",
    )(info, query_low, key_low, value_low, key_prev, value_prev)
    down_rows, out_rows = down_weight.shape[0], output_weight.shape[0]
    half_rows = (down_rows + out_rows) // 2
    chips = fsdp // 2
    (
        block_output,
        grad_middle,
        grad_attended,
        middle_gains,
        wide_grad_near,
        wide_grad_far,
        tall_grad_near,
        tall_grad_far,
    ) = pl.pallas_call(
        functools.partial(middle_kernel, 512, down_rows),
        grid=(steps,),
        in_specs=[model, model, whole] + [pl.BlockSpec(memory_space=pl.ANY)] * 6 + [whole, scalars],
        out_specs=[model, model, by_rows(query_columns)] + [whole] * 5,
        out_shape=[
            bf16(total, model_width),
            f32(total, model_width),
            bf16(total, query_columns),
            f32(8, model_width),
            bf16(2, chips, rows, ff),
            bf16(2, chips, rows, ff),
            bf16(chips, 2, half_rows, model_width),
            bf16(chips, 2, half_rows, model_width),
        ],
        scratch_shapes=[
            scratch(query_columns, model_width),
            scratch(model_width, ff),
            scratch(model_width, ff),
            scratch(ff, model_width),
            scratch(total, model_width),
            scratch(total, ff),
            scratch(total, model_width),
            scratch(total, ff),
            scratch(total, ff),
            scratch(total, model_width),
            pltpu.SemaphoreType.DMA((6,)),
        ],
        compiler_params=params,
        cost_estimate=cost(6 * total * model_width * (3 * ff + query_columns), 0.4),
        name="middle",
    )(
        x,
        upstream,
        attended_low,
        tall_near.reshape(chips, 2, half_rows, model_width),
        tall_far.reshape(chips, 2, half_rows, model_width),
        mine_near,
        mine_far,
        other_near,
        other_far,
        gain_rows,
        info,
    )
    far_mask, near_masks = chip_masks[0], chip_masks[:0:-1]
    wide_far_sum = swap(wide_grad_far, "fsdp", 1)
    tall_far_sum = swap(tall_grad_far, "fsdp", 1)

    def attention_back(sequence, grad, done):
        one = pl.BlockSpec((span_len, head_dim), lambda h: (sequence, h))
        for_all = pl.BlockSpec((span_len, head_dim), lambda h: (sequence, 0))
        return pl.pallas_call(
            functools.partial(attention_back_kernel, score_scale),
            grid=(head_count,),
            in_specs=[scalars, one] + [for_all] * 4 + [one] + [pl.BlockSpec(memory_space=pl.ANY)] * len(done),
            out_specs=[one] + [for_all] * 4,
            out_shape=[f32(total, query_columns)] + [f32(total, head_dim)] * 4,
            input_output_aliases={7 + index: index for index in range(len(done))},
            compiler_params=params,
            cost_estimate=cost(7.5 * span_len * span_len * query_columns, 0.2),
            name="attention_back",
        )(info, query_low, key_low, value_low, key_prev, value_prev, grad, *done)

    back = attention_back(0, grad_attended, ())
    wide_far_sum, tall_far_sum = after((wide_far_sum, tall_far_sum), back[0])
    wide = add(wide_grad_near, wide_far_sum)
    tall = add(tall_grad_near, tall_far_sum)
    bits = (2,) * len(chip_masks)
    wide = wide.reshape((2,) + bits + wide.shape[2:])
    tall = tall.reshape(bits + tall.shape[1:])
    wide_kept, wide_come = folded(wide, "fsdp", near_masks[0], 1)
    tall_kept, tall_come = folded(tall, "fsdp", near_masks[1], 1)
    wide, tall, grad_attended = lax.optimization_barrier((wide, tall, grad_attended))
    for sequence in range(1, sequences):
        back = attention_back(sequence, grad_attended, back)
    grad_query, grad_key, grad_value, key_send, value_send = back
    token_part, before_part, first_grad_near, first_grad_far = pl.pallas_call(
        functools.partial(head_back_kernel, head_dim),
        grid=(steps,),
        in_specs=[model, model]
        + [whole] * 5
        + [scalars]
        + [table] * 4
        + [by_rows(query_columns)]
        + [one_head] * 4
        + [model],
        out_specs=[model, model, whole, whole],
        out_shape=[
            f32(total, model_width),
            bf16(total, model_width),
            bf16(chips, rows, first_columns),
            bf16(chips, rows, first_columns),
        ],
        scratch_shapes=[
            scratch(total, model_width),
            scratch(total, qkv_columns),
            scratch(total, model_width),
            scratch(total, 2 * head_dim),
            pltpu.VMEM((8, model_width), jnp.float32),
            pltpu.VMEM((8, head_dim), jnp.float32),
            pltpu.VMEM((model_width, first_columns), jnp.float32),
        ],
        compiler_params=params,
        cost_estimate=cost(6 * total * model_width * (qkv_columns + 2 * head_dim), 0.38),
        name="head_back",
    )(
        x,
        x_before,
        first_full,
        gain_rows,
        head_gain_rows,
        pick,
        middle_gains,
        info,
        *tables,
        *tables_before,
        grad_query,
        grad_key,
        grad_value,
        key_send,
        value_send,
        grad_middle,
    )
    tall = add(tall_kept, after(tall_come, token_part))
    wide = add(wide_kept, after(wide_come, token_part))
    first_grad_far, before_part = after((first_grad_far, before_part), tall, wide)
    tall_kept, tall_come = folded(tall, "fsdp", near_masks[0], 0)
    wide_kept, wide_come = folded(wide, "fsdp", near_masks[1], 2)
    before_come = shifted(before_part, "ctx", -1)
    first = add(first_grad_near, swap(first_grad_far, "fsdp", 1))
    first = first.reshape(bits + first.shape[1:])
    first_kept, first_come = folded(first, "fsdp", near_masks[0], 0)
    first = add(first_kept, first_come)
    first_kept, first_come = folded(first, "fsdp", near_masks[1], 1)
    tall = add(tall_kept, after(tall_come, first))
    tall_kept, tall_come = folded(tall, "ctx", 1, len(bits))
    wide = add(wide_kept, after(wide_come, tall))
    wide_kept, wide_come = folded(wide, "ctx", 1, 0)
    for index in range(2, len(bits)):
        mask = (near_masks + [far_mask])[index]
        first = add(first_kept, after(first_come, wide))
        first_kept, first_come = folded(first, "fsdp", mask, index)
        if index == 2:
            tall = add(tall_kept, after(tall_come, first))
        tall_kept, tall_come = folded(tall, "fsdp", mask, index)
        if index == 2:
            wide = add(wide_kept, after(wide_come, tall))
        wide_kept, wide_come = folded(wide, "fsdp", mask, index + 1)
        tall = add(tall_kept, after(tall_come, first))
        wide = add(wide_kept, after(wide_come, tall))
    first = add(first_kept, after(first_come, tall))
    tall = other_spans(tall.reshape(tall.shape[-2:]), "ctx")
    wide = other_spans(wide.reshape(wide.shape[-2:]), "ctx")
    first = other_spans(first.reshape(first.shape[-2:]), "ctx")
    first_come = swap(first, "ctx", 1)
    before_come = after(before_come, first)
    token_grad = (token_part + before_come.astype(jnp.float32)).astype(jnp.bfloat16)

    def both(mine):
        other = swap(mine, "ctx", 1)
        left = jnp.where(low_span, mine, other).astype(jnp.float32)
        right = jnp.where(low_span, other, mine).astype(jnp.float32)
        return left, right

    grad_gate, grad_up = both(wide)
    grad_tall = jnp.concatenate(both(tall), axis=0)
    grad_first = first.astype(jnp.float32) + first_come.astype(jnp.float32)
    return (
        block_output.reshape(tokens.shape),
        token_grad.reshape(tokens.shape),
        grad_first[:, qkv_columns],
        grad_first[:, :query_columns],
        grad_first[:, query_columns : query_columns + head_dim],
        grad_first[:, query_columns + head_dim : qkv_columns],
        grad_first[:head_rows, qkv_columns + 4],
        grad_first[:head_rows, qkv_columns + 5],
        grad_tall[down_rows:],
        grad_first[:, qkv_columns + 1],
        grad_first[:, qkv_columns + 2],
        grad_gate,
        grad_up,
        grad_tall[:down_rows],
        grad_first[:, qkv_columns + 3],
    )


def solution(mesh):
    return jax.shard_map(
        per_device,
        mesh=mesh,
        in_specs=(
            P("fsdp", "ctx", None),
            P("fsdp", "ctx", None),
            P("fsdp"),
            P("fsdp", None),
            P("fsdp", None),
            P("fsdp", None),
            P("fsdp"),
            P("fsdp"),
            P("fsdp", None),
            P("fsdp"),
            P("fsdp"),
            P("fsdp", None),
            P("fsdp", None),
            P("fsdp", None),
            P("fsdp"),
        ),
        out_specs=(
            P("fsdp", "ctx", None),
            P("fsdp", "ctx", None),
            P("fsdp"),
            P("fsdp", None),
            P("fsdp", None),
            P("fsdp", None),
            P("fsdp"),
            P("fsdp"),
            P("fsdp", None),
            P("fsdp"),
            P("fsdp"),
            P("fsdp", None),
            P("fsdp", None),
            P("fsdp", None),
            P("fsdp"),
        ),
        check_vma=False,
    )
```

```python
import functools

import jax
import jax.numpy as jnp
from jax import lax
from jax.experimental import pallas as pl
from jax.experimental.pallas import tpu as pltpu
from jax.sharding import PartitionSpec as P

WINDOW = 512


EPSILON = 1e-06
MASKED = -1e30
ROOT = (2.0 / jnp.pi) ** 0.5
ROWS = 256
VMEM_BYTES = 60 * 1024 * 1024


LANES = 128


def swap(value, axis, mask):
    count = lax.axis_size(axis)
    return lax.ppermute(value, axis, [(source, source ^ mask) for source in range(count)])


def after(value, *others):
    return lax.optimization_barrier((value, others))[0]


def widen(held, axis, mask, *others):
    return jnp.concatenate([held, after(swap(held, axis, mask), *others)], axis=0)


def places(axis):
    count = lax.axis_size(axis)
    relative = jnp.arange(count, dtype=jnp.int32) ^ lax.axis_index(axis)
    place = jnp.zeros((count,), jnp.int32)
    low, high = 0, count // 2
    while high > 1:
        place = place + jnp.where((relative & high) != 0, 1 << low, 0)
        low, high = low + 1, high // 2
    return place


def cost(flops, spent):
    return pl.CostEstimate(flops=int(flops / spent / 4096), bytes_accessed=0, transcendentals=0)


def add(left, right):
    return (left.astype(jnp.float32) + right.astype(jnp.float32)).astype(jnp.bfloat16)


def folded(value, axis, mask, dim):
    kept, sent = jnp.split(value, 2, axis=dim)
    return kept, swap(sent, axis, mask)


def other_spans(value, axis):
    mask = 2
    while mask < lax.axis_size(axis):
        value = add(value, swap(value, axis, mask))
        mask *= 2
    return value


def shifted(value, axis, steps):
    count = lax.axis_size(axis)
    leading, last = (max(0, -steps), min(count, count - steps))
    return lax.ppermute(value, axis, [(source, source + steps) for source in range(leading, last)])


def dot(left, right):
    return jnp.dot(left, right, preferred_element_type=jnp.float32)


def dot_nt(left, right):
    return lax.dot_general(left, right, (((1,), (1,)), ((), ())), preferred_element_type=jnp.float32)


def dot_tn(left, right):
    return lax.dot_general(left, right, (((0,), (0,)), ((), ())), preferred_element_type=jnp.float32)


def inverse_rms(rows):
    return lax.rsqrt(jnp.mean(rows * rows, axis=-1, keepdims=True) + EPSILON)


def rms_back(rows, scale, gain, grad):
    weighted = gain * grad
    inner = jnp.mean(rows * weighted, axis=-1, keepdims=True)
    return scale * weighted - rows * (scale * scale * scale * inner), grad * rows * scale


def turn(rows, cosine, sine):
    half = rows.shape[-1] // 2
    front, back = rows[:, :half], rows[:, half:]
    return jnp.concatenate([front * cosine - back * sine, back * cosine + front * sine], axis=-1)


def turn_back(rows, cosine, sine):
    return turn(rows, cosine, -sine)


def each_core(core, body):
    for value in (0, 1):
        pl.when(core == value)(functools.partial(body, value))


def whole_block(ref, place):
    return [ref[place]]


def join_pairs(out_ref, near_ref, far_ref, core, info_ref, rows, read=whole_block):
    pairs = 1
    while (2 * rows * pairs) % 16:
        pairs *= 2
    size = 2 * rows * pairs

    def body(value):
        first, second = (near_ref, far_ref) if value == 0 else (far_ref, near_ref)

        def group(index, carry):
            blocks = []
            for pair in range(pairs):
                place = info_ref[2 * (index * pairs + pair)]
                blocks += read(first, place) + read(second, place)
            if rows % 8:
                blocks = [block.astype(jnp.float32) for block in blocks]
            lines = pl.ds(pl.multiple_of(index * size, size), size)
            out_ref[lines, :] = jnp.concatenate(blocks, axis=0).astype(jnp.bfloat16)
            return carry

        lax.fori_loop(0, near_ref.shape[0] // pairs, group, 0)

    each_core(core, body)


def projection_kernel(
    head_dim,
    columns,
    x_ref,
    xb_ref,
    near_ref,
    far_ref,
    pick_ref,
    info_ref,
    cos_ref,
    sin_ref,
    cosb_ref,
    sinb_ref,
    q_ref,
    k_ref,
    v_ref,
    kb_ref,
    vb_ref,
    w_ref,
    gain_ref,
    head_gain_ref,
    all_ref,
):
    count = info_ref.shape[0] - 3

    @pl.when(pl.program_id(0) == 0)
    def _():
        join_pairs(all_ref, near_ref, far_ref, info_ref[count], info_ref, near_ref.shape[1])
        w_ref[...] = all_ref[:, :columns]
        gains = all_ref[:, columns : columns + LANES].astype(jnp.float32).T[:8]
        gain_ref[...] = gains
        head_gain_ref[...] = dot(gains.astype(jnp.bfloat16), pick_ref[...])

    gain = gain_ref[0:1, :]
    queries = q_ref.shape[1]
    x = x_ref[...].astype(jnp.float32)
    normed = (x * inverse_rms(x) * gain).astype(jnp.bfloat16)
    x = xb_ref[...].astype(jnp.float32)
    normed_before = (x * inverse_rms(x) * gain).astype(jnp.bfloat16)
    key_part = slice(queries, queries + head_dim)
    value_part = slice(queries + head_dim, queries + 2 * head_dim)

    def turned(rows, part, head_gain, cosine, sine):
        raw = dot(rows, w_ref[:, part])
        return turn(raw * inverse_rms(raw) * head_gain, cosine, sine).astype(jnp.bfloat16)

    for start in range(0, queries, head_dim):
        part = slice(start, start + head_dim)
        q_ref[:, part] = turned(normed, part, head_gain_ref[4:5, :], cos_ref[...], sin_ref[...])
    k_ref[...] = turned(normed, key_part, head_gain_ref[5:6, :], cos_ref[...], sin_ref[...])
    v_ref[...] = dot(normed, w_ref[:, value_part]).astype(jnp.bfloat16)
    kb_ref[...] = turned(normed_before, key_part, head_gain_ref[5:6, :], cosb_ref[...], sinb_ref[...])
    vb_ref[...] = dot(normed_before, w_ref[:, value_part]).astype(jnp.bfloat16)


def window_parts(rows, now, before, has_before, product):
    half = rows.shape[0] // 2
    low = lax.broadcasted_iota(jnp.int32, (half, half), 1) <= lax.broadcasted_iota(
        jnp.int32, (half, half), 0
    )
    top, bottom = rows[:half], rows[half:]
    before_left = product(top, before[:half])
    before_right = product(top, before[half:])
    before_low = product(bottom, before[half:])
    if has_before is not None:
        before_left = jnp.where(has_before, before_left, MASKED)
        before_right = jnp.where(has_before, before_right, MASKED)
        before_low = jnp.where(has_before, before_low, MASKED)
    upper = jnp.concatenate([jnp.where(low, product(top, now[:half]), before_left), before_right], axis=1)
    lower = jnp.concatenate(
        [product(bottom, now[:half]), jnp.where(low, product(bottom, now[half:]), before_low)], axis=1
    )
    return jnp.concatenate([upper, lower], axis=0)


def window_split(matrix):
    half = matrix.shape[0] // 2
    low = lax.broadcasted_iota(jnp.int32, (half, half), 1) <= lax.broadcasted_iota(
        jnp.int32, (half, half), 0
    )
    first, last = matrix[:half, :half], matrix[half:, half:]
    zero = jnp.zeros_like(first)
    return (
        jnp.where(low, first, zero),
        jnp.where(low, zero, first),
        jnp.where(low, last, zero),
        jnp.where(low, zero, last),
        matrix[:half, half:],
        matrix[half:, :half],
    )


def window_apply(matrix, now, before):
    half = matrix.shape[0] // 2
    first_now, first_before, last_now, last_before, right, left = window_split(matrix)
    top = dot(first_now, now[:half]) + dot(first_before, before[:half]) + dot(right, before[half:])
    bottom = dot(left, now[:half]) + dot(last_now, now[half:]) + dot(last_before, before[half:])
    return jnp.concatenate([top, bottom], axis=0)


def window_apply_back(matrix, rows):
    half = matrix.shape[0] // 2
    first_now, first_before, last_now, last_before, right, left = window_split(matrix)
    top, bottom = rows[:half], rows[half:]
    now = jnp.concatenate([dot_tn(first_now, top) + dot_tn(left, bottom), dot_tn(last_now, bottom)], axis=0)
    before = jnp.concatenate(
        [dot_tn(first_before, top), dot_tn(right, top) + dot_tn(last_before, bottom)], axis=0
    )
    return now, before


def window_probs(query, key, key_before, has_before, scale):
    scores = window_parts(query, key, key_before, has_before, dot_nt) * scale
    terms = jnp.exp(scores - jnp.max(scores, axis=-1, keepdims=True))
    return terms * (1.0 / jnp.sum(terms, axis=-1, keepdims=True))


def attention_kernel(scale, flag_ref, q_ref, k_ref, v_ref, kb_ref, vb_ref, o_ref):
    has_before = flag_ref[flag_ref.shape[0] - 1] > 0
    probs = window_probs(q_ref[...], k_ref[...], kb_ref[...], has_before, scale)
    o_ref[...] = window_apply(probs.astype(jnp.bfloat16), v_ref[...], vb_ref[...]).astype(jnp.bfloat16)


def attention_back_kernel(scale, flag_ref, q_ref, k_ref, v_ref, kb_ref, vb_ref, do_ref, *refs):
    dq_ref, dk_ref, dv_ref, dkb_ref, dvb_ref = refs[-5:]
    has_before = flag_ref[flag_ref.shape[0] - 1] > 0
    query, grad = q_ref[...], do_ref[...]
    probs = window_probs(query, k_ref[...], kb_ref[...], has_before, scale)
    grad_probs = window_parts(grad, v_ref[...], vb_ref[...], None, dot_nt)
    inner = jnp.sum(grad_probs * probs, axis=-1, keepdims=True)
    grad_scores = (probs * (grad_probs - inner)).astype(jnp.bfloat16)
    dq_ref[...] = window_apply(grad_scores, k_ref[...], kb_ref[...]) * scale
    key_now, key_before = window_apply_back(grad_scores, query)
    value_now, value_before = window_apply_back(probs.astype(jnp.bfloat16), grad)

    @pl.when(pl.program_id(0) == 0)
    def _():
        dk_ref[...] = key_now * scale
        dkb_ref[...] = key_before * scale
        dv_ref[...] = value_now
        dvb_ref[...] = value_before

    @pl.when(pl.program_id(0) > 0)
    def _():
        dk_ref[...] += key_now * scale
        dkb_ref[...] += key_before * scale
        dv_ref[...] += value_now
        dvb_ref[...] += value_before


def middle_kernel(
    chunk,
    down_rows,
    x_ref,
    dy_ref,
    att_ref,
    rows_near,
    rows_far,
    mine_near,
    mine_far,
    other_near,
    other_far,
    gain_ref,
    info_ref,
    out_ref,
    dmid_ref,
    datt_ref,
    gain_grad_ref,
    wide_near,
    wide_far,
    tall_near,
    tall_far,
    wo_ref,
    wg_ref,
    wu_ref,
    wd_ref,
    mlp_all,
    hidden_all,
    dmlp_all,
    dgate_all,
    dup_all,
    dattn_all,
    sems,
):
    count = info_ref.shape[0] - 3
    core, span = info_ref[count], info_ref[count + 1]
    half = rows_near.shape[2]
    out_rows = 2 * half - down_rows
    feature_rows = mine_near.shape[1]

    @pl.when(pl.program_id(0) == 0)
    def _():
        copies = [
            pltpu.make_async_copy(source, target, sems.at[index])
            for index, (source, target) in enumerate(
                (
                    (rows_near, tall_near),
                    (rows_far, tall_far),
                    (mine_near, wide_near.at[0]),
                    (other_near, wide_near.at[1]),
                    (mine_far, wide_far.at[0]),
                    (other_far, wide_far.at[1]),
                )
            )
        ]
        for copy in copies:
            copy.start()
        for copy in copies:
            copy.wait()

        def down_block(ref, place):
            return [ref[place, 0], ref[place, 1, : down_rows - half]]

        def out_block(ref, place):
            return [ref[place, 1, down_rows - half :]]

        join_pairs(wd_ref, tall_near, tall_far, core, info_ref, down_rows, down_block)
        join_pairs(wo_ref, tall_near, tall_far, core, info_ref, out_rows, out_block)
        for value in (0, 1):
            first, second = (wg_ref, wu_ref) if value == 0 else (wu_ref, wg_ref)

            @pl.when(span == value)
            def _():
                join_pairs(first, wide_near.at[0], wide_far.at[0], core, info_ref, feature_rows)
                join_pairs(second, wide_near.at[1], wide_far.at[1], core, info_ref, feature_rows)

    step = pl.program_id(0)
    block = x_ref.shape[0]
    rows = pl.ds(pl.multiple_of(step * block, block), block)
    ff = wg_ref.shape[1]
    gain_attn, gain_mlp, gain_final = gain_ref[1:2, :], gain_ref[2:3, :], gain_ref[3:4, :]
    x = x_ref[...].astype(jnp.float32)
    raw = dot(att_ref[rows, :], wo_ref[...])
    raw_scale = inverse_rms(raw)
    middle = x + raw * raw_scale * gain_attn
    middle_scale = inverse_rms(middle)
    mlp_low = (middle * middle_scale * gain_mlp).astype(jnp.bfloat16)
    mlp_all[rows, :] = mlp_low
    kept = []
    mlp_raw = None
    for start in range(0, ff, chunk):
        part = slice(start, start + chunk)
        gate = dot(mlp_low, wg_ref[:, part])
        up = dot(mlp_low, wu_ref[:, part])
        square = gate * gate
        bend = jnp.tanh(ROOT * (gate + 0.044715 * (gate * square)))
        lift = 0.5 * (1.0 + bend)
        gelu = gate * lift
        slope = lift + (0.5 * ROOT) * gate * (1.0 - bend * bend) * (1.0 + (3 * 0.044715) * square)
        hidden = (gelu * up).astype(jnp.bfloat16)
        hidden_all[rows, part] = hidden
        kept.append((up * slope, gelu))
        term = dot(hidden, wd_ref[part, :])
        mlp_raw = term if mlp_raw is None else mlp_raw + term
    mlp_scale = inverse_rms(mlp_raw)
    out_ref[...] = (middle + mlp_raw * mlp_scale * gain_final).astype(jnp.bfloat16)
    dy = dy_ref[...].astype(jnp.float32)
    grad_raw, final_rows = rms_back(mlp_raw, mlp_scale, gain_final, dy)
    dmlp_low = grad_raw.astype(jnp.bfloat16)
    dmlp_all[rows, :] = dmlp_low
    grad_in = None
    for index, start in enumerate(range(0, ff, chunk)):
        part = slice(start, start + chunk)
        grad_hidden = dot_nt(dmlp_low, wd_ref[part, :])
        up_slope, gelu = kept[index]
        dgate = (grad_hidden * up_slope).astype(jnp.bfloat16)
        dup = (grad_hidden * gelu).astype(jnp.bfloat16)
        dgate_all[rows, part] = dgate
        dup_all[rows, part] = dup
        term = dot_nt(dgate, wg_ref[:, part]) + dot_nt(dup, wu_ref[:, part])
        grad_in = term if grad_in is None else grad_in + term
    grad_middle, mlp_rows = rms_back(middle, middle_scale, gain_mlp, grad_in)
    grad_middle = dy + grad_middle
    dmid_ref[...] = grad_middle
    grad_attn, attn_rows = rms_back(raw, raw_scale, gain_attn, grad_middle)
    dattn_low = grad_attn.astype(jnp.bfloat16)
    dattn_all[rows, :] = dattn_low
    datt_ref[...] = dot_nt(dattn_low, wo_ref[...]).astype(jnp.bfloat16)
    sums = [jnp.sum(part, axis=0, keepdims=True) for part in (attn_rows, mlp_rows, final_rows)]
    gain_sums = jnp.concatenate(sums + [jnp.zeros((8 - len(sums), x.shape[1]), jnp.float32)], axis=0)

    @pl.when(step == 0)
    def _():
        gain_grad_ref[...] = gain_sums

    @pl.when(step > 0)
    def _():
        gain_grad_ref[...] += gain_sums

    @pl.when(step == pl.num_programs(0) - 1)
    def _():
        for start in range(0, ff, chunk):
            part = slice(start, start + chunk)
            gate_grad = dot_tn(mlp_all[...], dgate_all[:, part])
            up_grad = dot_tn(mlp_all[...], dup_all[:, part])
            down_grad = dot_tn(hidden_all[:, part], dmlp_all[...]).astype(jnp.bfloat16)

            def store(value):
                for index in range(0, count, 2):
                    place = info_ref[index]
                    for other in (0, 1):
                        to = wide_near if other == value else wide_far
                        lines = slice((index + other) * feature_rows, (index + other + 1) * feature_rows)
                        to[span, place, :, part] = gate_grad[lines].astype(jnp.bfloat16)
                        to[1 - span, place, :, part] = up_grad[lines].astype(jnp.bfloat16)
                for line in range(0, chunk, down_rows):
                    index = (start + line) // down_rows
                    to = tall_near if index % 2 == value else tall_far
                    place = info_ref[index]
                    to[place, span] = down_grad[line : line + half]
                    to[place, 1 - span, : down_rows - half] = down_grad[line + half : line + down_rows]

            each_core(core, store)
        for start in range(0, wo_ref.shape[0], chunk):
            part = slice(start, start + chunk)
            out_grad = dot_tn(att_ref[:, part], dattn_all[...]).astype(jnp.bfloat16)

            def store_out(value):
                for line in range(0, chunk, out_rows):
                    index = (start + line) // out_rows
                    to = tall_near if index % 2 == value else tall_far
                    to[info_ref[index], 1 - span, down_rows - half :] = out_grad[line : line + out_rows]

            each_core(core, store_out)


def head_back_kernel(
    head_dim,
    x_ref,
    xb_ref,
    w_ref,
    gain_ref,
    head_gain_ref,
    pick_ref,
    middle_gain_ref,
    info_ref,
    cos_ref,
    sin_ref,
    cosb_ref,
    sinb_ref,
    dq_ref,
    dk_ref,
    dv_ref,
    dkb_ref,
    dvb_ref,
    dmid_ref,
    token_ref,
    before_ref,
    near_ref,
    far_ref,
    normed_all,
    draw_all,
    normed_before_all,
    draw_before_all,
    gain_sum,
    head_sum,
    grad_all,
):
    step = pl.program_id(0)
    block = x_ref.shape[0]
    rows = pl.ds(pl.multiple_of(step * block, block), block)
    queries = dq_ref.shape[1]
    keys = slice(queries, queries + head_dim)
    pair = slice(queries, queries + 2 * head_dim)
    norm_gain = gain_ref[0:1, :]
    query_gain, key_gain = head_gain_ref[4:5, :], head_gain_ref[5:6, :]
    x = x_ref[...].astype(jnp.float32)
    x_scale = inverse_rms(x)
    normed = (x * x_scale * norm_gain).astype(jnp.bfloat16)
    normed_all[rows, :] = normed
    cosine, sine = cos_ref[...], sin_ref[...]
    query_rows = None
    for start in range(0, queries, head_dim):
        part = slice(start, start + head_dim)
        raw = dot(normed, w_ref[:, part])
        grad = turn_back(dq_ref[:, part], cosine, sine)
        grad_raw, head_rows = rms_back(raw, inverse_rms(raw), query_gain, grad)
        query_rows = head_rows if query_rows is None else query_rows + head_rows
        draw_all[rows, part] = grad_raw.astype(jnp.bfloat16)
    raw = dot(normed, w_ref[:, keys])
    grad_raw, key_rows = rms_back(raw, inverse_rms(raw), key_gain, turn_back(dk_ref[...], cosine, sine))
    draw_all[rows, keys] = grad_raw.astype(jnp.bfloat16)
    draw_all[rows, queries + head_dim : queries + 2 * head_dim] = dv_ref[...].astype(jnp.bfloat16)
    grad_normed = dot_nt(draw_all[rows, :], w_ref[...])
    grad_x, norm_rows = rms_back(x, x_scale, norm_gain, grad_normed)
    token_ref[...] = dmid_ref[...] + grad_x

    xb = xb_ref[...].astype(jnp.float32)
    xb_scale = inverse_rms(xb)
    normed_before = (xb * xb_scale * norm_gain).astype(jnp.bfloat16)
    normed_before_all[rows, :] = normed_before
    raw = dot(normed_before, w_ref[:, keys])
    grad = turn_back(dkb_ref[...], cosb_ref[...], sinb_ref[...])
    grad_raw, key_before_rows = rms_back(raw, inverse_rms(raw), key_gain, grad)
    draw_before = jnp.concatenate([grad_raw, dvb_ref[...]], axis=1).astype(jnp.bfloat16)
    draw_before_all[rows, :] = draw_before
    grad_xb, norm_before_rows = rms_back(xb, xb_scale, norm_gain, dot_nt(draw_before, w_ref[:, pair]))
    before_ref[...] = grad_xb.astype(jnp.bfloat16)

    norm_sums = jnp.sum(norm_rows + norm_before_rows, axis=0, keepdims=True)
    head_sums = jnp.concatenate(
        [
            jnp.zeros((4, head_dim), jnp.float32),
            jnp.sum(query_rows, axis=0, keepdims=True),
            jnp.sum(key_rows + key_before_rows, axis=0, keepdims=True),
            jnp.zeros((2, head_dim), jnp.float32),
        ],
        axis=0,
    )

    @pl.when(step == 0)
    def _():
        gain_sum[...] = jnp.zeros_like(gain_sum)
        gain_sum[0:1, :] = norm_sums
        gain_sum[1:4, :] = middle_gain_ref[0:3, :]
        head_sum[...] = head_sums

    @pl.when(step > 0)
    def _():
        gain_sum[0:1, :] += norm_sums
        head_sum[...] += head_sums

    @pl.when(step == pl.num_programs(0) - 1)
    def _():
        count = info_ref.shape[0] - 3
        core = info_ref[count]
        total = queries + 2 * head_dim
        feature_rows = near_ref.shape[1]
        for start in range(0, queries, 512):
            part = slice(start, start + 512)
            grad_all[:, part] = dot_tn(normed_all[...], draw_all[:, part])
        grad_all[:, pair] = dot_tn(normed_all[...], draw_all[:, pair]) + dot_tn(
            normed_before_all[...], draw_before_all[...]
        )
        heads = dot_nt(head_sum[...].astype(jnp.bfloat16), pick_ref[...])
        sums = jnp.concatenate(
            [gain_sum[...] + heads, jnp.zeros((LANES - gain_sum.shape[0], gain_sum.shape[1]), jnp.float32)],
            axis=0,
        )
        grad_all[:, total : total + LANES] = sums.T
        grad_all[:, total + LANES :] = jnp.zeros((grad_all.shape[0], grad_all.shape[1] - total - LANES), jnp.float32)

        def store(value):
            for index in range(count):
                to = near_ref if index % 2 == value else far_ref
                place = info_ref[index]
                lines = slice(index * feature_rows, (index + 1) * feature_rows)
                to[place] = grad_all[lines, :].astype(jnp.bfloat16)

        each_core(core, store)


def angle_tables(offset, length_rows, head_dim):
    half_dim = head_dim // 2
    frequency = 10000.0 ** (-(jnp.arange(half_dim).astype(jnp.float32) * 2.0 / head_dim))
    positions = (offset + jnp.arange(length_rows)).astype(jnp.float32)
    angles = positions[:, None] * frequency[None, :]
    return (jnp.cos(angles), jnp.sin(angles))


def per_device(
    tokens,
    cotangent,
    norm_gain,
    query_weight,
    key_weight,
    value_weight,
    query_norm,
    key_norm,
    output_weight,
    attn_post_gain,
    mlp_pre_gain,
    gate_weight,
    up_weight,
    down_weight,
    mlp_post_gain,
):
    fsdp = lax.axis_size("fsdp")
    rows = norm_gain.shape[0]
    head_rows = query_norm.shape[0]
    gain_columns = jnp.stack(
        [
            norm_gain,
            attn_post_gain,
            mlp_pre_gain,
            mlp_post_gain,
            jnp.pad(query_norm, (0, rows - head_rows)),
            jnp.pad(key_norm, (0, rows - head_rows)),
        ],
        axis=1,
    )
    query_columns = query_weight.shape[1]
    head_dim = key_weight.shape[1]
    ff = gate_weight.shape[1]
    qkv_columns = query_columns + 2 * head_dim
    first_columns = -(-(qkv_columns + LANES) // (2 * LANES)) * 2 * LANES
    gain_columns = jnp.pad(
        gain_columns, ((0, 0), (0, first_columns - qkv_columns - gain_columns.shape[1]))
    )
    first_shard = jnp.concatenate([query_weight, key_weight, value_weight, gain_columns], axis=1)
    tall_shard = jnp.concatenate([down_weight, output_weight], axis=0)
    core = lax.axis_index("fsdp") & 1
    span = lax.axis_index("ctx") & 1
    low_span = span == 0
    info = jnp.concatenate(
        [
            places("fsdp"),
            jnp.stack([core, span, (lax.axis_index("ctx") > 0).astype(jnp.int32)]),
        ]
    )
    sequences, span_len, model_width = tokens.shape
    head_count = query_columns // head_dim
    assert span_len == WINDOW
    offset = lax.axis_index("ctx") * span_len
    score_scale = head_dim ** (-0.5)
    tables = angle_tables(offset, span_len, head_dim)
    tables_before = angle_tables(offset - span_len, span_len, head_dim)
    row = jnp.arange(fsdp * rows)
    pick = (
        (row[:, None] // rows == jnp.arange(head_dim)[None, :] // head_rows)
        & (row[:, None] % rows == jnp.arange(head_dim)[None, :] % head_rows)
    ).astype(jnp.bfloat16)
    chip_masks = [1 << bit for bit in range(fsdp.bit_length() - 2, 0, -1)]
    before = shifted(tokens, "ctx", 1)
    first_shard, info, pick, tables, tables_before = lax.optimization_barrier(
        (first_shard, info, pick, tables, tables_before)
    )
    mine_near = jnp.where(low_span, gate_weight, up_weight)[None]
    first_near, tall_near = first_shard[None], tall_shard[None]
    for step, mask in enumerate(chip_masks):
        if step == len(chip_masks) - 1:
            mine_near = after(mine_near, tall_first, before)
        mine_near = widen(mine_near, "fsdp", mask)
        first_near = widen(first_near, "fsdp", mask, mine_near)
        if step == 0:
            tall_near = after(tall_near, mine_near)
        if step < len(chip_masks) - 1:
            tall_near = widen(tall_near, "fsdp", mask)
        if step == 0:
            tall_first = tall_near
    first_near = after(first_near, tall_near)
    first_far = swap(first_near, "fsdp", 1)
    mine_far = swap(mine_near, "fsdp", 1)
    other_near = swap(mine_near, "ctx", 1)
    tall_late = swap(tall_near, "fsdp", chip_masks[-1])
    total = sequences * span_len
    steps = total // ROWS
    span_steps = span_len // ROWS
    x = tokens.reshape(total, model_width)
    x_before = before.reshape(total, model_width)
    upstream = cotangent.reshape(total, model_width)
    params = pltpu.CompilerParams(vmem_limit_bytes=VMEM_BYTES)
    whole = pl.BlockSpec(memory_space=pltpu.VMEM)
    scalars = pl.BlockSpec(memory_space=pltpu.SMEM)

    def by_rows(columns):
        return pl.BlockSpec((ROWS, columns), lambda i: (i, 0))

    table = pl.BlockSpec((ROWS, head_dim // 2), lambda i: (i % span_steps, 0))

    def bf16(*shape):
        return jax.ShapeDtypeStruct(shape, jnp.bfloat16)

    def f32(*shape):
        return jax.ShapeDtypeStruct(shape, jnp.float32)

    def scratch(*shape):
        return pltpu.VMEM(shape, jnp.bfloat16)

    one_head = by_rows(head_dim)
    model = by_rows(model_width)
    (
        query_low,
        key_low,
        value_low,
        key_prev,
        value_prev,
        first_full,
        gain_rows,
        head_gain_rows,
    ) = pl.pallas_call(
        functools.partial(projection_kernel, head_dim, qkv_columns),
        grid=(steps,),
        in_specs=[model, model, whole, whole, whole, scalars] + [table] * 4,
        out_specs=[by_rows(query_columns)] + [one_head] * 4 + [whole] * 3,
        out_shape=[bf16(total, query_columns)]
        + [bf16(total, head_dim)] * 4
        + [bf16(model_width, qkv_columns), f32(8, model_width), f32(8, head_dim)],
        scratch_shapes=[scratch(model_width, first_columns)],
        compiler_params=params,
        cost_estimate=cost(2 * total * model_width * (qkv_columns + 2 * head_dim), 0.25),
        name="projection",
    )(x, x_before, first_near, first_far, pick, info, *tables, *tables_before)
    head = pl.BlockSpec((span_len, head_dim), lambda s, h: (s, h))
    shared = pl.BlockSpec((span_len, head_dim), lambda s, h: (s, 0))
    attended_low = pl.pallas_call(
        functools.partial(attention_kernel, score_scale),
        grid=(sequences, head_count),
        in_specs=[scalars, head, shared, shared, shared, shared],
        out_specs=head,
        out_shape=bf16(total, query_columns),
        compiler_params=params,
        cost_estimate=cost(3 * total * span_len * query_columns, 0.14),
        name="attention",
    )(info, query_low, key_low, value_low, key_prev, value_prev)
    tall_near = jnp.concatenate([tall_near, after(tall_late, attended_low)], axis=0)
    tall_far = swap(tall_near, "fsdp", 1)
    other_near = after(other_near, tall_near)
    other_far = swap(other_near, "fsdp", 1)
    down_rows, out_rows = down_weight.shape[0], output_weight.shape[0]
    half_rows = (down_rows + out_rows) // 2
    chips = fsdp // 2
    (
        block_output,
        grad_middle,
        grad_attended,
        middle_gains,
        wide_grad_near,
        wide_grad_far,
        tall_grad_near,
        tall_grad_far,
    ) = pl.pallas_call(
        functools.partial(middle_kernel, 512, down_rows),
        grid=(steps,),
        in_specs=[model, model, whole] + [pl.BlockSpec(memory_space=pl.ANY)] * 6 + [whole, scalars],
        out_specs=[model, model, by_rows(query_columns)] + [whole] * 5,
        out_shape=[
            bf16(total, model_width),
            f32(total, model_width),
            bf16(total, query_columns),
            f32(8, model_width),
            bf16(2, chips, rows, ff),
            bf16(2, chips, rows, ff),
            bf16(chips, 2, half_rows, model_width),
            bf16(chips, 2, half_rows, model_width),
        ],
        scratch_shapes=[
            scratch(query_columns, model_width),
            scratch(model_width, ff),
            scratch(model_width, ff),
            scratch(ff, model_width),
            scratch(total, model_width),
            scratch(total, ff),
            scratch(total, model_width),
            scratch(total, ff),
            scratch(total, ff),
            scratch(total, model_width),
            pltpu.SemaphoreType.DMA((6,)),
        ],
        compiler_params=params,
        cost_estimate=cost(6 * total * model_width * (3 * ff + query_columns), 0.4),
        name="middle",
    )(
        x,
        upstream,
        attended_low,
        tall_near.reshape(chips, 2, half_rows, model_width),
        tall_far.reshape(chips, 2, half_rows, model_width),
        mine_near,
        mine_far,
        other_near,
        other_far,
        gain_rows,
        info,
    )
    far_mask, near_masks = chip_masks[0], chip_masks[:0:-1]
    wide_far_sum = swap(wide_grad_far, "fsdp", 1)
    tall_far_sum = swap(tall_grad_far, "fsdp", 1)

    def attention_back(sequence, grad, done):
        one = pl.BlockSpec((span_len, head_dim), lambda h: (sequence, h))
        for_all = pl.BlockSpec((span_len, head_dim), lambda h: (sequence, 0))
        return pl.pallas_call(
            functools.partial(attention_back_kernel, score_scale),
            grid=(head_count,),
            in_specs=[scalars, one] + [for_all] * 4 + [one] + [pl.BlockSpec(memory_space=pl.ANY)] * len(done),
            out_specs=[one] + [for_all] * 4,
            out_shape=[f32(total, query_columns)] + [f32(total, head_dim)] * 4,
            input_output_aliases={7 + index: index for index in range(len(done))},
            compiler_params=params,
            cost_estimate=cost(7.5 * span_len * span_len * query_columns, 0.2),
            name="attention_back",
        )(info, query_low, key_low, value_low, key_prev, value_prev, grad, *done)

    back = attention_back(0, grad_attended, ())
    wide_far_sum, tall_far_sum = after((wide_far_sum, tall_far_sum), back[0])
    wide = add(wide_grad_near, wide_far_sum)
    tall = add(tall_grad_near, tall_far_sum)
    bits = (2,) * len(chip_masks)
    wide = wide.reshape((2,) + bits + wide.shape[2:])
    tall = tall.reshape(bits + tall.shape[1:])
    wide_kept, wide_come = folded(wide, "fsdp", near_masks[0], 1)
    tall_kept, tall_come = folded(tall, "fsdp", near_masks[1], 1)
    wide, tall, grad_attended = lax.optimization_barrier((wide, tall, grad_attended))
    for sequence in range(1, sequences):
        back = attention_back(sequence, grad_attended, back)
    grad_query, grad_key, grad_value, key_send, value_send = back
    token_part, before_part, first_grad_near, first_grad_far = pl.pallas_call(
        functools.partial(head_back_kernel, head_dim),
        grid=(steps,),
        in_specs=[model, model]
        + [whole] * 5
        + [scalars]
        + [table] * 4
        + [by_rows(query_columns)]
        + [one_head] * 4
        + [model],
        out_specs=[model, model, whole, whole],
        out_shape=[
            f32(total, model_width),
            bf16(total, model_width),
            bf16(chips, rows, first_columns),
            bf16(chips, rows, first_columns),
        ],
        scratch_shapes=[
            scratch(total, model_width),
            scratch(total, qkv_columns),
            scratch(total, model_width),
            scratch(total, 2 * head_dim),
            pltpu.VMEM((8, model_width), jnp.float32),
            pltpu.VMEM((8, head_dim), jnp.float32),
            pltpu.VMEM((model_width, first_columns), jnp.float32),
        ],
        compiler_params=params,
        cost_estimate=cost(6 * total * model_width * (qkv_columns + 2 * head_dim), 0.38),
        name="head_back",
    )(
        x,
        x_before,
        first_full,
        gain_rows,
        head_gain_rows,
        pick,
        middle_gains,
        info,
        *tables,
        *tables_before,
        grad_query,
        grad_key,
        grad_value,
        key_send,
        value_send,
        grad_middle,
    )
    tall = add(tall_kept, after(tall_come, token_part))
    wide = add(wide_kept, after(wide_come, token_part))
    first_grad_far, before_part = after((first_grad_far, before_part), tall, wide)
    tall_kept, tall_come = folded(tall, "fsdp", near_masks[0], 0)
    wide_kept, wide_come = folded(wide, "fsdp", near_masks[1], 2)
    before_come = shifted(before_part, "ctx", -1)
    first = add(first_grad_near, swap(first_grad_far, "fsdp", 1))
    first = first.reshape(bits + first.shape[1:])
    first_kept, first_come = folded(first, "fsdp", near_masks[0], 0)
    first = add(first_kept, first_come)
    first_kept, first_come = folded(first, "fsdp", near_masks[1], 1)
    wide = add(wide_kept, after(wide_come, first))
    wide_kept, wide_come = folded(wide, "ctx", 1, 0)
    first = add(first_kept, after(first_come, wide))
    first_kept, first_come = folded(first, "fsdp", (near_masks + [far_mask])[2], 2)
    tall = add(tall_kept, after(tall_come, first))
    tall_kept, tall_come = folded(tall, "ctx", 1, len(bits))
    first = add(first_kept, after(first_come, tall))
    wide = add(wide_kept, after(wide_come, first))
    tall = add(tall_kept, after(tall_come, wide))
    for index in range(2, len(bits)):
        mask = (near_masks + [far_mask])[index]
        if index > 2:
            first_kept, first_come = folded(first, "fsdp", mask, index)
            first = add(first_kept, first_come)
        wide_kept, wide_come = folded(wide, "fsdp", mask, index + 1)
        tall_kept, tall_come = folded(tall, "fsdp", mask, index)
        wide = add(wide_kept, wide_come)
        tall = add(tall_kept, after(tall_come, wide))
    tall = other_spans(tall.reshape(tall.shape[-2:]), "ctx")
    wide = other_spans(wide.reshape(wide.shape[-2:]), "ctx")
    first = other_spans(first.reshape(first.shape[-2:]), "ctx")
    first_come = swap(first, "ctx", 1)
    before_come = after(before_come, tall)
    token_grad = (token_part + before_come.astype(jnp.float32)).astype(jnp.bfloat16)

    def both(mine):
        other = swap(mine, "ctx", 1)
        left = jnp.where(low_span, mine, other).astype(jnp.float32)
        right = jnp.where(low_span, other, mine).astype(jnp.float32)
        return left, right

    grad_gate, grad_up = both(wide)
    grad_tall = jnp.concatenate(both(tall), axis=0)
    grad_first = first.astype(jnp.float32) + first_come.astype(jnp.float32)
    return (
        block_output.reshape(tokens.shape),
        token_grad.reshape(tokens.shape),
        grad_first[:, qkv_columns],
        grad_first[:, :query_columns],
        grad_first[:, query_columns : query_columns + head_dim],
        grad_first[:, query_columns + head_dim : qkv_columns],
        grad_first[:head_rows, qkv_columns + 4],
        grad_first[:head_rows, qkv_columns + 5],
        grad_tall[down_rows:],
        grad_first[:, qkv_columns + 1],
        grad_first[:, qkv_columns + 2],
        grad_gate,
        grad_up,
        grad_tall[:down_rows],
        grad_first[:, qkv_columns + 3],
    )


def solution(mesh):
    return jax.shard_map(
        per_device,
        mesh=mesh,
        in_specs=(
            P("fsdp", "ctx", None),
            P("fsdp", "ctx", None),
            P("fsdp"),
            P("fsdp", None),
            P("fsdp", None),
            P("fsdp", None),
            P("fsdp"),
            P("fsdp"),
            P("fsdp", None),
            P("fsdp"),
            P("fsdp"),
            P("fsdp", None),
            P("fsdp", None),
            P("fsdp", None),
            P("fsdp"),
        ),
        out_specs=(
            P("fsdp", "ctx", None),
            P("fsdp", "ctx", None),
            P("fsdp"),
            P("fsdp", None),
            P("fsdp", None),
            P("fsdp", None),
            P("fsdp"),
            P("fsdp"),
            P("fsdp", None),
            P("fsdp"),
            P("fsdp"),
            P("fsdp", None),
            P("fsdp", None),
            P("fsdp", None),
            P("fsdp"),
        ),
        check_vma=False,
    )
```

```python
import functools

import jax
import jax.numpy as jnp
from jax import lax
from jax.experimental import pallas as pl
from jax.experimental.pallas import tpu as pltpu
from jax.sharding import PartitionSpec as P

WINDOW = 512


EPSILON = 1e-06
MASKED = -1e30
ROOT = (2.0 / jnp.pi) ** 0.5
ROWS = 256
VMEM_BYTES = 60 * 1024 * 1024


LANES = 128


def swap(value, axis, mask):
    count = lax.axis_size(axis)
    return lax.ppermute(value, axis, [(source, source ^ mask) for source in range(count)])


def after(value, *others):
    return lax.optimization_barrier((value, others))[0]


def widen(held, axis, mask, *others):
    return jnp.concatenate([held, after(swap(held, axis, mask), *others)], axis=0)


def places(axis):
    count = lax.axis_size(axis)
    relative = jnp.arange(count, dtype=jnp.int32) ^ lax.axis_index(axis)
    place = jnp.zeros((count,), jnp.int32)
    low, high = 0, count // 2
    while high > 1:
        place = place + jnp.where((relative & high) != 0, 1 << low, 0)
        low, high = low + 1, high // 2
    return place


def cost(flops, spent):
    return pl.CostEstimate(flops=int(flops / spent / 4096), bytes_accessed=0, transcendentals=0)


def add(left, right):
    return (left.astype(jnp.float32) + right.astype(jnp.float32)).astype(jnp.bfloat16)


def folded(value, axis, mask, dim):
    kept, sent = jnp.split(value, 2, axis=dim)
    return kept, swap(sent, axis, mask)


def first_fold(near, come, axis, mask, dim):
    (near, near_sent), (come, come_sent) = (jnp.split(part, 2, axis=dim) for part in (near, come))
    sent = add(near_sent, come_sent)
    return (near, come), sent, swap(sent, axis, mask)


def add_terms(terms, come):
    return sum(term.astype(jnp.float32) for term in (*terms, come)).astype(jnp.bfloat16)


def other_spans(value, axis):
    mask = 2
    while mask < lax.axis_size(axis):
        value = add(value, swap(value, axis, mask))
        mask *= 2
    return value


def shifted(value, axis, steps):
    count = lax.axis_size(axis)
    leading, last = (max(0, -steps), min(count, count - steps))
    return lax.ppermute(value, axis, [(source, source + steps) for source in range(leading, last)])


def dot(left, right):
    return jnp.dot(left, right, preferred_element_type=jnp.float32)


def dot_nt(left, right):
    return lax.dot_general(left, right, (((1,), (1,)), ((), ())), preferred_element_type=jnp.float32)


def dot_tn(left, right):
    return lax.dot_general(left, right, (((0,), (0,)), ((), ())), preferred_element_type=jnp.float32)


def inverse_rms(rows):
    return lax.rsqrt(jnp.mean(rows * rows, axis=-1, keepdims=True) + EPSILON)


def rms_back(rows, scale, gain, grad):
    weighted = gain * grad
    inner = jnp.mean(rows * weighted, axis=-1, keepdims=True)
    return scale * weighted - rows * (scale * scale * scale * inner), grad * rows * scale


def turn(rows, cosine, sine):
    half = rows.shape[-1] // 2
    front, back = rows[:, :half], rows[:, half:]
    return jnp.concatenate([front * cosine - back * sine, back * cosine + front * sine], axis=-1)


def turn_back(rows, cosine, sine):
    return turn(rows, cosine, -sine)


def each_core(core, body):
    for value in (0, 1):
        pl.when(core == value)(functools.partial(body, value))


def whole_block(ref, place):
    return [ref[place]]


def join_pairs(out_ref, near_ref, far_ref, core, info_ref, rows, read=whole_block):
    pairs = 1
    while (2 * rows * pairs) % 16:
        pairs *= 2
    size = 2 * rows * pairs

    def body(value):
        first, second = (near_ref, far_ref) if value == 0 else (far_ref, near_ref)

        def group(index, carry):
            blocks = []
            for pair in range(pairs):
                place = info_ref[2 * (index * pairs + pair)]
                blocks += read(first, place) + read(second, place)
            if rows % 8:
                blocks = [block.astype(jnp.float32) for block in blocks]
            lines = pl.ds(pl.multiple_of(index * size, size), size)
            out_ref[lines, :] = jnp.concatenate(blocks, axis=0).astype(jnp.bfloat16)
            return carry

        lax.fori_loop(0, near_ref.shape[0] // pairs, group, 0)

    each_core(core, body)


def projection_kernel(
    head_dim,
    columns,
    x_ref,
    xb_ref,
    near_ref,
    far_ref,
    pick_ref,
    info_ref,
    cos_ref,
    sin_ref,
    cosb_ref,
    sinb_ref,
    q_ref,
    k_ref,
    v_ref,
    kb_ref,
    vb_ref,
    w_ref,
    gain_ref,
    head_gain_ref,
    all_ref,
):
    count = info_ref.shape[0] - 3

    @pl.when(pl.program_id(0) == 0)
    def _():
        join_pairs(all_ref, near_ref, far_ref, info_ref[count], info_ref, near_ref.shape[1])
        w_ref[...] = all_ref[:, :columns]
        gains = all_ref[:, columns : columns + LANES].astype(jnp.float32).T[:8]
        gain_ref[...] = gains
        head_gain_ref[...] = dot(gains.astype(jnp.bfloat16), pick_ref[...])

    gain = gain_ref[0:1, :]
    queries = q_ref.shape[1]
    x = x_ref[...].astype(jnp.float32)
    normed = (x * inverse_rms(x) * gain).astype(jnp.bfloat16)
    x = xb_ref[...].astype(jnp.float32)
    normed_before = (x * inverse_rms(x) * gain).astype(jnp.bfloat16)
    key_part = slice(queries, queries + head_dim)
    value_part = slice(queries + head_dim, queries + 2 * head_dim)

    def turned(rows, part, head_gain, cosine, sine):
        raw = dot(rows, w_ref[:, part])
        return turn(raw * inverse_rms(raw) * head_gain, cosine, sine).astype(jnp.bfloat16)

    for start in range(0, queries, head_dim):
        part = slice(start, start + head_dim)
        q_ref[:, part] = turned(normed, part, head_gain_ref[4:5, :], cos_ref[...], sin_ref[...])
    k_ref[...] = turned(normed, key_part, head_gain_ref[5:6, :], cos_ref[...], sin_ref[...])
    v_ref[...] = dot(normed, w_ref[:, value_part]).astype(jnp.bfloat16)
    kb_ref[...] = turned(normed_before, key_part, head_gain_ref[5:6, :], cosb_ref[...], sinb_ref[...])
    vb_ref[...] = dot(normed_before, w_ref[:, value_part]).astype(jnp.bfloat16)


def window_parts(rows, now, before, has_before, product):
    half = rows.shape[0] // 2
    low = lax.broadcasted_iota(jnp.int32, (half, half), 1) <= lax.broadcasted_iota(
        jnp.int32, (half, half), 0
    )
    top, bottom = rows[:half], rows[half:]
    before_left = product(top, before[:half])
    before_right = product(top, before[half:])
    before_low = product(bottom, before[half:])
    if has_before is not None:
        before_left = jnp.where(has_before, before_left, MASKED)
        before_right = jnp.where(has_before, before_right, MASKED)
        before_low = jnp.where(has_before, before_low, MASKED)
    upper = jnp.concatenate([jnp.where(low, product(top, now[:half]), before_left), before_right], axis=1)
    lower = jnp.concatenate(
        [product(bottom, now[:half]), jnp.where(low, product(bottom, now[half:]), before_low)], axis=1
    )
    return jnp.concatenate([upper, lower], axis=0)


def window_split(matrix):
    half = matrix.shape[0] // 2
    low = lax.broadcasted_iota(jnp.int32, (half, half), 1) <= lax.broadcasted_iota(
        jnp.int32, (half, half), 0
    )
    first, last = matrix[:half, :half], matrix[half:, half:]
    zero = jnp.zeros_like(first)
    return (
        jnp.where(low, first, zero),
        jnp.where(low, zero, first),
        jnp.where(low, last, zero),
        jnp.where(low, zero, last),
        matrix[:half, half:],
        matrix[half:, :half],
    )


def window_apply(matrix, now, before):
    half = matrix.shape[0] // 2
    first_now, first_before, last_now, last_before, right, left = window_split(matrix)
    top = dot(first_now, now[:half]) + dot(first_before, before[:half]) + dot(right, before[half:])
    bottom = dot(left, now[:half]) + dot(last_now, now[half:]) + dot(last_before, before[half:])
    return jnp.concatenate([top, bottom], axis=0)


def window_apply_back(matrix, rows):
    half = matrix.shape[0] // 2
    first_now, first_before, last_now, last_before, right, left = window_split(matrix)
    top, bottom = rows[:half], rows[half:]
    now = jnp.concatenate([dot_tn(first_now, top) + dot_tn(left, bottom), dot_tn(last_now, bottom)], axis=0)
    before = jnp.concatenate(
        [dot_tn(first_before, top), dot_tn(right, top) + dot_tn(last_before, bottom)], axis=0
    )
    return now, before


def window_probs(query, key, key_before, has_before, scale):
    scores = window_parts(query, key, key_before, has_before, dot_nt) * scale
    terms = jnp.exp(scores - jnp.max(scores, axis=-1, keepdims=True))
    return terms * (1.0 / jnp.sum(terms, axis=-1, keepdims=True))


def attention_kernel(scale, flag_ref, q_ref, k_ref, v_ref, kb_ref, vb_ref, o_ref):
    has_before = flag_ref[flag_ref.shape[0] - 1] > 0
    probs = window_probs(q_ref[...], k_ref[...], kb_ref[...], has_before, scale)
    o_ref[...] = window_apply(probs.astype(jnp.bfloat16), v_ref[...], vb_ref[...]).astype(jnp.bfloat16)


def attention_back_kernel(scale, flag_ref, q_ref, k_ref, v_ref, kb_ref, vb_ref, do_ref, *refs):
    dq_ref, dk_ref, dv_ref, dkb_ref, dvb_ref = refs[-5:]
    has_before = flag_ref[flag_ref.shape[0] - 1] > 0
    query, grad = q_ref[...], do_ref[...]
    probs = window_probs(query, k_ref[...], kb_ref[...], has_before, scale)
    grad_probs = window_parts(grad, v_ref[...], vb_ref[...], None, dot_nt)
    inner = jnp.sum(grad_probs * probs, axis=-1, keepdims=True)
    grad_scores = (probs * (grad_probs - inner)).astype(jnp.bfloat16)
    dq_ref[...] = window_apply(grad_scores, k_ref[...], kb_ref[...]) * scale
    key_now, key_before = window_apply_back(grad_scores, query)
    value_now, value_before = window_apply_back(probs.astype(jnp.bfloat16), grad)

    @pl.when(pl.program_id(0) == 0)
    def _():
        dk_ref[...] = key_now * scale
        dkb_ref[...] = key_before * scale
        dv_ref[...] = value_now
        dvb_ref[...] = value_before

    @pl.when(pl.program_id(0) > 0)
    def _():
        dk_ref[...] += key_now * scale
        dkb_ref[...] += key_before * scale
        dv_ref[...] += value_now
        dvb_ref[...] += value_before


def middle_kernel(
    chunk,
    down_rows,
    x_ref,
    dy_ref,
    att_ref,
    rows_near,
    rows_far,
    mine_near,
    mine_far,
    other_near,
    other_far,
    gain_ref,
    info_ref,
    out_ref,
    dmid_ref,
    datt_ref,
    gain_grad_ref,
    wide_near,
    wide_far,
    tall_near,
    tall_far,
    wo_ref,
    wg_ref,
    wu_ref,
    wd_ref,
    mlp_all,
    hidden_all,
    dmlp_all,
    dgate_all,
    dup_all,
    dattn_all,
    sems,
):
    count = info_ref.shape[0] - 3
    core, span = info_ref[count], info_ref[count + 1]
    half = rows_near.shape[2]
    out_rows = 2 * half - down_rows
    feature_rows = mine_near.shape[1]

    @pl.when(pl.program_id(0) == 0)
    def _():
        copies = [
            pltpu.make_async_copy(source, target, sems.at[index])
            for index, (source, target) in enumerate(
                (
                    (rows_near, tall_near),
                    (rows_far, tall_far),
                    (mine_near, wide_near.at[0]),
                    (other_near, wide_near.at[1]),
                    (mine_far, wide_far.at[0]),
                    (other_far, wide_far.at[1]),
                )
            )
        ]
        for copy in copies:
            copy.start()
        for copy in copies:
            copy.wait()

        def down_block(ref, place):
            return [ref[place, 0], ref[place, 1, : down_rows - half]]

        def out_block(ref, place):
            return [ref[place, 1, down_rows - half :]]

        join_pairs(wd_ref, tall_near, tall_far, core, info_ref, down_rows, down_block)
        join_pairs(wo_ref, tall_near, tall_far, core, info_ref, out_rows, out_block)
        for value in (0, 1):
            first, second = (wg_ref, wu_ref) if value == 0 else (wu_ref, wg_ref)

            @pl.when(span == value)
            def _():
                join_pairs(first, wide_near.at[0], wide_far.at[0], core, info_ref, feature_rows)
                join_pairs(second, wide_near.at[1], wide_far.at[1], core, info_ref, feature_rows)

    step = pl.program_id(0)
    block = x_ref.shape[0]
    rows = pl.ds(pl.multiple_of(step * block, block), block)
    ff = wg_ref.shape[1]
    gain_attn, gain_mlp, gain_final = gain_ref[1:2, :], gain_ref[2:3, :], gain_ref[3:4, :]
    x = x_ref[...].astype(jnp.float32)
    raw = dot(att_ref[rows, :], wo_ref[...])
    raw_scale = inverse_rms(raw)
    middle = x + raw * raw_scale * gain_attn
    middle_scale = inverse_rms(middle)
    mlp_low = (middle * middle_scale * gain_mlp).astype(jnp.bfloat16)
    mlp_all[rows, :] = mlp_low
    kept = []
    mlp_raw = None
    for start in range(0, ff, chunk):
        part = slice(start, start + chunk)
        gate = dot(mlp_low, wg_ref[:, part])
        up = dot(mlp_low, wu_ref[:, part])
        square = gate * gate
        bend = jnp.tanh(ROOT * (gate + 0.044715 * (gate * square)))
        lift = 0.5 * (1.0 + bend)
        gelu = gate * lift
        slope = lift + (0.5 * ROOT) * gate * (1.0 - bend * bend) * (1.0 + (3 * 0.044715) * square)
        hidden = (gelu * up).astype(jnp.bfloat16)
        hidden_all[rows, part] = hidden
        kept.append((up * slope, gelu))
        term = dot(hidden, wd_ref[part, :])
        mlp_raw = term if mlp_raw is None else mlp_raw + term
    mlp_scale = inverse_rms(mlp_raw)
    out_ref[...] = (middle + mlp_raw * mlp_scale * gain_final).astype(jnp.bfloat16)
    dy = dy_ref[...].astype(jnp.float32)
    grad_raw, final_rows = rms_back(mlp_raw, mlp_scale, gain_final, dy)
    dmlp_low = grad_raw.astype(jnp.bfloat16)
    dmlp_all[rows, :] = dmlp_low
    grad_in = None
    for index, start in enumerate(range(0, ff, chunk)):
        part = slice(start, start + chunk)
        grad_hidden = dot_nt(dmlp_low, wd_ref[part, :])
        up_slope, gelu = kept[index]
        dgate = (grad_hidden * up_slope).astype(jnp.bfloat16)
        dup = (grad_hidden * gelu).astype(jnp.bfloat16)
        dgate_all[rows, part] = dgate
        dup_all[rows, part] = dup
        term = dot_nt(dgate, wg_ref[:, part]) + dot_nt(dup, wu_ref[:, part])
        grad_in = term if grad_in is None else grad_in + term
    grad_middle, mlp_rows = rms_back(middle, middle_scale, gain_mlp, grad_in)
    grad_middle = dy + grad_middle
    dmid_ref[...] = grad_middle
    grad_attn, attn_rows = rms_back(raw, raw_scale, gain_attn, grad_middle)
    dattn_low = grad_attn.astype(jnp.bfloat16)
    dattn_all[rows, :] = dattn_low
    datt_ref[...] = dot_nt(dattn_low, wo_ref[...]).astype(jnp.bfloat16)
    sums = [jnp.sum(part, axis=0, keepdims=True) for part in (attn_rows, mlp_rows, final_rows)]
    gain_sums = jnp.concatenate(sums + [jnp.zeros((8 - len(sums), x.shape[1]), jnp.float32)], axis=0)

    @pl.when(step == 0)
    def _():
        gain_grad_ref[...] = gain_sums

    @pl.when(step > 0)
    def _():
        gain_grad_ref[...] += gain_sums

    @pl.when(step == pl.num_programs(0) - 1)
    def _():
        for start in range(0, ff, chunk):
            part = slice(start, start + chunk)
            gate_grad = dot_tn(mlp_all[...], dgate_all[:, part])
            up_grad = dot_tn(mlp_all[...], dup_all[:, part])
            down_grad = dot_tn(hidden_all[:, part], dmlp_all[...]).astype(jnp.bfloat16)

            def store(value):
                for index in range(0, count, 2):
                    place = info_ref[index]
                    for other in (0, 1):
                        to = wide_near if other == value else wide_far
                        lines = slice((index + other) * feature_rows, (index + other + 1) * feature_rows)
                        to[span, place, :, part] = gate_grad[lines].astype(jnp.bfloat16)
                        to[1 - span, place, :, part] = up_grad[lines].astype(jnp.bfloat16)
                for line in range(0, chunk, down_rows):
                    index = (start + line) // down_rows
                    to = tall_near if index % 2 == value else tall_far
                    place = info_ref[index]
                    to[place, span] = down_grad[line : line + half]
                    to[place, 1 - span, : down_rows - half] = down_grad[line + half : line + down_rows]

            each_core(core, store)
        for start in range(0, wo_ref.shape[0], chunk):
            part = slice(start, start + chunk)
            out_grad = dot_tn(att_ref[:, part], dattn_all[...]).astype(jnp.bfloat16)

            def store_out(value):
                for line in range(0, chunk, out_rows):
                    index = (start + line) // out_rows
                    to = tall_near if index % 2 == value else tall_far
                    to[info_ref[index], 1 - span, down_rows - half :] = out_grad[line : line + out_rows]

            each_core(core, store_out)


def head_back_kernel(
    head_dim,
    x_ref,
    xb_ref,
    w_ref,
    gain_ref,
    head_gain_ref,
    pick_ref,
    middle_gain_ref,
    info_ref,
    cos_ref,
    sin_ref,
    cosb_ref,
    sinb_ref,
    dq_ref,
    dk_ref,
    dv_ref,
    dkb_ref,
    dvb_ref,
    dmid_ref,
    token_ref,
    before_ref,
    near_ref,
    far_ref,
    normed_all,
    draw_all,
    normed_before_all,
    draw_before_all,
    gain_sum,
    head_sum,
    grad_all,
):
    step = pl.program_id(0)
    block = x_ref.shape[0]
    rows = pl.ds(pl.multiple_of(step * block, block), block)
    queries = dq_ref.shape[1]
    keys = slice(queries, queries + head_dim)
    pair = slice(queries, queries + 2 * head_dim)
    norm_gain = gain_ref[0:1, :]
    query_gain, key_gain = head_gain_ref[4:5, :], head_gain_ref[5:6, :]
    x = x_ref[...].astype(jnp.float32)
    x_scale = inverse_rms(x)
    normed = (x * x_scale * norm_gain).astype(jnp.bfloat16)
    normed_all[rows, :] = normed
    cosine, sine = cos_ref[...], sin_ref[...]
    query_rows = None
    for start in range(0, queries, head_dim):
        part = slice(start, start + head_dim)
        raw = dot(normed, w_ref[:, part])
        grad = turn_back(dq_ref[:, part], cosine, sine)
        grad_raw, head_rows = rms_back(raw, inverse_rms(raw), query_gain, grad)
        query_rows = head_rows if query_rows is None else query_rows + head_rows
        draw_all[rows, part] = grad_raw.astype(jnp.bfloat16)
    raw = dot(normed, w_ref[:, keys])
    grad_raw, key_rows = rms_back(raw, inverse_rms(raw), key_gain, turn_back(dk_ref[...], cosine, sine))
    draw_all[rows, keys] = grad_raw.astype(jnp.bfloat16)
    draw_all[rows, queries + head_dim : queries + 2 * head_dim] = dv_ref[...].astype(jnp.bfloat16)
    grad_normed = dot_nt(draw_all[rows, :], w_ref[...])
    grad_x, norm_rows = rms_back(x, x_scale, norm_gain, grad_normed)
    token_ref[...] = dmid_ref[...] + grad_x

    xb = xb_ref[...].astype(jnp.float32)
    xb_scale = inverse_rms(xb)
    normed_before = (xb * xb_scale * norm_gain).astype(jnp.bfloat16)
    normed_before_all[rows, :] = normed_before
    raw = dot(normed_before, w_ref[:, keys])
    grad = turn_back(dkb_ref[...], cosb_ref[...], sinb_ref[...])
    grad_raw, key_before_rows = rms_back(raw, inverse_rms(raw), key_gain, grad)
    draw_before = jnp.concatenate([grad_raw, dvb_ref[...]], axis=1).astype(jnp.bfloat16)
    draw_before_all[rows, :] = draw_before
    grad_xb, norm_before_rows = rms_back(xb, xb_scale, norm_gain, dot_nt(draw_before, w_ref[:, pair]))
    before_ref[...] = grad_xb.astype(jnp.bfloat16)

    norm_sums = jnp.sum(norm_rows + norm_before_rows, axis=0, keepdims=True)
    head_sums = jnp.concatenate(
        [
            jnp.zeros((4, head_dim), jnp.float32),
            jnp.sum(query_rows, axis=0, keepdims=True),
            jnp.sum(key_rows + key_before_rows, axis=0, keepdims=True),
            jnp.zeros((2, head_dim), jnp.float32),
        ],
        axis=0,
    )

    @pl.when(step == 0)
    def _():
        gain_sum[...] = jnp.zeros_like(gain_sum)
        gain_sum[0:1, :] = norm_sums
        gain_sum[1:4, :] = middle_gain_ref[0:3, :]
        head_sum[...] = head_sums

    @pl.when(step > 0)
    def _():
        gain_sum[0:1, :] += norm_sums
        head_sum[...] += head_sums

    @pl.when(step == pl.num_programs(0) - 1)
    def _():
        count = info_ref.shape[0] - 3
        core = info_ref[count]
        total = queries + 2 * head_dim
        feature_rows = near_ref.shape[1]
        for start in range(0, queries, 512):
            part = slice(start, start + 512)
            grad_all[:, part] = dot_tn(normed_all[...], draw_all[:, part])
        grad_all[:, pair] = dot_tn(normed_all[...], draw_all[:, pair]) + dot_tn(
            normed_before_all[...], draw_before_all[...]
        )
        heads = dot_nt(head_sum[...].astype(jnp.bfloat16), pick_ref[...])
        sums = jnp.concatenate(
            [gain_sum[...] + heads, jnp.zeros((LANES - gain_sum.shape[0], gain_sum.shape[1]), jnp.float32)],
            axis=0,
        )
        grad_all[:, total : total + LANES] = sums.T
        grad_all[:, total + LANES :] = jnp.zeros((grad_all.shape[0], grad_all.shape[1] - total - LANES), jnp.float32)

        def store(value):
            for index in range(count):
                to = near_ref if index % 2 == value else far_ref
                place = info_ref[index]
                lines = slice(index * feature_rows, (index + 1) * feature_rows)
                to[place] = grad_all[lines, :].astype(jnp.bfloat16)

        each_core(core, store)


def angle_tables(offset, length_rows, head_dim):
    half_dim = head_dim // 2
    frequency = 10000.0 ** (-(jnp.arange(half_dim).astype(jnp.float32) * 2.0 / head_dim))
    positions = (offset + jnp.arange(length_rows)).astype(jnp.float32)
    angles = positions[:, None] * frequency[None, :]
    return (jnp.cos(angles), jnp.sin(angles))


def per_device(
    tokens,
    cotangent,
    norm_gain,
    query_weight,
    key_weight,
    value_weight,
    query_norm,
    key_norm,
    output_weight,
    attn_post_gain,
    mlp_pre_gain,
    gate_weight,
    up_weight,
    down_weight,
    mlp_post_gain,
):
    fsdp = lax.axis_size("fsdp")
    rows = norm_gain.shape[0]
    head_rows = query_norm.shape[0]
    gain_columns = jnp.stack(
        [
            norm_gain,
            attn_post_gain,
            mlp_pre_gain,
            mlp_post_gain,
            jnp.pad(query_norm, (0, rows - head_rows)),
            jnp.pad(key_norm, (0, rows - head_rows)),
        ],
        axis=1,
    )
    query_columns = query_weight.shape[1]
    head_dim = key_weight.shape[1]
    ff = gate_weight.shape[1]
    qkv_columns = query_columns + 2 * head_dim
    first_columns = -(-(qkv_columns + LANES) // (2 * LANES)) * 2 * LANES
    gain_columns = jnp.pad(
        gain_columns, ((0, 0), (0, first_columns - qkv_columns - gain_columns.shape[1]))
    )
    first_shard = jnp.concatenate([query_weight, key_weight, value_weight, gain_columns], axis=1)
    tall_shard = jnp.concatenate([down_weight, output_weight], axis=0)
    core = lax.axis_index("fsdp") & 1
    span = lax.axis_index("ctx") & 1
    low_span = span == 0
    info = jnp.concatenate(
        [
            places("fsdp"),
            jnp.stack([core, span, (lax.axis_index("ctx") > 0).astype(jnp.int32)]),
        ]
    )
    sequences, span_len, model_width = tokens.shape
    head_count = query_columns // head_dim
    assert span_len == WINDOW
    offset = lax.axis_index("ctx") * span_len
    score_scale = head_dim ** (-0.5)
    tables = angle_tables(offset, span_len, head_dim)
    tables_before = angle_tables(offset - span_len, span_len, head_dim)
    row = jnp.arange(fsdp * rows)
    pick = (
        (row[:, None] // rows == jnp.arange(head_dim)[None, :] // head_rows)
        & (row[:, None] % rows == jnp.arange(head_dim)[None, :] % head_rows)
    ).astype(jnp.bfloat16)
    chip_masks = [1 << bit for bit in range(fsdp.bit_length() - 2, 0, -1)]
    before = shifted(tokens, "ctx", 1)
    first_shard, info, pick, tables, tables_before = lax.optimization_barrier(
        (first_shard, info, pick, tables, tables_before)
    )
    mine_near = jnp.where(low_span, gate_weight, up_weight)[None]
    first_near, tall_near = first_shard[None], tall_shard[None]
    for step, mask in enumerate(chip_masks):
        if step == len(chip_masks) - 1:
            mine_near = after(mine_near, tall_first, before)
        mine_near = widen(mine_near, "fsdp", mask)
        if step == len(chip_masks) - 1:
            mine_far = swap(mine_near, "fsdp", 1)
            other_near = swap(mine_near, "ctx", 1)
            first_near = widen(first_near, "fsdp", mask, mine_far)
        else:
            first_near = widen(first_near, "fsdp", mask, mine_near)
        if step == 0:
            tall_near = after(tall_near, mine_near)
        if step < len(chip_masks) - 1:
            tall_near = widen(tall_near, "fsdp", mask)
        if step == 0:
            tall_first = tall_near
    first_near = after(first_near, tall_near)
    first_far = swap(first_near, "fsdp", 1)
    tall_late = swap(tall_near, "fsdp", chip_masks[-1])
    total = sequences * span_len
    steps = total // ROWS
    span_steps = span_len // ROWS
    x = tokens.reshape(total, model_width)
    x_before = before.reshape(total, model_width)
    upstream = cotangent.reshape(total, model_width)
    params = pltpu.CompilerParams(vmem_limit_bytes=VMEM_BYTES)
    whole = pl.BlockSpec(memory_space=pltpu.VMEM)
    scalars = pl.BlockSpec(memory_space=pltpu.SMEM)

    def by_rows(columns):
        return pl.BlockSpec((ROWS, columns), lambda i: (i, 0))

    table = pl.BlockSpec((ROWS, head_dim // 2), lambda i: (i % span_steps, 0))

    def bf16(*shape):
        return jax.ShapeDtypeStruct(shape, jnp.bfloat16)

    def f32(*shape):
        return jax.ShapeDtypeStruct(shape, jnp.float32)

    def scratch(*shape):
        return pltpu.VMEM(shape, jnp.bfloat16)

    one_head = by_rows(head_dim)
    model = by_rows(model_width)
    (
        query_low,
        key_low,
        value_low,
        key_prev,
        value_prev,
        first_full,
        gain_rows,
        head_gain_rows,
    ) = pl.pallas_call(
        functools.partial(projection_kernel, head_dim, qkv_columns),
        grid=(steps,),
        in_specs=[model, model, whole, whole, whole, scalars] + [table] * 4,
        out_specs=[by_rows(query_columns)] + [one_head] * 4 + [whole] * 3,
        out_shape=[bf16(total, query_columns)]
        + [bf16(total, head_dim)] * 4
        + [bf16(model_width, qkv_columns), f32(8, model_width), f32(8, head_dim)],
        scratch_shapes=[scratch(model_width, first_columns)],
        compiler_params=params,
        cost_estimate=cost(2 * total * model_width * (qkv_columns + 2 * head_dim), 0.25),
        name="projection",
    )(x, x_before, first_near, first_far, pick, info, *tables, *tables_before)
    head = pl.BlockSpec((span_len, head_dim), lambda s, h: (s, h))
    shared = pl.BlockSpec((span_len, head_dim), lambda s, h: (s, 0))
    attended_low = pl.pallas_call(
        functools.partial(attention_kernel, score_scale),
        grid=(sequences, head_count),
        in_specs=[scalars, head, shared, shared, shared, shared],
        out_specs=head,
        out_shape=bf16(total, query_columns),
        compiler_params=params,
        cost_estimate=cost(3 * total * span_len * query_columns, 0.14),
        name="attention",
    )(info, query_low, key_low, value_low, key_prev, value_prev)
    tall_near = jnp.concatenate([tall_near, after(tall_late, attended_low)], axis=0)
    tall_far = swap(tall_near, "fsdp", 1)
    other_near = after(other_near, tall_near)
    other_far = swap(other_near, "fsdp", 1)
    down_rows, out_rows = down_weight.shape[0], output_weight.shape[0]
    half_rows = (down_rows + out_rows) // 2
    chips = fsdp // 2
    (
        block_output,
        grad_middle,
        grad_attended,
        middle_gains,
        wide_grad_near,
        wide_grad_far,
        tall_grad_near,
        tall_grad_far,
    ) = pl.pallas_call(
        functools.partial(middle_kernel, 512, down_rows),
        grid=(steps,),
        in_specs=[model, model, whole] + [pl.BlockSpec(memory_space=pl.ANY)] * 6 + [whole, scalars],
        out_specs=[model, model, by_rows(query_columns)] + [whole] * 5,
        out_shape=[
            bf16(total, model_width),
            f32(total, model_width),
            bf16(total, query_columns),
            f32(8, model_width),
            bf16(2, chips, rows, ff),
            bf16(2, chips, rows, ff),
            bf16(chips, 2, half_rows, model_width),
            bf16(chips, 2, half_rows, model_width),
        ],
        scratch_shapes=[
            scratch(query_columns, model_width),
            scratch(model_width, ff),
            scratch(model_width, ff),
            scratch(ff, model_width),
            scratch(total, model_width),
            scratch(total, ff),
            scratch(total, model_width),
            scratch(total, ff),
            scratch(total, ff),
            scratch(total, model_width),
            pltpu.SemaphoreType.DMA((6,)),
        ],
        compiler_params=params,
        cost_estimate=cost(6 * total * model_width * (3 * ff + query_columns), 0.4),
        name="middle",
    )(
        x,
        upstream,
        attended_low,
        tall_near.reshape(chips, 2, half_rows, model_width),
        tall_far.reshape(chips, 2, half_rows, model_width),
        mine_near,
        mine_far,
        other_near,
        other_far,
        gain_rows,
        info,
    )
    far_mask, near_masks = chip_masks[0], chip_masks[:0:-1]
    wide_far_sum = swap(wide_grad_far, "fsdp", 1)
    tall_far_sum = swap(tall_grad_far, "fsdp", 1)

    def attention_back(sequence, grad, done):
        one = pl.BlockSpec((span_len, head_dim), lambda h: (sequence, h))
        for_all = pl.BlockSpec((span_len, head_dim), lambda h: (sequence, 0))
        return pl.pallas_call(
            functools.partial(attention_back_kernel, score_scale),
            grid=(head_count,),
            in_specs=[scalars, one] + [for_all] * 4 + [one] + [pl.BlockSpec(memory_space=pl.ANY)] * len(done),
            out_specs=[one] + [for_all] * 4,
            out_shape=[f32(total, query_columns)] + [f32(total, head_dim)] * 4,
            input_output_aliases={7 + index: index for index in range(len(done))},
            compiler_params=params,
            cost_estimate=cost(7.5 * span_len * span_len * query_columns, 0.2),
            name="attention_back",
        )(info, query_low, key_low, value_low, key_prev, value_prev, grad, *done)

    back = attention_back(0, grad_attended, ())
    wide_far_sum, tall_far_sum = after((wide_far_sum, tall_far_sum), back[0])
    bits = (2,) * len(chip_masks)
    wide_shape = (2,) + bits + wide_grad_near.shape[2:]
    tall_shape = bits + tall_grad_near.shape[1:]
    wide_kept, wide_sent, wide_come = first_fold(
        wide_grad_near.reshape(wide_shape), wide_far_sum.reshape(wide_shape), "fsdp", near_masks[0], 1
    )
    tall_kept, tall_sent, tall_come = first_fold(
        tall_grad_near.reshape(tall_shape), tall_far_sum.reshape(tall_shape), "fsdp", near_masks[1], 1
    )
    grad_attended = after(grad_attended, wide_sent, tall_sent)
    for sequence in range(1, sequences):
        back = attention_back(sequence, grad_attended, back)
    grad_query, grad_key, grad_value, key_send, value_send = back
    token_part, before_part, first_grad_near, first_grad_far = pl.pallas_call(
        functools.partial(head_back_kernel, head_dim),
        grid=(steps,),
        in_specs=[model, model]
        + [whole] * 5
        + [scalars]
        + [table] * 4
        + [by_rows(query_columns)]
        + [one_head] * 4
        + [model],
        out_specs=[model, model, whole, whole],
        out_shape=[
            f32(total, model_width),
            bf16(total, model_width),
            bf16(chips, rows, first_columns),
            bf16(chips, rows, first_columns),
        ],
        scratch_shapes=[
            scratch(total, model_width),
            scratch(total, qkv_columns),
            scratch(total, model_width),
            scratch(total, 2 * head_dim),
            pltpu.VMEM((8, model_width), jnp.float32),
            pltpu.VMEM((8, head_dim), jnp.float32),
            pltpu.VMEM((model_width, first_columns), jnp.float32),
        ],
        compiler_params=params,
        cost_estimate=cost(6 * total * model_width * (qkv_columns + 2 * head_dim), 0.38),
        name="head_back",
    )(
        x,
        x_before,
        first_full,
        gain_rows,
        head_gain_rows,
        pick,
        middle_gains,
        info,
        *tables,
        *tables_before,
        grad_query,
        grad_key,
        grad_value,
        key_send,
        value_send,
        grad_middle,
    )
    tall = add_terms(tall_kept, after(tall_come, token_part))
    wide = add_terms(wide_kept, after(wide_come, token_part))
    first_grad_far, before_part = after((first_grad_far, before_part), tall, wide)
    tall_kept, tall_come = folded(tall, "fsdp", near_masks[0], 0)
    wide_kept, wide_come = folded(wide, "fsdp", near_masks[1], 2)
    before_come = shifted(before_part, "ctx", -1)
    first_shape = bits + first_grad_near.shape[1:]
    first_kept, _, first_come = first_fold(
        first_grad_near.reshape(first_shape),
        swap(first_grad_far, "fsdp", 1).reshape(first_shape),
        "fsdp",
        near_masks[0],
        0,
    )
    first = add_terms(first_kept, first_come)
    first_kept, first_come = folded(first, "fsdp", near_masks[1], 1)
    wide = add(wide_kept, after(wide_come, first))
    wide_kept, wide_come = folded(wide, "ctx", 1, 0)
    first = add(first_kept, after(first_come, wide))
    first_kept, first_come = folded(first, "fsdp", (near_masks + [far_mask])[2], 2)
    tall = add(tall_kept, after(tall_come, first))
    tall_kept, tall_come = folded(tall, "ctx", 1, len(bits))
    first = add(first_kept, after(first_come, tall))
    wide = add(wide_kept, after(wide_come, first))
    tall = add(tall_kept, after(tall_come, wide))
    for index in range(2, len(bits)):
        mask = (near_masks + [far_mask])[index]
        if index > 2:
            first_kept, first_come = folded(first, "fsdp", mask, index)
            first = add(first_kept, first_come)
        wide_kept, wide_come = folded(wide, "fsdp", mask, index + 1)
        tall_kept, tall_come = folded(tall, "fsdp", mask, index)
        wide = add(wide_kept, wide_come)
        tall = add(tall_kept, after(tall_come, wide))
    tall = other_spans(tall.reshape(tall.shape[-2:]), "ctx")
    wide = other_spans(wide.reshape(wide.shape[-2:]), "ctx")
    first = other_spans(first.reshape(first.shape[-2:]), "ctx")
    first_come = swap(first, "ctx", 1)
    before_come = after(before_come, tall)
    token_grad = (token_part + before_come.astype(jnp.float32)).astype(jnp.bfloat16)

    def both(mine):
        other = swap(mine, "ctx", 1)
        left = jnp.where(low_span, mine, other).astype(jnp.float32)
        right = jnp.where(low_span, other, mine).astype(jnp.float32)
        return left, right

    grad_gate, grad_up = both(wide)
    grad_tall = jnp.concatenate(both(tall), axis=0)
    grad_first = first.astype(jnp.float32) + first_come.astype(jnp.float32)
    return (
        block_output.reshape(tokens.shape),
        token_grad.reshape(tokens.shape),
        grad_first[:, qkv_columns],
        grad_first[:, :query_columns],
        grad_first[:, query_columns : query_columns + head_dim],
        grad_first[:, query_columns + head_dim : qkv_columns],
        grad_first[:head_rows, qkv_columns + 4],
        grad_first[:head_rows, qkv_columns + 5],
        grad_tall[down_rows:],
        grad_first[:, qkv_columns + 1],
        grad_first[:, qkv_columns + 2],
        grad_gate,
        grad_up,
        grad_tall[:down_rows],
        grad_first[:, qkv_columns + 3],
    )


def solution(mesh):
    return jax.shard_map(
        per_device,
        mesh=mesh,
        in_specs=(
            P("fsdp", "ctx", None),
            P("fsdp", "ctx", None),
            P("fsdp"),
            P("fsdp", None),
            P("fsdp", None),
            P("fsdp", None),
            P("fsdp"),
            P("fsdp"),
            P("fsdp", None),
            P("fsdp"),
            P("fsdp"),
            P("fsdp", None),
            P("fsdp", None),
            P("fsdp", None),
            P("fsdp"),
        ),
        out_specs=(
            P("fsdp", "ctx", None),
            P("fsdp", "ctx", None),
            P("fsdp"),
            P("fsdp", None),
            P("fsdp", None),
            P("fsdp", None),
            P("fsdp"),
            P("fsdp"),
            P("fsdp", None),
            P("fsdp"),
            P("fsdp"),
            P("fsdp", None),
            P("fsdp", None),
            P("fsdp", None),
            P("fsdp"),
        ),
        check_vma=False,
    )
```

```python
import functools

import jax
import jax.numpy as jnp
from jax import lax
from jax.experimental import pallas as pl
from jax.experimental.pallas import tpu as pltpu
from jax.sharding import PartitionSpec as P

WINDOW = 512


EPSILON = 1e-06
MASKED = -1e30
ROOT = (2.0 / jnp.pi) ** 0.5
ROWS = 256
VMEM_BYTES = 60 * 1024 * 1024


LANES = 128


def swap(value, axis, mask):
    count = lax.axis_size(axis)
    return lax.ppermute(value, axis, [(source, source ^ mask) for source in range(count)])


def after(value, *others):
    return lax.optimization_barrier((value, others))[0]


def widen(held, axis, mask, *others):
    return jnp.concatenate([held, after(swap(held, axis, mask), *others)], axis=0)


def places(axis):
    count = lax.axis_size(axis)
    relative = jnp.arange(count, dtype=jnp.int32) ^ lax.axis_index(axis)
    place = jnp.zeros((count,), jnp.int32)
    low, high = 0, count // 2
    while high > 1:
        place = place + jnp.where((relative & high) != 0, 1 << low, 0)
        low, high = low + 1, high // 2
    return place


def cost(flops, spent):
    return pl.CostEstimate(flops=int(flops / spent / 4096), bytes_accessed=0, transcendentals=0)


def add(left, right):
    return (left.astype(jnp.float32) + right.astype(jnp.float32)).astype(jnp.bfloat16)


def folded(value, axis, mask, dim):
    kept, sent = jnp.split(value, 2, axis=dim)
    return kept, swap(sent, axis, mask)


def first_fold(near, come, axis, mask, dim):
    (near, near_sent), (come, come_sent) = (jnp.split(part, 2, axis=dim) for part in (near, come))
    sent = add(near_sent, come_sent)
    return (near, come), sent, swap(sent, axis, mask)


def add_terms(terms, come):
    return sum(term.astype(jnp.float32) for term in (*terms, come)).astype(jnp.bfloat16)


def other_spans(value, axis):
    mask = 2
    while mask < lax.axis_size(axis):
        value = add(value, swap(value, axis, mask))
        mask *= 2
    return value


def shifted(value, axis, steps):
    count = lax.axis_size(axis)
    leading, last = (max(0, -steps), min(count, count - steps))
    return lax.ppermute(value, axis, [(source, source + steps) for source in range(leading, last)])


def dot(left, right):
    return jnp.dot(left, right, preferred_element_type=jnp.float32)


def dot_nt(left, right):
    return lax.dot_general(left, right, (((1,), (1,)), ((), ())), preferred_element_type=jnp.float32)


def dot_tn(left, right):
    return lax.dot_general(left, right, (((0,), (0,)), ((), ())), preferred_element_type=jnp.float32)


def inverse_rms(rows):
    return lax.rsqrt(jnp.mean(rows * rows, axis=-1, keepdims=True) + EPSILON)


def rms_back(rows, scale, gain, grad):
    weighted = gain * grad
    inner = jnp.mean(rows * weighted, axis=-1, keepdims=True)
    return scale * weighted - rows * (scale * scale * scale * inner), grad * rows * scale


def turn(rows, cosine, sine):
    half = rows.shape[-1] // 2
    front, back = rows[:, :half], rows[:, half:]
    return jnp.concatenate([front * cosine - back * sine, back * cosine + front * sine], axis=-1)


def turn_back(rows, cosine, sine):
    return turn(rows, cosine, -sine)


def each_core(core, body):
    for value in (0, 1):
        pl.when(core == value)(functools.partial(body, value))


def whole_block(ref, place):
    return [ref[place]]


def join_pairs(out_ref, near_ref, far_ref, core, info_ref, rows, read=whole_block):
    pairs = 1
    while (2 * rows * pairs) % 16:
        pairs *= 2
    size = 2 * rows * pairs

    def body(value):
        first, second = (near_ref, far_ref) if value == 0 else (far_ref, near_ref)

        def group(index, carry):
            blocks = []
            for pair in range(pairs):
                place = info_ref[2 * (index * pairs + pair)]
                blocks += read(first, place) + read(second, place)
            if rows % 8:
                blocks = [block.astype(jnp.float32) for block in blocks]
            lines = pl.ds(pl.multiple_of(index * size, size), size)
            out_ref[lines, :] = jnp.concatenate(blocks, axis=0).astype(jnp.bfloat16)
            return carry

        lax.fori_loop(0, near_ref.shape[0] // pairs, group, 0)

    each_core(core, body)


def projection_kernel(
    head_dim,
    columns,
    x_ref,
    xb_ref,
    near_ref,
    far_ref,
    pick_ref,
    info_ref,
    cos_ref,
    sin_ref,
    cosb_ref,
    sinb_ref,
    q_ref,
    k_ref,
    v_ref,
    kb_ref,
    vb_ref,
    w_ref,
    gain_ref,
    head_gain_ref,
    all_ref,
):
    count = info_ref.shape[0] - 3

    @pl.when(pl.program_id(0) == 0)
    def _():
        join_pairs(all_ref, near_ref, far_ref, info_ref[count], info_ref, near_ref.shape[1])
        w_ref[...] = all_ref[:, :columns]
        gains = all_ref[:, columns : columns + LANES].astype(jnp.float32).T[:8]
        gain_ref[...] = gains
        head_gain_ref[...] = dot(gains.astype(jnp.bfloat16), pick_ref[...])

    gain = gain_ref[0:1, :]
    queries = q_ref.shape[1]
    x = x_ref[...].astype(jnp.float32)
    normed = (x * inverse_rms(x) * gain).astype(jnp.bfloat16)
    x = xb_ref[...].astype(jnp.float32)
    normed_before = (x * inverse_rms(x) * gain).astype(jnp.bfloat16)
    key_part = slice(queries, queries + head_dim)
    value_part = slice(queries + head_dim, queries + 2 * head_dim)

    def turned(rows, part, head_gain, cosine, sine):
        raw = dot(rows, w_ref[:, part])
        return turn(raw * inverse_rms(raw) * head_gain, cosine, sine).astype(jnp.bfloat16)

    for start in range(0, queries, head_dim):
        part = slice(start, start + head_dim)
        q_ref[:, part] = turned(normed, part, head_gain_ref[4:5, :], cos_ref[...], sin_ref[...])
    k_ref[...] = turned(normed, key_part, head_gain_ref[5:6, :], cos_ref[...], sin_ref[...])
    v_ref[...] = dot(normed, w_ref[:, value_part]).astype(jnp.bfloat16)
    kb_ref[...] = turned(normed_before, key_part, head_gain_ref[5:6, :], cosb_ref[...], sinb_ref[...])
    vb_ref[...] = dot(normed_before, w_ref[:, value_part]).astype(jnp.bfloat16)


def window_parts(rows, now, before, has_before, product):
    half = rows.shape[0] // 2
    low = lax.broadcasted_iota(jnp.int32, (half, half), 1) <= lax.broadcasted_iota(
        jnp.int32, (half, half), 0
    )
    top, bottom = rows[:half], rows[half:]
    before_left = product(top, before[:half])
    before_right = product(top, before[half:])
    before_low = product(bottom, before[half:])
    if has_before is not None:
        before_left = jnp.where(has_before, before_left, MASKED)
        before_right = jnp.where(has_before, before_right, MASKED)
        before_low = jnp.where(has_before, before_low, MASKED)
    upper = jnp.concatenate([jnp.where(low, product(top, now[:half]), before_left), before_right], axis=1)
    lower = jnp.concatenate(
        [product(bottom, now[:half]), jnp.where(low, product(bottom, now[half:]), before_low)], axis=1
    )
    return jnp.concatenate([upper, lower], axis=0)


def window_split(matrix):
    half = matrix.shape[0] // 2
    low = lax.broadcasted_iota(jnp.int32, (half, half), 1) <= lax.broadcasted_iota(
        jnp.int32, (half, half), 0
    )
    first, last = matrix[:half, :half], matrix[half:, half:]
    zero = jnp.zeros_like(first)
    return (
        jnp.where(low, first, zero),
        jnp.where(low, zero, first),
        jnp.where(low, last, zero),
        jnp.where(low, zero, last),
        matrix[:half, half:],
        matrix[half:, :half],
    )


def window_apply(matrix, now, before):
    half = matrix.shape[0] // 2
    first_now, first_before, last_now, last_before, right, left = window_split(matrix)
    top = dot(first_now, now[:half]) + dot(first_before, before[:half]) + dot(right, before[half:])
    bottom = dot(left, now[:half]) + dot(last_now, now[half:]) + dot(last_before, before[half:])
    return jnp.concatenate([top, bottom], axis=0)


def window_apply_back(matrix, rows):
    half = matrix.shape[0] // 2
    first_now, first_before, last_now, last_before, right, left = window_split(matrix)
    top, bottom = rows[:half], rows[half:]
    now = jnp.concatenate([dot_tn(first_now, top) + dot_tn(left, bottom), dot_tn(last_now, bottom)], axis=0)
    before = jnp.concatenate(
        [dot_tn(first_before, top), dot_tn(right, top) + dot_tn(last_before, bottom)], axis=0
    )
    return now, before


def window_probs(query, key, key_before, has_before, scale):
    scores = window_parts(query, key, key_before, has_before, dot_nt) * scale
    terms = jnp.exp(scores - jnp.max(scores, axis=-1, keepdims=True))
    return terms * (1.0 / jnp.sum(terms, axis=-1, keepdims=True))


def attention_kernel(scale, flag_ref, q_ref, k_ref, v_ref, kb_ref, vb_ref, o_ref):
    has_before = flag_ref[flag_ref.shape[0] - 1] > 0
    probs = window_probs(q_ref[...], k_ref[...], kb_ref[...], has_before, scale)
    o_ref[...] = window_apply(probs.astype(jnp.bfloat16), v_ref[...], vb_ref[...]).astype(jnp.bfloat16)


def attention_back_kernel(scale, flag_ref, q_ref, k_ref, v_ref, kb_ref, vb_ref, do_ref, *refs):
    dq_ref, dk_ref, dv_ref, dkb_ref, dvb_ref = refs[-5:]
    has_before = flag_ref[flag_ref.shape[0] - 1] > 0
    query, grad = q_ref[...], do_ref[...]
    probs = window_probs(query, k_ref[...], kb_ref[...], has_before, scale)
    grad_probs = window_parts(grad, v_ref[...], vb_ref[...], None, dot_nt)
    inner = jnp.sum(grad_probs * probs, axis=-1, keepdims=True)
    grad_scores = (probs * (grad_probs - inner)).astype(jnp.bfloat16)
    dq_ref[...] = window_apply(grad_scores, k_ref[...], kb_ref[...]) * scale
    key_now, key_before = window_apply_back(grad_scores, query)
    value_now, value_before = window_apply_back(probs.astype(jnp.bfloat16), grad)

    @pl.when(pl.program_id(0) == 0)
    def _():
        dk_ref[...] = key_now * scale
        dkb_ref[...] = key_before * scale
        dv_ref[...] = value_now
        dvb_ref[...] = value_before

    @pl.when(pl.program_id(0) > 0)
    def _():
        dk_ref[...] += key_now * scale
        dkb_ref[...] += key_before * scale
        dv_ref[...] += value_now
        dvb_ref[...] += value_before


def middle_kernel(
    chunk,
    down_rows,
    x_ref,
    dy_ref,
    att_ref,
    rows_near,
    rows_far,
    mine_near,
    mine_far,
    other_near,
    other_far,
    gain_ref,
    info_ref,
    out_ref,
    dmid_ref,
    datt_ref,
    gain_grad_ref,
    wide_near,
    wide_far,
    tall_near,
    tall_far,
    wo_ref,
    wg_ref,
    wu_ref,
    wd_ref,
    mlp_all,
    hidden_all,
    dmlp_all,
    dgate_all,
    dup_all,
    dattn_all,
    sems,
):
    count = info_ref.shape[0] - 3
    core, span = info_ref[count], info_ref[count + 1]
    half = rows_near.shape[2]
    out_rows = 2 * half - down_rows
    feature_rows = mine_near.shape[1]

    @pl.when(pl.program_id(0) == 0)
    def _():
        copies = [
            pltpu.make_async_copy(source, target, sems.at[index])
            for index, (source, target) in enumerate(
                (
                    (rows_near, tall_near),
                    (rows_far, tall_far),
                    (mine_near, wide_near.at[0]),
                    (other_near, wide_near.at[1]),
                    (mine_far, wide_far.at[0]),
                    (other_far, wide_far.at[1]),
                )
            )
        ]
        for copy in copies:
            copy.start()
        for copy in copies:
            copy.wait()

        def down_block(ref, place):
            return [ref[place, 0], ref[place, 1, : down_rows - half]]

        def out_block(ref, place):
            return [ref[place, 1, down_rows - half :]]

        join_pairs(wd_ref, tall_near, tall_far, core, info_ref, down_rows, down_block)
        join_pairs(wo_ref, tall_near, tall_far, core, info_ref, out_rows, out_block)
        for value in (0, 1):
            first, second = (wg_ref, wu_ref) if value == 0 else (wu_ref, wg_ref)

            @pl.when(span == value)
            def _():
                join_pairs(first, wide_near.at[0], wide_far.at[0], core, info_ref, feature_rows)
                join_pairs(second, wide_near.at[1], wide_far.at[1], core, info_ref, feature_rows)

    step = pl.program_id(0)
    block = x_ref.shape[0]
    rows = pl.ds(pl.multiple_of(step * block, block), block)
    ff = wg_ref.shape[1]
    gain_attn, gain_mlp, gain_final = gain_ref[1:2, :], gain_ref[2:3, :], gain_ref[3:4, :]
    x = x_ref[...].astype(jnp.float32)
    raw = dot(att_ref[rows, :], wo_ref[...])
    raw_scale = inverse_rms(raw)
    middle = x + raw * raw_scale * gain_attn
    middle_scale = inverse_rms(middle)
    mlp_low = (middle * middle_scale * gain_mlp).astype(jnp.bfloat16)
    mlp_all[rows, :] = mlp_low
    kept = []
    mlp_raw = None
    for start in range(0, ff, chunk):
        part = slice(start, start + chunk)
        gate = dot(mlp_low, wg_ref[:, part])
        up = dot(mlp_low, wu_ref[:, part])
        square = gate * gate
        bend = jnp.tanh(ROOT * (gate + 0.044715 * (gate * square)))
        lift = 0.5 * (1.0 + bend)
        gelu = gate * lift
        slope = lift + (0.5 * ROOT) * gate * (1.0 - bend * bend) * (1.0 + (3 * 0.044715) * square)
        hidden = (gelu * up).astype(jnp.bfloat16)
        hidden_all[rows, part] = hidden
        kept.append((up * slope, gelu))
        term = dot(hidden, wd_ref[part, :])
        mlp_raw = term if mlp_raw is None else mlp_raw + term
    mlp_scale = inverse_rms(mlp_raw)
    out_ref[...] = (middle + mlp_raw * mlp_scale * gain_final).astype(jnp.bfloat16)
    dy = dy_ref[...].astype(jnp.float32)
    grad_raw, final_rows = rms_back(mlp_raw, mlp_scale, gain_final, dy)
    dmlp_low = grad_raw.astype(jnp.bfloat16)
    dmlp_all[rows, :] = dmlp_low
    grad_in = None
    for index, start in enumerate(range(0, ff, chunk)):
        part = slice(start, start + chunk)
        grad_hidden = dot_nt(dmlp_low, wd_ref[part, :])
        up_slope, gelu = kept[index]
        dgate = (grad_hidden * up_slope).astype(jnp.bfloat16)
        dup = (grad_hidden * gelu).astype(jnp.bfloat16)
        dgate_all[rows, part] = dgate
        dup_all[rows, part] = dup
        term = dot_nt(dgate, wg_ref[:, part]) + dot_nt(dup, wu_ref[:, part])
        grad_in = term if grad_in is None else grad_in + term
    grad_middle, mlp_rows = rms_back(middle, middle_scale, gain_mlp, grad_in)
    grad_middle = dy + grad_middle
    dmid_ref[...] = grad_middle
    grad_attn, attn_rows = rms_back(raw, raw_scale, gain_attn, grad_middle)
    dattn_low = grad_attn.astype(jnp.bfloat16)
    dattn_all[rows, :] = dattn_low
    datt_ref[...] = dot_nt(dattn_low, wo_ref[...]).astype(jnp.bfloat16)
    sums = [jnp.sum(part, axis=0, keepdims=True) for part in (attn_rows, mlp_rows, final_rows)]
    gain_sums = jnp.concatenate(sums + [jnp.zeros((8 - len(sums), x.shape[1]), jnp.float32)], axis=0)

    @pl.when(step == 0)
    def _():
        gain_grad_ref[...] = gain_sums

    @pl.when(step > 0)
    def _():
        gain_grad_ref[...] += gain_sums

    @pl.when(step == pl.num_programs(0) - 1)
    def _():
        for start in range(0, ff, chunk):
            part = slice(start, start + chunk)
            gate_grad = dot_tn(mlp_all[...], dgate_all[:, part])
            up_grad = dot_tn(mlp_all[...], dup_all[:, part])
            down_grad = dot_tn(hidden_all[:, part], dmlp_all[...]).astype(jnp.bfloat16)

            def store(value):
                for index in range(0, count, 2):
                    place = info_ref[index]
                    for other in (0, 1):
                        to = wide_near if other == value else wide_far
                        lines = slice((index + other) * feature_rows, (index + other + 1) * feature_rows)
                        to[span, place, :, part] = gate_grad[lines].astype(jnp.bfloat16)
                        to[1 - span, place, :, part] = up_grad[lines].astype(jnp.bfloat16)
                for line in range(0, chunk, down_rows):
                    index = (start + line) // down_rows
                    to = tall_near if index % 2 == value else tall_far
                    place = info_ref[index]
                    to[place, span] = down_grad[line : line + half]
                    to[place, 1 - span, : down_rows - half] = down_grad[line + half : line + down_rows]

            each_core(core, store)
        for start in range(0, wo_ref.shape[0], chunk):
            part = slice(start, start + chunk)
            out_grad = dot_tn(att_ref[:, part], dattn_all[...]).astype(jnp.bfloat16)

            def store_out(value):
                for line in range(0, chunk, out_rows):
                    index = (start + line) // out_rows
                    to = tall_near if index % 2 == value else tall_far
                    to[info_ref[index], 1 - span, down_rows - half :] = out_grad[line : line + out_rows]

            each_core(core, store_out)


def head_back_kernel(
    head_dim,
    x_ref,
    xb_ref,
    w_ref,
    gain_ref,
    head_gain_ref,
    pick_ref,
    middle_gain_ref,
    info_ref,
    cos_ref,
    sin_ref,
    cosb_ref,
    sinb_ref,
    dq_ref,
    dk_ref,
    dv_ref,
    dkb_ref,
    dvb_ref,
    dmid_ref,
    token_ref,
    before_ref,
    near_ref,
    far_ref,
    normed_all,
    draw_all,
    normed_before_all,
    draw_before_all,
    gain_sum,
    head_sum,
    grad_all,
):
    step = pl.program_id(0)
    block = x_ref.shape[0]
    rows = pl.ds(pl.multiple_of(step * block, block), block)
    queries = dq_ref.shape[1]
    keys = slice(queries, queries + head_dim)
    pair = slice(queries, queries + 2 * head_dim)
    norm_gain = gain_ref[0:1, :]
    query_gain, key_gain = head_gain_ref[4:5, :], head_gain_ref[5:6, :]
    x = x_ref[...].astype(jnp.float32)
    x_scale = inverse_rms(x)
    normed = (x * x_scale * norm_gain).astype(jnp.bfloat16)
    normed_all[rows, :] = normed
    cosine, sine = cos_ref[...], sin_ref[...]
    query_rows = None
    for start in range(0, queries, head_dim):
        part = slice(start, start + head_dim)
        raw = dot(normed, w_ref[:, part])
        grad = turn_back(dq_ref[:, part], cosine, sine)
        grad_raw, head_rows = rms_back(raw, inverse_rms(raw), query_gain, grad)
        query_rows = head_rows if query_rows is None else query_rows + head_rows
        draw_all[rows, part] = grad_raw.astype(jnp.bfloat16)
    raw = dot(normed, w_ref[:, keys])
    grad_raw, key_rows = rms_back(raw, inverse_rms(raw), key_gain, turn_back(dk_ref[...], cosine, sine))
    draw_all[rows, keys] = grad_raw.astype(jnp.bfloat16)
    draw_all[rows, queries + head_dim : queries + 2 * head_dim] = dv_ref[...].astype(jnp.bfloat16)
    grad_normed = dot_nt(draw_all[rows, :], w_ref[...])
    grad_x, norm_rows = rms_back(x, x_scale, norm_gain, grad_normed)
    token_ref[...] = dmid_ref[...] + grad_x

    xb = xb_ref[...].astype(jnp.float32)
    xb_scale = inverse_rms(xb)
    normed_before = (xb * xb_scale * norm_gain).astype(jnp.bfloat16)
    normed_before_all[rows, :] = normed_before
    raw = dot(normed_before, w_ref[:, keys])
    grad = turn_back(dkb_ref[...], cosb_ref[...], sinb_ref[...])
    grad_raw, key_before_rows = rms_back(raw, inverse_rms(raw), key_gain, grad)
    draw_before = jnp.concatenate([grad_raw, dvb_ref[...]], axis=1).astype(jnp.bfloat16)
    draw_before_all[rows, :] = draw_before
    grad_xb, norm_before_rows = rms_back(xb, xb_scale, norm_gain, dot_nt(draw_before, w_ref[:, pair]))
    before_ref[...] = grad_xb.astype(jnp.bfloat16)

    norm_sums = jnp.sum(norm_rows + norm_before_rows, axis=0, keepdims=True)
    head_sums = jnp.concatenate(
        [
            jnp.zeros((4, head_dim), jnp.float32),
            jnp.sum(query_rows, axis=0, keepdims=True),
            jnp.sum(key_rows + key_before_rows, axis=0, keepdims=True),
            jnp.zeros((2, head_dim), jnp.float32),
        ],
        axis=0,
    )

    @pl.when(step == 0)
    def _():
        gain_sum[...] = jnp.zeros_like(gain_sum)
        gain_sum[0:1, :] = norm_sums
        gain_sum[1:4, :] = middle_gain_ref[0:3, :]
        head_sum[...] = head_sums

    @pl.when(step > 0)
    def _():
        gain_sum[0:1, :] += norm_sums
        head_sum[...] += head_sums

    @pl.when(step == pl.num_programs(0) - 1)
    def _():
        count = info_ref.shape[0] - 3
        core = info_ref[count]
        total = queries + 2 * head_dim
        feature_rows = near_ref.shape[1]
        for start in range(0, queries, 512):
            part = slice(start, start + 512)
            grad_all[:, part] = dot_tn(normed_all[...], draw_all[:, part])
        grad_all[:, pair] = dot_tn(normed_all[...], draw_all[:, pair]) + dot_tn(
            normed_before_all[...], draw_before_all[...]
        )
        heads = dot_nt(head_sum[...].astype(jnp.bfloat16), pick_ref[...])
        sums = jnp.concatenate(
            [gain_sum[...] + heads, jnp.zeros((LANES - gain_sum.shape[0], gain_sum.shape[1]), jnp.float32)],
            axis=0,
        )
        grad_all[:, total : total + LANES] = sums.T
        grad_all[:, total + LANES :] = jnp.zeros((grad_all.shape[0], grad_all.shape[1] - total - LANES), jnp.float32)

        def store(value):
            for index in range(count):
                to = near_ref if index % 2 == value else far_ref
                place = info_ref[index]
                lines = slice(index * feature_rows, (index + 1) * feature_rows)
                to[place] = grad_all[lines, :].astype(jnp.bfloat16)

        each_core(core, store)


def angle_tables(offset, length_rows, head_dim):
    half_dim = head_dim // 2
    frequency = 10000.0 ** (-(jnp.arange(half_dim).astype(jnp.float32) * 2.0 / head_dim))
    positions = (offset + jnp.arange(length_rows)).astype(jnp.float32)
    angles = positions[:, None] * frequency[None, :]
    return (jnp.cos(angles), jnp.sin(angles))


def per_device(
    tokens,
    cotangent,
    norm_gain,
    query_weight,
    key_weight,
    value_weight,
    query_norm,
    key_norm,
    output_weight,
    attn_post_gain,
    mlp_pre_gain,
    gate_weight,
    up_weight,
    down_weight,
    mlp_post_gain,
):
    fsdp = lax.axis_size("fsdp")
    rows = norm_gain.shape[0]
    head_rows = query_norm.shape[0]
    gain_columns = jnp.stack(
        [
            norm_gain,
            attn_post_gain,
            mlp_pre_gain,
            mlp_post_gain,
            jnp.pad(query_norm, (0, rows - head_rows)),
            jnp.pad(key_norm, (0, rows - head_rows)),
        ],
        axis=1,
    )
    query_columns = query_weight.shape[1]
    head_dim = key_weight.shape[1]
    ff = gate_weight.shape[1]
    qkv_columns = query_columns + 2 * head_dim
    first_columns = -(-(qkv_columns + LANES) // (2 * LANES)) * 2 * LANES
    gain_columns = jnp.pad(
        gain_columns, ((0, 0), (0, first_columns - qkv_columns - gain_columns.shape[1]))
    )
    first_shard = jnp.concatenate([query_weight, key_weight, value_weight, gain_columns], axis=1)
    tall_shard = jnp.concatenate([down_weight, output_weight], axis=0)
    core = lax.axis_index("fsdp") & 1
    span = lax.axis_index("ctx") & 1
    low_span = span == 0
    info = jnp.concatenate(
        [
            places("fsdp"),
            jnp.stack([core, span, (lax.axis_index("ctx") > 0).astype(jnp.int32)]),
        ]
    )
    sequences, span_len, model_width = tokens.shape
    head_count = query_columns // head_dim
    assert span_len == WINDOW
    offset = lax.axis_index("ctx") * span_len
    score_scale = head_dim ** (-0.5)
    tables = angle_tables(offset, span_len, head_dim)
    tables_before = angle_tables(offset - span_len, span_len, head_dim)
    row = jnp.arange(fsdp * rows)
    pick = (
        (row[:, None] // rows == jnp.arange(head_dim)[None, :] // head_rows)
        & (row[:, None] % rows == jnp.arange(head_dim)[None, :] % head_rows)
    ).astype(jnp.bfloat16)
    chip_masks = [1 << bit for bit in range(fsdp.bit_length() - 2, 0, -1)]
    before = shifted(tokens, "ctx", 1)
    first_shard, info, pick, tables, tables_before = lax.optimization_barrier(
        (first_shard, info, pick, tables, tables_before)
    )
    mine_near = jnp.where(low_span, gate_weight, up_weight)[None]
    first_near, tall_near = first_shard[None], tall_shard[None]
    for step, mask in enumerate(chip_masks):
        if step == len(chip_masks) - 1:
            mine_near = after(mine_near, tall_first, before)
        mine_near = widen(mine_near, "fsdp", mask)
        first_near = widen(first_near, "fsdp", mask, mine_near)
        if step == 0:
            tall_near = after(tall_near, mine_near)
        if step < len(chip_masks) - 1:
            tall_near = widen(tall_near, "fsdp", mask)
        if step == 0:
            tall_first = tall_near
    first_near = after(first_near, tall_near)
    first_far = swap(first_near, "fsdp", 1)
    mine_far = swap(mine_near, "fsdp", 1)
    other_near = swap(mine_near, "ctx", 1)
    tall_late = swap(tall_near, "fsdp", chip_masks[-1])
    total = sequences * span_len
    steps = total // ROWS
    span_steps = span_len // ROWS
    x = tokens.reshape(total, model_width)
    x_before = before.reshape(total, model_width)
    upstream = cotangent.reshape(total, model_width)
    params = pltpu.CompilerParams(vmem_limit_bytes=VMEM_BYTES)
    whole = pl.BlockSpec(memory_space=pltpu.VMEM)
    scalars = pl.BlockSpec(memory_space=pltpu.SMEM)

    def by_rows(columns):
        return pl.BlockSpec((ROWS, columns), lambda i: (i, 0))

    table = pl.BlockSpec((ROWS, head_dim // 2), lambda i: (i % span_steps, 0))

    def bf16(*shape):
        return jax.ShapeDtypeStruct(shape, jnp.bfloat16)

    def f32(*shape):
        return jax.ShapeDtypeStruct(shape, jnp.float32)

    def scratch(*shape):
        return pltpu.VMEM(shape, jnp.bfloat16)

    one_head = by_rows(head_dim)
    model = by_rows(model_width)
    (
        query_low,
        key_low,
        value_low,
        key_prev,
        value_prev,
        first_full,
        gain_rows,
        head_gain_rows,
    ) = pl.pallas_call(
        functools.partial(projection_kernel, head_dim, qkv_columns),
        grid=(steps,),
        in_specs=[model, model, whole, whole, whole, scalars] + [table] * 4,
        out_specs=[by_rows(query_columns)] + [one_head] * 4 + [whole] * 3,
        out_shape=[bf16(total, query_columns)]
        + [bf16(total, head_dim)] * 4
        + [bf16(model_width, qkv_columns), f32(8, model_width), f32(8, head_dim)],
        scratch_shapes=[scratch(model_width, first_columns)],
        compiler_params=params,
        cost_estimate=cost(2 * total * model_width * (qkv_columns + 2 * head_dim), 0.25),
        name="projection",
    )(x, x_before, first_near, first_far, pick, info, *tables, *tables_before)
    head = pl.BlockSpec((span_len, head_dim), lambda s, h: (s, h))
    shared = pl.BlockSpec((span_len, head_dim), lambda s, h: (s, 0))
    attended_low = pl.pallas_call(
        functools.partial(attention_kernel, score_scale),
        grid=(sequences, head_count),
        in_specs=[scalars, head, shared, shared, shared, shared],
        out_specs=head,
        out_shape=bf16(total, query_columns),
        compiler_params=params,
        cost_estimate=cost(3 * total * span_len * query_columns, 0.14),
        name="attention",
    )(info, query_low, key_low, value_low, key_prev, value_prev)
    tall_near = jnp.concatenate([tall_near, after(tall_late, attended_low)], axis=0)
    tall_far = swap(tall_near, "fsdp", 1)
    other_near = after(other_near, tall_near)
    other_far = swap(other_near, "fsdp", 1)
    down_rows, out_rows = down_weight.shape[0], output_weight.shape[0]
    half_rows = (down_rows + out_rows) // 2
    chips = fsdp // 2
    (
        block_output,
        grad_middle,
        grad_attended,
        middle_gains,
        wide_grad_near,
        wide_grad_far,
        tall_grad_near,
        tall_grad_far,
    ) = pl.pallas_call(
        functools.partial(middle_kernel, 512, down_rows),
        grid=(steps,),
        in_specs=[model, model, whole] + [pl.BlockSpec(memory_space=pl.ANY)] * 6 + [whole, scalars],
        out_specs=[model, model, by_rows(query_columns)] + [whole] * 5,
        out_shape=[
            bf16(total, model_width),
            f32(total, model_width),
            bf16(total, query_columns),
            f32(8, model_width),
            bf16(2, chips, rows, ff),
            bf16(2, chips, rows, ff),
            bf16(chips, 2, half_rows, model_width),
            bf16(chips, 2, half_rows, model_width),
        ],
        scratch_shapes=[
            scratch(query_columns, model_width),
            scratch(model_width, ff),
            scratch(model_width, ff),
            scratch(ff, model_width),
            scratch(total, model_width),
            scratch(total, ff),
            scratch(total, model_width),
            scratch(total, ff),
            scratch(total, ff),
            scratch(total, model_width),
            pltpu.SemaphoreType.DMA((6,)),
        ],
        compiler_params=params,
        cost_estimate=cost(6 * total * model_width * (3 * ff + query_columns), 0.4),
        name="middle",
    )(
        x,
        upstream,
        attended_low,
        tall_near.reshape(chips, 2, half_rows, model_width),
        tall_far.reshape(chips, 2, half_rows, model_width),
        mine_near,
        mine_far,
        other_near,
        other_far,
        gain_rows,
        info,
    )
    far_mask, near_masks = chip_masks[0], chip_masks[:0:-1]
    wide_far_sum = swap(wide_grad_far, "fsdp", 1)
    tall_far_sum = swap(tall_grad_far, "fsdp", 1)

    def attention_back(sequence, grad, done):
        one = pl.BlockSpec((span_len, head_dim), lambda h: (sequence, h))
        for_all = pl.BlockSpec((span_len, head_dim), lambda h: (sequence, 0))
        return pl.pallas_call(
            functools.partial(attention_back_kernel, score_scale),
            grid=(head_count,),
            in_specs=[scalars, one] + [for_all] * 4 + [one] + [pl.BlockSpec(memory_space=pl.ANY)] * len(done),
            out_specs=[one] + [for_all] * 4,
            out_shape=[f32(total, query_columns)] + [f32(total, head_dim)] * 4,
            input_output_aliases={7 + index: index for index in range(len(done))},
            compiler_params=params,
            cost_estimate=cost(7.5 * span_len * span_len * query_columns, 0.2),
            name="attention_back",
        )(info, query_low, key_low, value_low, key_prev, value_prev, grad, *done)

    back = attention_back(0, grad_attended, ())
    wide_far_sum, tall_far_sum = after((wide_far_sum, tall_far_sum), back[0])
    bits = (2,) * len(chip_masks)
    wide_shape = (2,) + bits + wide_grad_near.shape[2:]
    tall_shape = bits + tall_grad_near.shape[1:]
    wide_kept, wide_sent, wide_come = first_fold(
        wide_grad_near.reshape(wide_shape), wide_far_sum.reshape(wide_shape), "fsdp", near_masks[0], 1
    )
    tall_kept, tall_sent, tall_come = first_fold(
        tall_grad_near.reshape(tall_shape), tall_far_sum.reshape(tall_shape), "fsdp", near_masks[1], 1
    )
    grad_attended = after(grad_attended, wide_sent, tall_sent)
    for sequence in range(1, sequences):
        back = attention_back(sequence, grad_attended, back)
    grad_query, grad_key, grad_value, key_send, value_send = back
    token_part, before_part, first_grad_near, first_grad_far = pl.pallas_call(
        functools.partial(head_back_kernel, head_dim),
        grid=(steps,),
        in_specs=[model, model]
        + [whole] * 5
        + [scalars]
        + [table] * 4
        + [by_rows(query_columns)]
        + [one_head] * 4
        + [model],
        out_specs=[model, model, whole, whole],
        out_shape=[
            f32(total, model_width),
            bf16(total, model_width),
            bf16(chips, rows, first_columns),
            bf16(chips, rows, first_columns),
        ],
        scratch_shapes=[
            scratch(total, model_width),
            scratch(total, qkv_columns),
            scratch(total, model_width),
            scratch(total, 2 * head_dim),
            pltpu.VMEM((8, model_width), jnp.float32),
            pltpu.VMEM((8, head_dim), jnp.float32),
            pltpu.VMEM((model_width, first_columns), jnp.float32),
        ],
        compiler_params=params,
        cost_estimate=cost(6 * total * model_width * (qkv_columns + 2 * head_dim), 0.38),
        name="head_back",
    )(
        x,
        x_before,
        first_full,
        gain_rows,
        head_gain_rows,
        pick,
        middle_gains,
        info,
        *tables,
        *tables_before,
        grad_query,
        grad_key,
        grad_value,
        key_send,
        value_send,
        grad_middle,
    )
    tall = add_terms(tall_kept, after(tall_come, token_part))
    wide = add_terms(wide_kept, after(wide_come, token_part))
    first_grad_far, before_part = after((first_grad_far, before_part), tall, wide)
    tall_kept, tall_come = folded(tall, "fsdp", near_masks[0], 0)
    wide_kept, wide_come = folded(wide, "fsdp", near_masks[1], 2)
    before_come = shifted(before_part, "ctx", -1)
    first_shape = bits + first_grad_near.shape[1:]
    first_kept, _, first_come = first_fold(
        first_grad_near.reshape(first_shape),
        swap(first_grad_far, "fsdp", 1).reshape(first_shape),
        "fsdp",
        near_masks[0],
        0,
    )
    first = add_terms(first_kept, first_come)
    first_kept, first_come = folded(first, "fsdp", near_masks[1], 1)
    wide = add(wide_kept, after(wide_come, first))
    wide_kept, wide_come = folded(wide, "ctx", 1, 0)
    first = add(first_kept, after(first_come, wide))
    first_kept, first_come = folded(first, "fsdp", (near_masks + [far_mask])[2], 2)
    tall = add(tall_kept, after(tall_come, first))
    tall_kept, tall_come = folded(tall, "ctx", 1, len(bits))
    first = add(first_kept, after(first_come, tall))
    wide = add(wide_kept, after(wide_come, first))
    tall = add(tall_kept, after(tall_come, wide))
    for index in range(2, len(bits)):
        mask = (near_masks + [far_mask])[index]
        if index > 2:
            first_kept, first_come = folded(first, "fsdp", mask, index)
            first = add(first_kept, first_come)
        wide_kept, wide_come = folded(wide, "fsdp", mask, index + 1)
        tall_kept, tall_come = folded(tall, "fsdp", mask, index)
        wide = add(wide_kept, wide_come)
        tall = add(tall_kept, after(tall_come, wide))
    tall = other_spans(tall.reshape(tall.shape[-2:]), "ctx")
    wide = other_spans(wide.reshape(wide.shape[-2:]), "ctx")
    first = other_spans(first.reshape(first.shape[-2:]), "ctx")
    first_come = swap(first, "ctx", 1)
    before_come = after(before_come, tall)
    token_grad = (token_part + before_come.astype(jnp.float32)).astype(jnp.bfloat16)

    def both(mine):
        other = swap(mine, "ctx", 1)
        left = jnp.where(low_span, mine, other).astype(jnp.float32)
        right = jnp.where(low_span, other, mine).astype(jnp.float32)
        return left, right

    grad_gate, grad_up = both(wide)
    grad_tall = jnp.concatenate(both(tall), axis=0)
    grad_first = first.astype(jnp.float32) + first_come.astype(jnp.float32)
    return (
        block_output.reshape(tokens.shape),
        token_grad.reshape(tokens.shape),
        grad_first[:, qkv_columns],
        grad_first[:, :query_columns],
        grad_first[:, query_columns : query_columns + head_dim],
        grad_first[:, query_columns + head_dim : qkv_columns],
        grad_first[:head_rows, qkv_columns + 4],
        grad_first[:head_rows, qkv_columns + 5],
        grad_tall[down_rows:],
        grad_first[:, qkv_columns + 1],
        grad_first[:, qkv_columns + 2],
        grad_gate,
        grad_up,
        grad_tall[:down_rows],
        grad_first[:, qkv_columns + 3],
    )


def solution(mesh):
    return jax.shard_map(
        per_device,
        mesh=mesh,
        in_specs=(
            P("fsdp", "ctx", None),
            P("fsdp", "ctx", None),
            P("fsdp"),
            P("fsdp", None),
            P("fsdp", None),
            P("fsdp", None),
            P("fsdp"),
            P("fsdp"),
            P("fsdp", None),
            P("fsdp"),
            P("fsdp"),
            P("fsdp", None),
            P("fsdp", None),
            P("fsdp", None),
            P("fsdp"),
        ),
        out_specs=(
            P("fsdp", "ctx", None),
            P("fsdp", "ctx", None),
            P("fsdp"),
            P("fsdp", None),
            P("fsdp", None),
            P("fsdp", None),
            P("fsdp"),
            P("fsdp"),
            P("fsdp", None),
            P("fsdp"),
            P("fsdp"),
            P("fsdp", None),
            P("fsdp", None),
            P("fsdp", None),
            P("fsdp"),
        ),
        check_vma=False,
    )
```
